128 devices in a mesh: wide: 64 (over x, z_lo, y, core), narrow: 2 (over z_hi).
Axes of the slice: x: 4, y: 4, z: 4 (z_hi: 2, z_lo: 2; z = z_hi * 2 + z_lo), core: 2. Of those that a mesh axis runs over, the one named last changes fastest.
Arguments:
- tests: float32 [1024, 32, 3, 8, 64], P('wide', None, None, 'narrow'), may hold values from -6 to 6
- block_inverse: float32 [1024, 3, 3, 8, 64], P('wide', None, None, 'narrow'), may hold values from -0.25 to 0.4, as said below
- face_weight: float32 [1024, 6, 8, 64], P('wide', None, 'narrow'), may hold values from 0.3 to 1
- mixing: float32 [6, 3, 3], replicated, may hold values from -3 to 3
- far_tiles: bfloat16 [1024, 2, 3, 256, 256], P('wide', 'narrow'), may hold values from -0.21875 to 0.21875
- far_column: int32 [1024, 2, 3], P('wide', 'narrow'), may hold values from 0 to 15
- aggregate: int32 [1024, 8, 64], P('wide', 'narrow'), may hold values from 0 to 127, as said below
- owner_map: int32 [8192], P(('wide', 'narrow')), may hold values from 0 to 127, as said below
Outputs:
- prolong: float32 [1024, 32, 3, 8, 64], P('wide', None, None, 'narrow')
- coarse_basis: float32 [128, 256, 1024], P(('wide', 'narrow'))
The draws below stay inside these ranges and needn't reach their ends.
Inputs may be any that keep to these rules, and one draw needn't show every extreme that they name: `aggregate`: aggregate numbers of the nodes of one wide rank; every number of a wide rank is used. `owner_map`: no home device has more than 2 aggregates with the same owner; in every draw some owner receives 2 aggregates from every home device. `block_inverse`: diagonal entries lie in 0.2 to 0.4.
All inputs are finite; a program needn't handle non-finite values.
Results may differ from the reference program's by a relative error of at most 0.0022.
Values may be sent and summed in bfloat16 or wider, within the bound.
A program may use at most 128 MiB of HBM per device.

```python
import math
import jax
import jax.numpy as jnp
from jax import lax

K = 32
CX = 16
CY = 4
CZ = 64
SWEEPS = 3
REACH = 1
SLOT = 2
HEAVY = 2
NODES_AGG = 64
TILE = 256
NB = 3
NX = 1024
NY = 8
NZ = 64
AGG_DEV = 64
AGG_W = 128
AGGS = 8192
N_WIDE = 64
N_NARROW = 2
DEVICES = 128


def draw_block_inverse(key, part):
    diagonal_key, other_key = jax.random.split(key)
    diagonal_part = jax.random.uniform(diagonal_key, (NX, 3, NY, NZ), jnp.float32, 0.2, 0.4)
    off_part = jnp.clip(0.07 * jax.random.normal(other_key, (NX, 3, 3, NY, NZ), jnp.float32), -0.25, 0.25)
    identity = jnp.eye(3, dtype=jnp.float32)[None, :, :, None, None]
    return identity * diagonal_part[:, :, None] + (1.0 - identity) * off_part


def draw_aggregate(key, part):
    rank_count = NX // CX
    rank_nodes = CX * NY * NZ
    lowest = NODES_AGG // 2

    def one_rank(rank_key):
        order_key, extra_key = jax.random.split(rank_key)
        position = jax.random.permutation(order_key, rank_nodes)
        extra_label = jax.random.randint(extra_key, (rank_nodes,), 0, AGG_W)
        return jnp.where(position < AGG_W * lowest, position % AGG_W, extra_label).astype(jnp.int32)
    labels = jax.vmap(one_rank)(jax.random.split(key, rank_count))
    return labels.reshape(NX, NY, NZ)


def draw_owner_map(key, part):
    heavy_key, home_key = jax.random.split(key)
    places = jnp.arange(SLOT * DEVICES, dtype=jnp.int32)
    candidates = places % DEVICES
    chosen_heavy = jax.random.permutation(heavy_key, DEVICES)[:HEAVY]
    heavy_flag = jnp.zeros((DEVICES,), jnp.int32).at[chosen_heavy].set(1)

    def one_home(single_key):
        score_key, shuffle_key = jax.random.split(single_key)
        scores = jax.random.randint(score_key, (SLOT * DEVICES,), 0, 1048576) * (SLOT * DEVICES) + places
        scores = jnp.where(heavy_flag[candidates] == 1, places - SLOT * DEVICES, scores)
        picked = candidates[jnp.argsort(scores)[:AGG_DEV]]
        return jax.random.permutation(shuffle_key, picked)
    return jax.vmap(one_home)(jax.random.split(home_key, DEVICES)).reshape(AGGS).astype(jnp.int32)


def with_ends(result, own_key, least, top_value):
    index_at = [jax.random.randint(jax.random.fold_in(own_key, axis), (), 0, length) for axis, length in enumerate(result.shape)]
    main_axis = result.shape.index(max(result.shape))
    beside = index_at[:main_axis] + [(index_at[main_axis] + 1) % result.shape[main_axis]] + index_at[main_axis + 1:]
    return result.at[tuple(index_at)].set(least).at[tuple(beside)].set(top_value)


def levels(own_key, shape, shards, low, top_value):
    def one(dim, parts):
        draws = jax.random.uniform(jax.random.fold_in(jax.random.fold_in(own_key, 6), dim), (parts,), jnp.float32, low / len(shards), top_value / len(shards))
        return jnp.repeat(jnp.exp(draws), shape[dim] // parts).reshape((-1,) + (1,) * (len(shape) - dim - 1))

    loudness = one(*shards[0])
    for cut in shards[1:]:
        loudness = loudness * one(*cut)
    return loudness


def normal_values(own_key, dims, width, bound, cuts=(), kind=jnp.bfloat16):
    gain = levels(own_key, dims, cuts, -0.22, 0.18) if cuts else 1.0
    array = jax.random.normal(own_key, dims, jnp.float32) * width * gain
    return jnp.minimum(jnp.maximum(array, -bound), bound).astype(kind)


def setup_inputs(seed: int = 0) -> dict:
    streams_of = jax.random.split(jax.random.key(seed), 9)
    tests = normal_values(streams_of[0], (NX, K, 3, NY, NZ), 1.0, 6.0, ((0, 64), (3, 2)), jnp.float32)
    block_inverse = draw_block_inverse(jax.random.fold_in(streams_of[8], 71), 0)
    face_weight = jnp.clip(jnp.exp(math.log(1.0) - 1.2039728 * jax.random.uniform(streams_of[2], (NX, 6, NY, NZ), jnp.float32) ** levels(streams_of[2], (NX, 6, NY, NZ), ((0, 64), (2, 2)), -0.2, 0.2)), 0.3, 1.0)
    mixing = normal_values(streams_of[3], (6, 3, 3), 0.6, 3.0, (), jnp.float32)
    far_tiles = normal_values(streams_of[4], (NX, N_NARROW, NB, TILE, TILE), (TILE * NB) ** -0.5, 0.21875, ((0, 64), (1, 2)))
    far_column = with_ends(jax.random.randint(streams_of[5], (NX, N_NARROW, NB), 0, CX), jax.random.fold_in(streams_of[5], 1), 0, CX - 1).astype(jnp.int32)
    aggregate = draw_aggregate(jax.random.fold_in(streams_of[8], 71), 0)
    owner_map = draw_owner_map(jax.random.fold_in(streams_of[8], 71), 0)
    return dict(tests=tests, block_inverse=block_inverse, face_weight=face_weight, mixing=mixing, far_tiles=far_tiles, far_column=far_column, aggregate=aggregate, owner_map=owner_map)


omega_relax = 0.5
ridge_shift = 0.001

def mix_components(matrix, field_values):
    return jnp.stack([matrix[component, 0] * field_values[:, :, 0] + matrix[component, 1] * field_values[:, :, 1] + matrix[component, 2] * field_values[:, :, 2] for component in range(3)], axis=2)

def relax_step(field_values, padded, block_inverse, face_weight, mixing):
    zero_face = jnp.zeros_like(field_values[..., :1])
    neighbours = [padded[2:, :, :, 1:-1], padded[:-2, :, :, 1:-1], padded[1:-1, :, :, 2:], padded[1:-1, :, :, :-2], jnp.concatenate([field_values[..., 1:], zero_face], axis=4), jnp.concatenate([zero_face, field_values[..., :-1]], axis=4)]
    coupled = face_weight[:, 0][:, None, None] * mix_components(mixing[0], neighbours[0])
    for direction in range(1, 6):
        coupled = coupled + face_weight[:, direction][:, None, None] * mix_components(mixing[direction], neighbours[direction])
    jacobi = jnp.stack([block_inverse[:, component, 0][:, None] * coupled[:, :, 0] + block_inverse[:, component, 1][:, None] * coupled[:, :, 1] + block_inverse[:, component, 2][:, None] * coupled[:, :, 2] for component in range(3)], axis=2)
    return (1.0 - omega_relax) * field_values + omega_relax * jacobi

def factorize(matrices):
    order = matrices.shape[1]
    source = jnp.transpose(matrices, (1, 2, 0))
    row_ids = jnp.arange(order, dtype=jnp.int32)
    factor = jnp.zeros_like(source)
    for column in range(order):
        column_values = source[:, column, :] - lax.optimization_barrier(jnp.sum(factor * factor[column][None, :, :], axis=1))
        pivot = jnp.sqrt(column_values[column])
        keep = (row_ids >= column).astype(source.dtype)[:, None]
        factor = factor.at[:, column, :].set(keep * column_values / pivot[None, :])
    inverse = jnp.zeros_like(source)
    eye_table = jnp.eye(order, dtype=source.dtype)
    for row in range(order):
        row_values = eye_table[row][:, None] - lax.optimization_barrier(jnp.sum(factor[row][:, None, :] * inverse, axis=0))
        inverse = inverse.at[row].set(row_values / factor[row, row][None, :])
    return (jnp.transpose(factor, (2, 0, 1)), jnp.transpose(inverse, (2, 0, 1)))

def reference(tests, block_inverse, face_weight, mixing, far_tiles, far_column, aggregate, owner_map):
    relaxed = tests
    for sweep_index in range(SWEEPS):
        padded = jnp.pad(relaxed, ((1, 1), (0, 0), (0, 0), (1, 1), (0, 0)))
        relaxed = relax_step(relaxed, padded, block_inverse, face_weight, mixing)
    tile_nodes = CY * CZ
    plane_values = relaxed.astype(jnp.bfloat16).reshape(NX, K, 3, N_NARROW, CY, CZ).transpose(0, 3, 1, 2, 4, 5).reshape(NX, N_NARROW, 3 * K, tile_nodes)
    halves = jnp.arange(N_NARROW, dtype=jnp.int32)

    def far_rank(rank_index):
        tiles_rank = lax.dynamic_slice_in_dim(far_tiles, rank_index * CX, CX, 0)
        columns = lax.dynamic_slice_in_dim(far_column, rank_index * CX, CX, 0)
        running = jnp.zeros((CX, N_NARROW, 3 * K, tile_nodes), jnp.float32)
        for slot_index in range(NB):
            source_rank = ((rank_index + slot_index - REACH) % N_WIDE).astype(jnp.int32)
            source = lax.dynamic_slice_in_dim(plane_values, source_rank * CX, CX, 0)
            chosen = source[columns[:, :, slot_index].astype(jnp.int32), halves[None, :]]
            running = running + jnp.einsum('rnkj,rnji->rnki', chosen.astype(jnp.float32), tiles_rank[:, :, slot_index].astype(jnp.float32), precision=lax.Precision.HIGHEST)
        return running
    correction = lax.map(far_rank, jnp.arange(N_WIDE, dtype=jnp.int32))
    correction = correction.reshape(NX, N_NARROW, K, 3, CY, CZ).transpose(0, 2, 3, 1, 4, 5).reshape(NX, K, 3, NY, NZ)
    combined = relaxed + correction
    eye_k = jnp.eye(K, dtype=jnp.float32)

    def coarse_rank(rank_index):
        block_values = lax.dynamic_slice_in_dim(combined, rank_index * CX, CX, 0)
        labels = lax.dynamic_slice_in_dim(aggregate, rank_index * CX, CX, 0).reshape(-1).astype(jnp.int32)
        values = block_values.transpose(1, 2, 0, 3, 4).reshape(K, 3, CX * NY * NZ)
        outer_sum = lax.optimization_barrier(jnp.sum(values[:, None] * values[None, :], axis=2)).reshape(K * K, CX * NY * NZ).T
        gram_part = jax.ops.segment_sum(outer_sum, labels, num_segments=AGG_W)
        counts = jax.ops.segment_sum(jnp.ones(labels.shape, jnp.float32), labels, num_segments=AGG_W)
        shifted = gram_part.reshape(AGG_W, K, K) / (3.0 * counts)[:, None, None] + ridge_shift * eye_k
        lower_factor, inverse = factorize(shifted)
        lookup = inverse[labels].transpose(1, 2, 0)
        projected = lax.optimization_barrier(jnp.sum(lookup[:, :, None, :] * values[None, :, :, :], axis=1))
        prolong_rank = projected.reshape(K, 3, CX, NY, NZ).transpose(2, 0, 1, 3, 4)
        upper_rows = jnp.swapaxes(lower_factor, 1, 2).reshape(AGG_W, K * K)
        return (prolong_rank, upper_rows)
    prolong_parts, upper_rows = lax.map(coarse_rank, jnp.arange(N_WIDE, dtype=jnp.int32))
    prolong = prolong_parts.reshape(NX, K, 3, NY, NZ)
    owner_grid = owner_map.reshape(DEVICES, AGG_DEV).astype(jnp.int32)
    home_order = jnp.arange(AGG_DEV, dtype=jnp.int32)
    same_owner = (owner_grid[:, :, None] == owner_grid[:, None, :]) & (home_order[None, None, :] < home_order[None, :, None])
    within = lax.optimization_barrier(jnp.sum(same_owner.astype(jnp.int32), axis=2))
    slot_column = (jnp.arange(DEVICES, dtype=jnp.int32)[:, None] * SLOT + within).astype(jnp.int32)
    coarse_basis = jnp.zeros((DEVICES, DEVICES * SLOT, K * K), jnp.float32).at[owner_grid, slot_column].set(upper_rows.reshape(DEVICES, AGG_DEV, K * K))
    return (prolong, coarse_basis)
```

```python
import functools

import jax
import jax.numpy as jnp
from jax import lax
from jax.experimental import pallas as pl
from jax.experimental.pallas import tpu as pltpu
from jax.sharding import PartitionSpec as P

MESH = pl.DeviceIdType.MESH
SWEEPS = 3
SLOT = 2
K = 32
ROWS = 3 * K
PLANES = 16
NODES = 256
WIDTH = 128
RIDGE = 0.001

BLOCKS = [(k, b) for k in range(K) for b in range(k // 8, K // 8)]
TRI = 8 * len(BLOCKS)
STARTS = {}
for place, (block_k, block_b) in enumerate(BLOCKS):
    STARTS.setdefault(block_k, 8 * place)
GRAM_ROWS = TRI + 16


def split3(x):
    hi = x.astype(jnp.bfloat16)
    rest = x - hi.astype(jnp.float32)
    mid = rest.astype(jnp.bfloat16)
    low = (rest - mid.astype(jnp.float32)).astype(jnp.bfloat16)
    return hi, mid, low


def relax_kernel(
    n_wide,
    tests_hbm, bi_ref, fw_ref, mix_ref, tiles_hbm, col_ref, label_ref,
    comb_ref, gram_ref,
    x0, x1, x2, coef, ysend, yrecv, ydup, from_left, planes, from_right, tiles, outer, acc, gram_in,
    local_sems, xsend_sems, xrecv_sems, ysend_sems, yrecv_sems, psend_sems, precv_sems, gsend_sem, grecv_sem,
):
    w = lax.axis_index("wide")
    n = lax.axis_index("narrow")
    right = lax.rem(w + 1, n_wide)
    left = lax.rem(w + n_wide - 1, n_wide)
    other = 1 - n
    fields = [x0, x1, x2]

    tests_copy = pltpu.make_async_copy(tests_hbm, x0.at[pl.ds(1, PLANES)], local_sems.at[0])
    tests_copy.start()
    tiles_copy = pltpu.make_async_copy(tiles_hbm, tiles, local_sems.at[1])
    tiles_copy.start()

    barrier = pltpu.get_barrier_semaphore()
    for target in ((left, n), (right, n), (w, other)):
        pl.semaphore_signal(barrier, inc=1, device_id=target, device_id_type=MESH)
    pl.semaphore_wait(barrier, 3)

    lane = lax.broadcasted_iota(jnp.int32, (K + 16, WIDTH), 1)
    low_half = lane < 64
    is_low = n == 0

    def pack_row(first, second):
        chosen = jnp.where(is_low, second, first)
        turned = pltpu.roll(chosen, 64, 1)
        a = jnp.where(is_low, turned, chosen)[0:48]
        b = jnp.where(is_low, chosen, turned)[48:96]
        return jnp.where(low_half, a, b).astype(jnp.bfloat16)

    def y_copy(s):
        return pltpu.make_async_remote_copy(
            src_ref=ysend.at[s], dst_ref=yrecv.at[s], send_sem=ysend_sems.at[s], recv_sem=yrecv_sems.at[s],
            device_id=(w, other), device_id_type=MESH,
        )

    def x_copies(s):
        up = pltpu.make_async_remote_copy(
            src_ref=fields[s].at[PLANES], dst_ref=fields[s].at[0], send_sem=xsend_sems.at[2 * s],
            recv_sem=xrecv_sems.at[2 * s], device_id=(right, n), device_id_type=MESH,
        )
        down = pltpu.make_async_remote_copy(
            src_ref=fields[s].at[1], dst_ref=fields[s].at[PLANES + 1], send_sem=xsend_sems.at[2 * s + 1],
            recv_sem=xrecv_sems.at[2 * s + 1], device_id=(left, n), device_id_type=MESH,
        )
        return up, down

    tests_copy.wait()

    def pack_tests(p, carry):
        ysend[0, p] = pack_row(x0[p + 1, :, 0:128], x0[p + 1, :, 128:256])
        return carry

    for copy in x_copies(0):
        copy.start()
    lax.fori_loop(0, PLANES, pack_tests, 0)
    y_copy(0).start()

    lane_wide = lax.broadcasted_iota(jnp.int32, (8, NODES), 1)
    z_place = lax.rem(lane_wide, 64)

    def make_coef(p, carry):
        inv_rows = [jnp.broadcast_to(bi_ref[p, i : i + 1, :], (8, NODES)) for i in range(9)]
        edges = [
            jnp.logical_and(p == PLANES - 1, w == n_wide - 1),
            jnp.logical_and(p == 0, w == 0),
            jnp.logical_and(lane_wide >= 192, n == 1),
            jnp.logical_and(lane_wide < 64, n == 0),
            z_place == 63,
            z_place == 0,
        ]
        for d in range(6):
            weight = 0.5 * jnp.broadcast_to(fw_ref[p, d : d + 1, :], (8, NODES))
            weight = jnp.where(edges[d], 0.0, weight)
            for a in range(3):
                for b in range(3):
                    total = inv_rows[3 * a] * mix_ref[9 * d + b]
                    total += inv_rows[3 * a + 1] * mix_ref[9 * d + 3 + b]
                    total += inv_rows[3 * a + 2] * mix_ref[9 * d + 6 + b]
                    coef[p, 9 * d + 3 * a + b] = total * weight
        return carry

    lax.fori_loop(0, PLANES, make_coef, 0)

    low8 = low_half[0:8]

    def sweep_plane(s, p):
        src = fields[s]
        packed = yrecv[s, p].astype(jnp.float32)
        turned = pltpu.roll(packed, 64, 1)
        ydup[0:48] = jnp.where(low_half, packed, turned)
        ydup[48:96] = jnp.where(low_half, turned, packed)
        for kb in range(K // 8):
            near = []
            own = []
            for c in range(3):
                rows = pl.ds(c * K + kb * 8, 8)
                mid = src[p + 1, rows, :]
                own.append(mid)
                c0, c1 = mid[:, 0:128], mid[:, 128:256]
                r0, r1 = pltpu.roll(c0, 64, 1), pltpu.roll(c1, 64, 1)
                dup = ydup[rows]
                between = jnp.where(low8, r0, r1)
                y_up = jnp.concatenate([between, jnp.where(low8, r1, dup)], axis=1)
                y_down = jnp.concatenate([jnp.where(low8, dup, r0), between], axis=1)
                z_up = jnp.concatenate([pltpu.roll(c0, 127, 1), pltpu.roll(c1, 127, 1)], axis=1)
                z_down = jnp.concatenate([pltpu.roll(c0, 1, 1), pltpu.roll(c1, 1, 1)], axis=1)
                near.append([src[p + 2, rows, :], src[p, rows, :], y_up, y_down, z_up, z_down])
            for a in range(3):
                total = 0.5 * own[a]
                for d in range(6):
                    for b in range(3):
                        total += coef[p, 9 * d + 3 * a + b] * near[b][d]
                rows = pl.ds(a * K + kb * 8, 8)
                if s + 1 < SWEEPS:
                    fields[s + 1][p + 1, rows, :] = total
                else:
                    comb_ref[p, rows, :] = total

    def wait_sweep(s):
        for copy in x_copies(s):
            copy.wait()
        y_copy(s).wait()

    for s in range(SWEEPS - 1):
        wait_sweep(s)

        def one_plane(p, carry, s=s):
            sweep_plane(s, p)
            ysend[s + 1, p] = pack_row(fields[s + 1][p + 1, :, 0:128], fields[s + 1][p + 1, :, 128:256])
            return carry

        lax.fori_loop(0, PLANES, one_plane, 0)
        for copy in x_copies(s + 1):
            copy.start()
        y_copy(s + 1).start()

    wait_sweep(SWEEPS - 1)
    chunk_planes = 4
    chunks = PLANES // chunk_planes

    def plane_copies(q):
        span = pl.ds(q * chunk_planes, chunk_planes)
        up = pltpu.make_async_remote_copy(
            src_ref=planes.at[span], dst_ref=from_left.at[span], send_sem=psend_sems.at[2 * q],
            recv_sem=precv_sems.at[2 * q], device_id=(right, n), device_id_type=MESH,
        )
        down = pltpu.make_async_remote_copy(
            src_ref=planes.at[span], dst_ref=from_right.at[span], send_sem=psend_sems.at[2 * q + 1],
            recv_sem=precv_sems.at[2 * q + 1], device_id=(left, n), device_id_type=MESH,
        )
        return up, down

    for q in range(chunks):

        def last_plane(p, carry):
            sweep_plane(SWEEPS - 1, p)
            planes[p] = comb_ref[p].astype(jnp.bfloat16)
            return carry

        lax.fori_loop(q * chunk_planes, (q + 1) * chunk_planes, last_plane, 0)
        for copy in plane_copies(q):
            copy.start()

    tiles_copy.wait()

    acc[...] = jnp.zeros_like(acc)
    ones = jnp.ones((16, NODES), jnp.bfloat16)
    outer[0, TRI:GRAM_ROWS] = ones
    outer[1, TRI:GRAM_ROWS] = jnp.zeros_like(ones)
    outer[2, TRI:GRAM_ROWS] = jnp.zeros_like(ones)

    sources = [from_left, planes, from_right]

    def far_product(r, slot):
        return jnp.dot(
            sources[slot][col_ref[r, slot]], tiles[r, slot], preferred_element_type=jnp.float32
        )

    def near_far(r, carry):
        comb_ref[r] = comb_ref[r] + far_product(r, 1)
        return carry

    lax.fori_loop(0, PLANES, near_far, 0)

    for q in range(chunks):
        for copy in plane_copies(q):
            copy.wait()

    groups = lax.broadcasted_iota(jnp.int32, (WIDTH, NODES), 0)

    def gram_plane(r, carry):
        comb_ref[r] = comb_ref[r] + (far_product(r, 0) + far_product(r, 2))
        member = jnp.where(groups == label_ref[r], 1.0, 0.0).astype(jnp.bfloat16)
        for pair in range(len(BLOCKS) // 2):
            parts = []
            for k, b in BLOCKS[2 * pair : 2 * pair + 2]:
                value = None
                for c in range(3):
                    term = comb_ref[r, c * K + k : c * K + k + 1, :] * comb_ref[r, pl.ds(c * K + 8 * b, 8), :]
                    value = term if value is None else value + term
                parts.append(value)
            pieces = split3(jnp.concatenate(parts, axis=0))
            for i in range(3):
                outer[i, pl.ds(16 * pair, 16), :] = pieces[i]
        total = None
        for i in range(3):
            term = lax.dot_general(
                outer[i], member, (((1,), (1,)), ((), ())), preferred_element_type=jnp.float32
            )
            total = term if total is None else total + term
        acc[...] += total
        return carry

    lax.fori_loop(0, PLANES, gram_plane, 0)

    gram_copy = pltpu.make_async_remote_copy(
        src_ref=acc, dst_ref=gram_in, send_sem=gsend_sem.at[0], recv_sem=grecv_sem.at[0],
        device_id=(w, other), device_id_type=MESH,
    )
    gram_copy.start()
    gram_copy.wait()
    gram_ref[...] = acc[...] + gram_in[...]


def factor_kernel(gram_ref, table_ref, packed_ref, inverse_ref, lower, inv):
    scale = 1.0 / (3.0 * gram_ref[TRI : TRI + 1, :])
    row = lax.broadcasted_iota(jnp.int32, (K, WIDTH), 0)
    columns = []
    for k in range(K):
        first = 8 * (k // 8)
        height = K - first
        column = gram_ref[pl.ds(STARTS[k], height), :] * scale
        columns.append(column + jnp.where(row[first:] == k, RIDGE, 0.0))
    reciprocals = []
    for k in range(K):
        first = 8 * (k // 8)
        at = k - first
        pivot = jnp.sqrt(columns[k][at : at + 1])
        reciprocal = 1.0 / pivot
        reciprocals.append(reciprocal)
        column = jnp.where(row[first:] >= k, columns[k] * reciprocal, 0.0)
        columns[k] = column
        for m in range(k + 1, K):
            begin = 8 * (m // 8)
            columns[m] = columns[m] - column[m - first : m - first + 1] * column[begin - first :]
        lower[pl.ds(K * k, K), :] = (
            column if first == 0 else jnp.concatenate([jnp.zeros((first, WIDTH), jnp.float32), column], axis=0)
        )
    for l in range(K):
        first = 8 * (l // 8)
        solved = jnp.where(row[first:] == l, 1.0, 0.0)
        for m in range(l, K):
            base = 8 * (m // 8)
            value = solved[m - first : m - first + 1] * reciprocals[m]
            here = solved[base - first :]
            here = jnp.where(row[base:] == m, value, jnp.where(row[base:] > m, here - columns[m] * value, here))
            solved = here if base == first else jnp.concatenate([solved[: base - first], here], axis=0)
        inv[pl.ds(STARTS[l], K - first), :] = solved
    for i, piece in enumerate(split3(inv[...])):
        inverse_ref[:, i * WIDTH : (i + 1) * WIDTH] = piece
    table = table_ref[...]
    total = None
    for piece in split3(lower[...]):
        term = lax.dot_general(table, piece, (((1,), (1,)), ((), ())), preferred_element_type=jnp.float32)
        total = term if total is None else total + term
    packed_ref[...] = total


def project_kernel(comb_ref, label_ref, inverse_ref, out_ref, look):
    groups = lax.broadcasted_iota(jnp.int32, (WIDTH, NODES), 0)
    member = jnp.where(groups == label_ref[0], 1.0, 0.0).astype(jnp.bfloat16)
    look[...] = jnp.dot(
        inverse_ref[...], jnp.concatenate([member, member, member], axis=0), preferred_element_type=jnp.float32
    )
    for b in range(K // 8):
        totals = [None] * 3
        for l in range(8 * (b + 1)):
            weight = look[pl.ds(STARTS[l] + 8 * (b - l // 8), 8), :]
            for c in range(3):
                term = weight * comb_ref[0, c * K + l : c * K + l + 1, :]
                totals[c] = term if totals[c] is None else totals[c] + term
        for c in range(3):
            out_ref[0, pl.ds(c * K + 8 * b, 8), :] = totals[c]


def vmem(shape, dtype=jnp.float32):
    return pltpu.VMEM(shape, dtype)


def shards(n_wide, n_narrow, tests, block_inverse, face_weight, mixing, far_tiles, far_column, aggregate, owner_map):
    bf16 = jnp.bfloat16
    whole = pl.BlockSpec(memory_space=pltpu.VMEM)
    any_spec = pl.BlockSpec(memory_space=pl.ANY)
    smem = pl.BlockSpec(memory_space=pltpu.SMEM)
    field = tests.reshape(PLANES, K, 3, NODES).transpose(0, 2, 1, 3).reshape(PLANES, ROWS, NODES)
    labels = aggregate.reshape(PLANES, 1, NODES)

    agg_dev = owner_map.shape[0]
    slot_order = jnp.arange(agg_dev, dtype=jnp.int32)
    same_owner = (owner_map[:, None] == owner_map[None, :]) & (slot_order[None, :] < slot_order[:, None])
    within = jnp.sum(same_owner.astype(jnp.int32), axis=1)
    target = owner_map * SLOT + within
    slots_total = n_wide * n_narrow * SLOT
    own_lane = jnp.arange(WIDTH, dtype=jnp.int32) // agg_dev == lax.axis_index("narrow")
    target_lane = jnp.where(own_lane, jnp.tile(target, n_narrow), -1)
    table = (jnp.arange(slots_total, dtype=jnp.int32)[:, None] == target_lane[None, :]).astype(bf16)

    combined, gram = pl.pallas_call(
        functools.partial(relax_kernel, n_wide),
        out_shape=(
            jax.ShapeDtypeStruct((PLANES, ROWS, NODES), jnp.float32),
            jax.ShapeDtypeStruct((GRAM_ROWS, WIDTH), jnp.float32),
        ),
        in_specs=[any_spec, whole, whole, smem, any_spec, smem, whole],
        out_specs=(whole, whole),
        scratch_shapes=[
            vmem((PLANES + 2, ROWS, NODES)),
            vmem((PLANES + 2, ROWS, NODES)),
            vmem((PLANES + 2, ROWS, NODES)),
            vmem((PLANES, 54, 8, NODES)),
            vmem((SWEEPS, PLANES, 48, WIDTH), bf16),
            vmem((SWEEPS, PLANES, 48, WIDTH), bf16),
            vmem((ROWS, WIDTH)),
            vmem((PLANES, ROWS, NODES), bf16),
            vmem((PLANES, ROWS, NODES), bf16),
            vmem((PLANES, ROWS, NODES), bf16),
            vmem((PLANES, 3, NODES, NODES), bf16),
            vmem((3, GRAM_ROWS, NODES), bf16),
            vmem((GRAM_ROWS, WIDTH)),
            vmem((GRAM_ROWS, WIDTH)),
            pltpu.SemaphoreType.DMA((2,)),
            pltpu.SemaphoreType.DMA((2 * SWEEPS,)),
            pltpu.SemaphoreType.DMA((2 * SWEEPS,)),
            pltpu.SemaphoreType.DMA((SWEEPS,)),
            pltpu.SemaphoreType.DMA((SWEEPS,)),
            pltpu.SemaphoreType.DMA((8,)),
            pltpu.SemaphoreType.DMA((8,)),
            pltpu.SemaphoreType.DMA((1,)),
            pltpu.SemaphoreType.DMA((1,)),
        ],
        compiler_params=pltpu.CompilerParams(
            collective_id=0, has_side_effects=True, vmem_limit_bytes=56 * 1024 * 1024
        ),
        name="relax_far_gram",
    )(
        field,
        block_inverse.reshape(PLANES, 9, NODES),
        face_weight.reshape(PLANES, 6, NODES),
        mixing.reshape(54),
        far_tiles.reshape(PLANES, 3, NODES, NODES),
        far_column.reshape(PLANES, 3),
        labels,
    )

    packed, inverse = pl.pallas_call(
        factor_kernel,
        out_shape=(
            jax.ShapeDtypeStruct((slots_total, K * K), jnp.float32),
            jax.ShapeDtypeStruct((TRI, 3 * WIDTH), bf16),
        ),
        in_specs=[whole, whole],
        out_specs=(whole, whole),
        scratch_shapes=[vmem((K * K, WIDTH)), vmem((TRI, WIDTH))],
        compiler_params=pltpu.CompilerParams(vmem_limit_bytes=32 * 1024 * 1024),
        name="factor",
    )(gram, table)

    received = lax.all_to_all(
        packed.reshape(n_wide * n_narrow, SLOT, K * K), ("wide", "narrow"), split_axis=0, concat_axis=0, tiled=True
    )

    projected = pl.pallas_call(
        project_kernel,
        grid=(PLANES,),
        out_shape=jax.ShapeDtypeStruct((PLANES, ROWS, NODES), jnp.float32),
        in_specs=[
            pl.BlockSpec((1, ROWS, NODES), lambda r: (r, 0, 0)),
            pl.BlockSpec((1, 1, NODES), lambda r: (r, 0, 0)),
            whole,
        ],
        out_specs=pl.BlockSpec((1, ROWS, NODES), lambda r: (r, 0, 0)),
        scratch_shapes=[vmem((TRI, NODES))],
        compiler_params=pltpu.CompilerParams(vmem_limit_bytes=32 * 1024 * 1024),
        cost_estimate=pl.CostEstimate(flops=8_000_000_000, bytes_accessed=4_000_000, transcendentals=0),
        name="project",
    )(combined, labels, inverse)
    prolong = projected.reshape(PLANES, 3, K, NODES).transpose(0, 2, 1, 3).reshape(tests.shape)
    return prolong, received.reshape(1, slots_total, K * K)


def solution(mesh):
    in_specs = (
        P("wide", None, None, "narrow", None),
        P("wide", None, None, "narrow", None),
        P("wide", None, "narrow", None),
        P(),
        P("wide", "narrow", None, None, None),
        P("wide", "narrow", None),
        P("wide", "narrow", None),
        P(("wide", "narrow")),
    )
    out_specs = (P("wide", None, None, "narrow", None), P(("wide", "narrow"), None, None))
    body = functools.partial(shards, mesh.shape["wide"], mesh.shape["narrow"])
    return jax.shard_map(body, mesh=mesh, in_specs=in_specs, out_specs=out_specs, check_vma=False)
```

```python
import functools

import jax
import jax.numpy as jnp
from jax import lax
from jax.experimental import pallas as pl
from jax.experimental.pallas import tpu as pltpu
from jax.sharding import PartitionSpec as P

MESH = pl.DeviceIdType.MESH
SWEEPS = 3
SLOT = 2
K = 32
ROWS = 3 * K
PLANES = 16
NODES = 256
WIDTH = 128
RIDGE = 0.001

BLOCKS = [(k, b) for k in range(K) for b in range(k // 8, K // 8)]
TRI = 8 * len(BLOCKS)
STARTS = {}
for place, (block_k, block_b) in enumerate(BLOCKS):
    STARTS.setdefault(block_k, 8 * place)
GRAM_ROWS = TRI + 16
CHUNKS = 4
PART = PLANES // CHUNKS


def split3(x):
    hi = x.astype(jnp.bfloat16)
    rest = x - hi.astype(jnp.float32)
    mid = rest.astype(jnp.bfloat16)
    low = (rest - mid.astype(jnp.float32)).astype(jnp.bfloat16)
    return hi, mid, low


def join_rows(rows):
    return jnp.concatenate(rows, axis=1)


def relax_kernel(
    n_wide,
    tests_hbm, bi_ref, fw_ref, mix_ref, tiles_hbm, col_ref, label_ref,
    comb_ref, gram_ref,
    raw, x0, x1, x2, coef, ysend, yrecv, ydup, from_left, planes, from_right, tiles, members, outer, acc, gram_in,
    tests_sems, tiles_sem, xsend_sems, xrecv_sems, ysend_sems, yrecv_sems, psend_sems, precv_sems, gsend_sems,
    grecv_sems,
):
    w = lax.axis_index("wide")
    n = lax.axis_index("narrow")
    right = lax.rem(w + 1, n_wide)
    left = lax.rem(w + n_wide - 1, n_wide)
    other = 1 - n
    fields = [x0, x1, x2]

    def plane_at(i):
        half = i // 2
        return jnp.where(lax.rem(i, 2) == 0, half, PLANES - 1 - half)

    tests_copies = []
    for q in range(CHUNKS):
        for j, start in enumerate((2 * q, PLANES - 2 - 2 * q)):
            span = pl.ds(start, 2)
            copy = pltpu.make_async_copy(tests_hbm.at[span], raw.at[span], tests_sems.at[2 * q + j])
            copy.start()
            tests_copies.append(copy)
    tiles_copy = pltpu.make_async_copy(tiles_hbm, tiles, tiles_sem.at[0])
    tiles_copy.start()

    barrier = pltpu.get_barrier_semaphore()
    for target in ((left, n), (right, n), (w, other)):
        pl.semaphore_signal(barrier, inc=1, device_id=target, device_id_type=MESH)

    lane = lax.broadcasted_iota(jnp.int32, (K + 16, WIDTH), 1)
    low_half = lane < 64
    low8 = low_half[0:8]
    is_low = n == 0

    def pack_row(first, second):
        chosen = jnp.where(is_low, second, first)
        turned = pltpu.roll(chosen, 64, 1)
        a = jnp.where(is_low, turned, chosen)[0:48]
        b = jnp.where(is_low, chosen, turned)[48:96]
        return jnp.where(low_half, a, b).astype(jnp.bfloat16)

    def y_copy(s, q):
        span = pl.ds(q * PART, PART)
        return pltpu.make_async_remote_copy(
            src_ref=ysend.at[s, span], dst_ref=yrecv.at[s, span], send_sem=ysend_sems.at[s * CHUNKS + q],
            recv_sem=yrecv_sems.at[s * CHUNKS + q], device_id=(w, other), device_id_type=MESH,
        )

    def x_copies(s):
        up = pltpu.make_async_remote_copy(
            src_ref=fields[s].at[PLANES], dst_ref=fields[s].at[0], send_sem=xsend_sems.at[2 * s],
            recv_sem=xrecv_sems.at[2 * s], device_id=(right, n), device_id_type=MESH,
        )
        down = pltpu.make_async_remote_copy(
            src_ref=fields[s].at[1], dst_ref=fields[s].at[PLANES + 1], send_sem=xsend_sems.at[2 * s + 1],
            recv_sem=xrecv_sems.at[2 * s + 1], device_id=(left, n), device_id_type=MESH,
        )
        return up, down

    def start_x(s):
        for copy in x_copies(s):
            copy.start()

    def unpack_tests(i, carry):
        p = plane_at(i)
        for c in range(3):
            for kb in range(K // 8):
                pieces = [raw[p, pl.ds(96 * kb + 4 * c + y, 8, stride=12), :] for y in range(4)]
                x0[p + 1, pl.ds(c * K + 8 * kb, 8), :] = join_rows(pieces)
        ysend[0, i] = pack_row(x0[p + 1, :, 0:128], x0[p + 1, :, 128:256])
        return carry

    for q in range(CHUNKS):
        tests_copies[2 * q].wait()
        tests_copies[2 * q + 1].wait()
        lax.fori_loop(q * PART, (q + 1) * PART, unpack_tests, 0)
        if q == 0:
            pl.semaphore_wait(barrier, 3)
            start_x(0)
        y_copy(0, q).start()

    lane_wide = lax.broadcasted_iota(jnp.int32, (8, NODES), 1)
    z_place = lax.rem(lane_wide, 64)

    def make_coef(p, carry):
        def wide_row(ref, first):
            row = join_rows([ref[pl.ds(first + y, 1), :] for y in range(4)])
            return jnp.broadcast_to(row, (8, NODES))

        inv_rows = [wide_row(bi_ref, 36 * p + 4 * i) for i in range(9)]
        edges = [
            jnp.logical_and(p == PLANES - 1, w == n_wide - 1),
            jnp.logical_and(p == 0, w == 0),
            jnp.logical_and(lane_wide >= 192, n == 1),
            jnp.logical_and(lane_wide < 64, n == 0),
            z_place == 63,
            z_place == 0,
        ]
        for d in range(6):
            weight = jnp.where(edges[d], 0.0, 0.5 * wide_row(fw_ref, 24 * p + 4 * d))
            for a in range(3):
                for b in range(3):
                    total = inv_rows[3 * a] * mix_ref[9 * d + b]
                    total += inv_rows[3 * a + 1] * mix_ref[9 * d + 3 + b]
                    total += inv_rows[3 * a + 2] * mix_ref[9 * d + 6 + b]
                    coef[p, 9 * d + 3 * a + b] = total * weight
        label = join_rows([label_ref[pl.ds(4 * p + y, 1), :] for y in range(4)])
        groups = lax.broadcasted_iota(jnp.int32, (WIDTH, NODES), 0)
        members[p] = jnp.where(groups == label, 1.0, 0.0).astype(jnp.bfloat16)
        return carry

    lax.fori_loop(0, PLANES, make_coef, 0)

    def sweep_plane(s, i):
        p = plane_at(i)
        src = fields[s]
        packed = yrecv[s, i].astype(jnp.float32)
        turned = pltpu.roll(packed, 64, 1)
        ydup[0:48] = jnp.where(low_half, packed, turned)
        ydup[48:96] = jnp.where(low_half, turned, packed)
        for kb in range(K // 8):
            near = []
            own = []
            for c in range(3):
                rows = pl.ds(c * K + kb * 8, 8)
                mid = src[p + 1, rows, :]
                own.append(mid)
                c0, c1 = mid[:, 0:128], mid[:, 128:256]
                r0, r1 = pltpu.roll(c0, 64, 1), pltpu.roll(c1, 64, 1)
                dup = ydup[rows]
                between = jnp.where(low8, r0, r1)
                y_up = jnp.concatenate([between, jnp.where(low8, r1, dup)], axis=1)
                y_down = jnp.concatenate([jnp.where(low8, dup, r0), between], axis=1)
                z_up = jnp.concatenate([pltpu.roll(c0, 127, 1), pltpu.roll(c1, 127, 1)], axis=1)
                z_down = jnp.concatenate([pltpu.roll(c0, 1, 1), pltpu.roll(c1, 1, 1)], axis=1)
                near.append([src[p + 2, rows, :], src[p, rows, :], y_up, y_down, z_up, z_down])
            for a in range(3):
                total = 0.5 * own[a]
                for d in range(6):
                    for b in range(3):
                        total += coef[p, 9 * d + 3 * a + b] * near[b][d]
                rows = pl.ds(a * K + kb * 8, 8)
                if s + 1 < SWEEPS:
                    fields[s + 1][p + 1, rows, :] = total
                else:
                    comb_ref[p, rows, :] = total
        if s + 1 < SWEEPS:
            ysend[s + 1, i] = pack_row(fields[s + 1][p + 1, :, 0:128], fields[s + 1][p + 1, :, 128:256])
        else:
            planes[p] = comb_ref[p].astype(jnp.bfloat16)

    def plane_copies(q):
        copies = []
        for j, start in enumerate((2 * q, PLANES - 2 - 2 * q)):
            span = pl.ds(start, 2)
            for side, (target, landing) in enumerate(((right, from_left), (left, from_right))):
                at = 4 * q + 2 * j + side
                copies.append(
                    pltpu.make_async_remote_copy(
                        src_ref=planes.at[span], dst_ref=landing.at[span], send_sem=psend_sems.at[at],
                        recv_sem=precv_sems.at[at], device_id=(target, n), device_id_type=MESH,
                    )
                )
        return copies

    for s in range(SWEEPS):
        for copy in x_copies(s):
            copy.wait()

        def one_chunk(q, carry, s=s):
            y_copy(s, q).wait()

            def one_plane(j, inner):
                sweep_plane(s, q * PART + j)
                if s + 1 < SWEEPS:
                    pl.when(jnp.logical_and(q == 0, j == 1))(lambda: start_x(s + 1))
                return inner

            lax.fori_loop(0, PART, one_plane, 0)
            if s + 1 < SWEEPS:
                y_copy(s + 1, q).start()
            else:
                for copy in plane_copies(q):
                    copy.start()
            return carry

        lax.fori_loop(0, CHUNKS, one_chunk, 0)

    tiles_copy.wait()
    sources = [from_left, planes, from_right]

    def far_product(r, slot):
        return jnp.dot(
            sources[slot][col_ref[r, slot]], tiles[r, slot], preferred_element_type=jnp.float32
        )

    def near_far(r, carry):
        comb_ref[r] = comb_ref[r] + far_product(r, 1)
        return carry

    lax.fori_loop(0, PLANES, near_far, 0)

    acc[...] = jnp.zeros_like(acc)
    for q in range(CHUNKS):
        for copy in plane_copies(q):
            copy.wait()

    def side_far(r, carry):
        comb_ref[r] = comb_ref[r] + (far_product(r, 0) + far_product(r, 2))
        return carry

    lax.fori_loop(0, PLANES, side_far, 0)

    pairs = len(BLOCKS) // 2 // CHUNKS
    rows_part = 16 * pairs

    def gram_copy(t):
        height = rows_part if t + 1 < CHUNKS else GRAM_ROWS - rows_part * t
        span = pl.ds(rows_part * t, height)
        return pltpu.make_async_remote_copy(
            src_ref=acc.at[span], dst_ref=gram_in.at[span], send_sem=gsend_sems.at[t], recv_sem=grecv_sems.at[t],
            device_id=(w, other), device_id_type=MESH,
        )

    def contract(values, member):
        return lax.dot_general(values, member, (((1,), (1,)), ((), ())), preferred_element_type=jnp.float32)

    for t in range(CHUNKS):

        def gram_planes(h, carry, t=t):
            for side in range(2):
                r = 2 * h + side
                lanes = pl.ds(side * NODES, NODES)
                for pair in range(pairs):
                    parts = []
                    for k, b in BLOCKS[2 * (pairs * t + pair) : 2 * (pairs * t + pair) + 2]:
                        value = None
                        for c in range(3):
                            term = comb_ref[r, c * K + k : c * K + k + 1, :] * comb_ref[r, pl.ds(c * K + 8 * b, 8), :]
                            value = term if value is None else value + term
                        parts.append(value)
                    for piece, values in enumerate(split3(jnp.concatenate(parts, axis=0))):
                        outer[piece, pl.ds(16 * pair, 16), lanes] = values
            total = None
            for side in range(2):
                member = members[2 * h + side]
                lanes = pl.ds(side * NODES, NODES)
                for piece in range(3):
                    term = contract(outer[piece, :, lanes], member)
                    total = term if total is None else total + term
            acc[pl.ds(rows_part * t, rows_part), :] += total
            if t + 1 == CHUNKS:
                ones = jnp.ones((16, NODES), jnp.bfloat16)
                acc[TRI:GRAM_ROWS] += contract(ones, members[2 * h]) + contract(ones, members[2 * h + 1])
            return carry

        lax.fori_loop(0, PLANES // 2, gram_planes, 0)
        gram_copy(t).start()

    for t in range(CHUNKS):
        gram_copy(t).wait()
    gram_ref[...] = acc[...] + gram_in[...]


def factor_kernel(gram_ref, table_ref, packed_ref, inverse_ref, lower, inv):
    scale = 1.0 / (3.0 * gram_ref[TRI : TRI + 1, :])
    row = lax.broadcasted_iota(jnp.int32, (K, WIDTH), 0)
    columns = []
    for k in range(K):
        first = 8 * (k // 8)
        height = K - first
        column = gram_ref[pl.ds(STARTS[k], height), :] * scale
        columns.append(column + jnp.where(row[first:] == k, RIDGE, 0.0))
    reciprocals = []
    for k in range(K):
        first = 8 * (k // 8)
        at = k - first
        pivot = jnp.sqrt(columns[k][at : at + 1])
        reciprocal = 1.0 / pivot
        reciprocals.append(reciprocal)
        column = jnp.where(row[first:] >= k, columns[k] * reciprocal, 0.0)
        columns[k] = column
        for m in range(k + 1, K):
            begin = 8 * (m // 8)
            columns[m] = columns[m] - column[m - first : m - first + 1] * column[begin - first :]
        lower[pl.ds(K * k, K), :] = (
            column if first == 0 else jnp.concatenate([jnp.zeros((first, WIDTH), jnp.float32), column], axis=0)
        )
    for l in range(K):
        first = 8 * (l // 8)
        solved = jnp.where(row[first:] == l, 1.0, 0.0)
        for m in range(l, K):
            base = 8 * (m // 8)
            value = solved[m - first : m - first + 1] * reciprocals[m]
            here = solved[base - first :]
            here = jnp.where(row[base:] == m, value, jnp.where(row[base:] > m, here - columns[m] * value, here))
            solved = here if base == first else jnp.concatenate([solved[: base - first], here], axis=0)
        inv[pl.ds(STARTS[l], K - first), :] = solved
    for i, piece in enumerate(split3(inv[...])):
        inverse_ref[:, i * WIDTH : (i + 1) * WIDTH] = piece
    table = table_ref[...]
    total = None
    for piece in split3(lower[...]):
        term = lax.dot_general(table, piece, (((1,), (1,)), ((), ())), preferred_element_type=jnp.float32)
        total = term if total is None else total + term
    packed_ref[...] = total


def project_kernel(comb_ref, label_ref, inverse_ref, out_ref, look):
    groups = lax.broadcasted_iota(jnp.int32, (WIDTH, NODES), 0)
    r = pl.program_id(0)
    label = join_rows([label_ref[pl.ds(4 * r + y, 1), :] for y in range(4)])
    member = jnp.where(groups == label, 1.0, 0.0).astype(jnp.bfloat16)
    look[...] = jnp.dot(
        inverse_ref[...], jnp.concatenate([member, member, member], axis=0), preferred_element_type=jnp.float32
    )
    for b in range(K // 8):
        totals = [None] * 3
        for l in range(8 * (b + 1)):
            weight = look[pl.ds(STARTS[l] + 8 * (b - l // 8), 8), :]
            for c in range(3):
                term = weight * comb_ref[0, c * K + l : c * K + l + 1, :]
                totals[c] = term if totals[c] is None else totals[c] + term
        for c in range(3):
            for y in range(4):
                out_ref[0, pl.ds(96 * b + 4 * c + y, 8, stride=12), :] = totals[c][:, 64 * y : 64 * (y + 1)]


def vmem(shape, dtype=jnp.float32):
    return pltpu.VMEM(shape, dtype)


def shards(n_wide, n_narrow, tests, block_inverse, face_weight, mixing, far_tiles, far_column, aggregate, owner_map):
    bf16 = jnp.bfloat16
    whole = pl.BlockSpec(memory_space=pltpu.VMEM)
    any_spec = pl.BlockSpec(memory_space=pl.ANY)
    smem = pl.BlockSpec(memory_space=pltpu.SMEM)
    labels = aggregate.reshape(PLANES * 4, 64)

    agg_dev = owner_map.shape[0]
    slot_order = jnp.arange(agg_dev, dtype=jnp.int32)
    same_owner = (owner_map[:, None] == owner_map[None, :]) & (slot_order[None, :] < slot_order[:, None])
    within = jnp.sum(same_owner.astype(jnp.int32), axis=1)
    target = owner_map * SLOT + within
    slots_total = n_wide * n_narrow * SLOT
    own_lane = jnp.arange(WIDTH, dtype=jnp.int32) // agg_dev == lax.axis_index("narrow")
    target_lane = jnp.where(own_lane, jnp.tile(target, n_narrow), -1)
    table = (jnp.arange(slots_total, dtype=jnp.int32)[:, None] == target_lane[None, :]).astype(bf16)

    combined, gram = pl.pallas_call(
        functools.partial(relax_kernel, n_wide),
        out_shape=(
            jax.ShapeDtypeStruct((PLANES, ROWS, NODES), jnp.float32),
            jax.ShapeDtypeStruct((GRAM_ROWS, WIDTH), jnp.float32),
        ),
        in_specs=[any_spec, whole, whole, smem, any_spec, smem, whole],
        out_specs=(whole, whole),
        scratch_shapes=[
            vmem((PLANES, 4 * ROWS, 64)),
            vmem((PLANES + 2, ROWS, NODES)),
            vmem((PLANES + 2, ROWS, NODES)),
            vmem((PLANES + 2, ROWS, NODES)),
            vmem((PLANES, 54, 8, NODES)),
            vmem((SWEEPS, PLANES, 48, WIDTH), bf16),
            vmem((SWEEPS, PLANES, 48, WIDTH), bf16),
            vmem((ROWS, WIDTH)),
            vmem((PLANES, ROWS, NODES), bf16),
            vmem((PLANES, ROWS, NODES), bf16),
            vmem((PLANES, ROWS, NODES), bf16),
            vmem((PLANES, 3, NODES, NODES), bf16),
            vmem((PLANES, WIDTH, NODES), bf16),
            vmem((3, TRI // CHUNKS, 2 * NODES), bf16),
            vmem((GRAM_ROWS, WIDTH)),
            vmem((GRAM_ROWS, WIDTH)),
            pltpu.SemaphoreType.DMA((2 * CHUNKS,)),
            pltpu.SemaphoreType.DMA((1,)),
            pltpu.SemaphoreType.DMA((2 * SWEEPS,)),
            pltpu.SemaphoreType.DMA((2 * SWEEPS,)),
            pltpu.SemaphoreType.DMA((SWEEPS * CHUNKS,)),
            pltpu.SemaphoreType.DMA((SWEEPS * CHUNKS,)),
            pltpu.SemaphoreType.DMA((4 * CHUNKS,)),
            pltpu.SemaphoreType.DMA((4 * CHUNKS,)),
            pltpu.SemaphoreType.DMA((CHUNKS,)),
            pltpu.SemaphoreType.DMA((CHUNKS,)),
        ],
        compiler_params=pltpu.CompilerParams(
            collective_id=0, has_side_effects=True, vmem_limit_bytes=56 * 1024 * 1024
        ),
        name="relax_far_gram",
    )(
        tests.reshape(PLANES, 4 * ROWS, 64),
        block_inverse.reshape(PLANES * 36, 64),
        face_weight.reshape(PLANES * 24, 64),
        mixing.reshape(54),
        far_tiles.reshape(PLANES, 3, NODES, NODES),
        far_column.reshape(PLANES, 3),
        labels,
    )

    packed, inverse = pl.pallas_call(
        factor_kernel,
        out_shape=(
            jax.ShapeDtypeStruct((slots_total, K * K), jnp.float32),
            jax.ShapeDtypeStruct((TRI, 3 * WIDTH), bf16),
        ),
        in_specs=[whole, whole],
        out_specs=(whole, whole),
        scratch_shapes=[vmem((K * K, WIDTH)), vmem((TRI, WIDTH))],
        compiler_params=pltpu.CompilerParams(vmem_limit_bytes=32 * 1024 * 1024),
        name="factor",
    )(gram, table)

    received = lax.all_to_all(
        packed.reshape(n_wide * n_narrow, SLOT, K * K), ("wide", "narrow"), split_axis=0, concat_axis=0, tiled=True
    )

    projected = pl.pallas_call(
        project_kernel,
        grid=(PLANES,),
        out_shape=jax.ShapeDtypeStruct((PLANES, 4 * ROWS, 64), jnp.float32),
        in_specs=[pl.BlockSpec((1, ROWS, NODES), lambda r: (r, 0, 0)), whole, whole],
        out_specs=pl.BlockSpec((1, 4 * ROWS, 64), lambda r: (r, 0, 0)),
        scratch_shapes=[vmem((TRI, NODES))],
        compiler_params=pltpu.CompilerParams(vmem_limit_bytes=32 * 1024 * 1024),
        cost_estimate=pl.CostEstimate(flops=8_000_000_000, bytes_accessed=4_000_000, transcendentals=0),
        name="project",
    )(combined, labels, inverse)
    prolong = projected.reshape(tests.shape)
    return prolong, received.reshape(1, slots_total, K * K)


def solution(mesh):
    in_specs = (
        P("wide", None, None, "narrow", None),
        P("wide", None, None, "narrow", None),
        P("wide", None, "narrow", None),
        P(),
        P("wide", "narrow", None, None, None),
        P("wide", "narrow", None),
        P("wide", "narrow", None),
        P(("wide", "narrow")),
    )
    out_specs = (P("wide", None, None, "narrow", None), P(("wide", "narrow"), None, None))
    body = functools.partial(shards, mesh.shape["wide"], mesh.shape["narrow"])
    return jax.shard_map(body, mesh=mesh, in_specs=in_specs, out_specs=out_specs, check_vma=False)
```

```python
import functools

import jax
import jax.numpy as jnp
from jax import lax
from jax.experimental import pallas as pl
from jax.experimental.pallas import tpu as pltpu
from jax.sharding import PartitionSpec as P

MESH = pl.DeviceIdType.MESH
SWEEPS = 3
SLOT = 2
K = 32
ROWS = 3 * K
PLANES = 16
NODES = 256
WIDTH = 128
RIDGE = 0.001

BLOCKS = [(k, b) for k in range(K) for b in range(k // 8, K // 8)]
TRI = 8 * len(BLOCKS)
STARTS = {}
for place, (block_k, block_b) in enumerate(BLOCKS):
    STARTS.setdefault(block_k, 8 * place)
GRAM_ROWS = TRI + 16
CHUNKS = 4
PART = PLANES // CHUNKS


def split3(x):
    hi = x.astype(jnp.bfloat16)
    rest = x - hi.astype(jnp.float32)
    mid = rest.astype(jnp.bfloat16)
    low = (rest - mid.astype(jnp.float32)).astype(jnp.bfloat16)
    return hi, mid, low


def join_rows(rows):
    return jnp.concatenate(rows, axis=1)


def relax_kernel(
    n_wide,
    tests_hbm, bi_ref, fw_ref, mix_ref, tiles_hbm, col_ref, label_ref,
    comb_ref, gram_ref,
    raw, x0, x1, x2, coef, ysend, yrecv, ydup, from_left, planes, from_right, tiles, members, outer, acc, gram_in,
    tests_sems, tiles_sem, xsend_sems, xrecv_sems, ysend_sems, yrecv_sems, psend_sems, precv_sems, gsend_sems,
    grecv_sems,
):
    w = lax.axis_index("wide")
    n = lax.axis_index("narrow")
    right = lax.rem(w + 1, n_wide)
    left = lax.rem(w + n_wide - 1, n_wide)
    other = 1 - n
    fields = [x0, x1, x2]

    def plane_at(i):
        half = i // 2
        return jnp.where(lax.rem(i, 2) == 0, half, PLANES - 1 - half)

    tests_copies = []
    for q in range(CHUNKS):
        for j, start in enumerate((2 * q, PLANES - 2 - 2 * q)):
            span = pl.ds(start, 2)
            copy = pltpu.make_async_copy(tests_hbm.at[span], raw.at[span], tests_sems.at[2 * q + j])
            copy.start()
            tests_copies.append(copy)
    tiles_copy = pltpu.make_async_copy(tiles_hbm, tiles, tiles_sem.at[0])
    tiles_copy.start()

    barrier = pltpu.get_barrier_semaphore()
    for target in ((left, n), (right, n), (w, other)):
        pl.semaphore_signal(barrier, inc=1, device_id=target, device_id_type=MESH)

    lane = lax.broadcasted_iota(jnp.int32, (K + 16, WIDTH), 1)
    low_half = lane < 64
    low8 = low_half[0:8]
    is_low = n == 0

    def pack_row(first, second):
        chosen = jnp.where(is_low, second, first)
        turned = pltpu.roll(chosen, 64, 1)
        a = jnp.where(is_low, turned, chosen)[0:48]
        b = jnp.where(is_low, chosen, turned)[48:96]
        return jnp.where(low_half, a, b).astype(jnp.bfloat16)

    def y_copy(s, q):
        span = pl.ds(q * PART, PART)
        return pltpu.make_async_remote_copy(
            src_ref=ysend.at[s, span], dst_ref=yrecv.at[s, span], send_sem=ysend_sems.at[s * CHUNKS + q],
            recv_sem=yrecv_sems.at[s * CHUNKS + q], device_id=(w, other), device_id_type=MESH,
        )

    def x_copies(s):
        up = pltpu.make_async_remote_copy(
            src_ref=fields[s].at[PLANES], dst_ref=fields[s].at[0], send_sem=xsend_sems.at[2 * s],
            recv_sem=xrecv_sems.at[2 * s], device_id=(right, n), device_id_type=MESH,
        )
        down = pltpu.make_async_remote_copy(
            src_ref=fields[s].at[1], dst_ref=fields[s].at[PLANES + 1], send_sem=xsend_sems.at[2 * s + 1],
            recv_sem=xrecv_sems.at[2 * s + 1], device_id=(left, n), device_id_type=MESH,
        )
        return up, down

    def start_x(s):
        for copy in x_copies(s):
            copy.start()

    def unpack_tests(i, carry):
        p = plane_at(i)
        for c in range(3):
            for kb in range(K // 8):
                pieces = [raw[p, pl.ds(96 * kb + 4 * c + y, 8, stride=12), :] for y in range(4)]
                x0[p + 1, pl.ds(c * K + 8 * kb, 8), :] = join_rows(pieces)
        ysend[0, i] = pack_row(x0[p + 1, :, 0:128], x0[p + 1, :, 128:256])
        return carry

    for q in range(CHUNKS):
        tests_copies[2 * q].wait()
        tests_copies[2 * q + 1].wait()
        lax.fori_loop(q * PART, (q + 1) * PART, unpack_tests, 0)
        if q == 0:
            pl.semaphore_wait(barrier, 3)
            start_x(0)
        y_copy(0, q).start()

    lane_wide = lax.broadcasted_iota(jnp.int32, (8, NODES), 1)
    z_place = lax.rem(lane_wide, 64)

    def make_coef(p, carry):
        def wide_row(ref, first):
            row = join_rows([ref[pl.ds(first + y, 1), :] for y in range(4)])
            return jnp.broadcast_to(row, (8, NODES))

        inv_rows = [wide_row(bi_ref, 36 * p + 4 * i) for i in range(9)]
        edges = [
            jnp.logical_and(p == PLANES - 1, w == n_wide - 1),
            jnp.logical_and(p == 0, w == 0),
            jnp.logical_and(lane_wide >= 192, n == 1),
            jnp.logical_and(lane_wide < 64, n == 0),
            z_place == 63,
            z_place == 0,
        ]
        for d in range(6):
            weight = jnp.where(edges[d], 0.0, 0.5 * wide_row(fw_ref, 24 * p + 4 * d))
            for a in range(3):
                for b in range(3):
                    total = inv_rows[3 * a] * mix_ref[0, b, d]
                    total += inv_rows[3 * a + 1] * mix_ref[1, b, d]
                    total += inv_rows[3 * a + 2] * mix_ref[2, b, d]
                    coef[p, 9 * d + 3 * a + b] = total * weight
        label = join_rows([label_ref[pl.ds(4 * p + y, 1), :] for y in range(4)])
        groups = lax.broadcasted_iota(jnp.int32, (WIDTH, NODES), 0)
        members[p] = jnp.where(groups == label, 1.0, 0.0).astype(jnp.bfloat16)
        return carry

    lax.fori_loop(0, PLANES, make_coef, 0)

    def sweep_plane(s, i):
        p = plane_at(i)
        src = fields[s]
        packed = yrecv[s, i].astype(jnp.float32)
        turned = pltpu.roll(packed, 64, 1)
        ydup[0:48] = jnp.where(low_half, packed, turned)
        ydup[48:96] = jnp.where(low_half, turned, packed)
        for kb in range(K // 8):
            near = []
            own = []
            for c in range(3):
                rows = pl.ds(c * K + kb * 8, 8)
                mid = src[p + 1, rows, :]
                own.append(mid)
                c0, c1 = mid[:, 0:128], mid[:, 128:256]
                r0, r1 = pltpu.roll(c0, 64, 1), pltpu.roll(c1, 64, 1)
                dup = ydup[rows]
                between = jnp.where(low8, r0, r1)
                y_up = jnp.concatenate([between, jnp.where(low8, r1, dup)], axis=1)
                y_down = jnp.concatenate([jnp.where(low8, dup, r0), between], axis=1)
                z_up = jnp.concatenate([pltpu.roll(c0, 127, 1), pltpu.roll(c1, 127, 1)], axis=1)
                z_down = jnp.concatenate([pltpu.roll(c0, 1, 1), pltpu.roll(c1, 1, 1)], axis=1)
                near.append([src[p + 2, rows, :], src[p, rows, :], y_up, y_down, z_up, z_down])
            for a in range(3):
                total = 0.5 * own[a]
                for d in range(6):
                    for b in range(3):
                        total += coef[p, 9 * d + 3 * a + b] * near[b][d]
                rows = pl.ds(a * K + kb * 8, 8)
                if s + 1 < SWEEPS:
                    fields[s + 1][p + 1, rows, :] = total
                else:
                    comb_ref[p, rows, :] = total
        if s + 1 < SWEEPS:
            ysend[s + 1, i] = pack_row(fields[s + 1][p + 1, :, 0:128], fields[s + 1][p + 1, :, 128:256])
        else:
            planes[p] = comb_ref[p].astype(jnp.bfloat16)

    def plane_copies(q):
        copies = []
        for j, start in enumerate((2 * q, PLANES - 2 - 2 * q)):
            span = pl.ds(start, 2)
            for side, (target, landing) in enumerate(((right, from_left), (left, from_right))):
                at = 4 * q + 2 * j + side
                copies.append(
                    pltpu.make_async_remote_copy(
                        src_ref=planes.at[span], dst_ref=landing.at[span], send_sem=psend_sems.at[at],
                        recv_sem=precv_sems.at[at], device_id=(target, n), device_id_type=MESH,
                    )
                )
        return copies

    for s in range(SWEEPS):
        for copy in x_copies(s):
            copy.wait()

        def one_chunk(q, carry, s=s):
            y_copy(s, q).wait()

            def one_plane(j, inner):
                sweep_plane(s, q * PART + j)
                if s + 1 < SWEEPS:
                    pl.when(jnp.logical_and(q == 0, j == 1))(lambda: start_x(s + 1))
                return inner

            lax.fori_loop(0, PART, one_plane, 0)
            if s + 1 < SWEEPS:
                y_copy(s + 1, q).start()
            else:
                for copy in plane_copies(q):
                    copy.start()
            return carry

        lax.fori_loop(0, CHUNKS, one_chunk, 0)

    tiles_copy.wait()
    sources = [from_left, planes, from_right]

    def far_product(r, slot):
        return jnp.dot(
            sources[slot][col_ref[slot, 0, r]], tiles[r, slot], preferred_element_type=jnp.float32
        )

    def near_far(r, carry):
        comb_ref[r] = comb_ref[r] + far_product(r, 1)
        return carry

    lax.fori_loop(0, PLANES, near_far, 0)

    acc[...] = jnp.zeros_like(acc)
    for q in range(CHUNKS):
        for copy in plane_copies(q):
            copy.wait()

    def side_far(r, carry):
        comb_ref[r] = comb_ref[r] + (far_product(r, 0) + far_product(r, 2))
        return carry

    lax.fori_loop(0, PLANES, side_far, 0)

    pairs = len(BLOCKS) // 2 // CHUNKS
    rows_part = 16 * pairs

    def gram_copy(t):
        height = rows_part if t + 1 < CHUNKS else GRAM_ROWS - rows_part * t
        span = pl.ds(rows_part * t, height)
        return pltpu.make_async_remote_copy(
            src_ref=acc.at[span], dst_ref=gram_in.at[span], send_sem=gsend_sems.at[t], recv_sem=grecv_sems.at[t],
            device_id=(w, other), device_id_type=MESH,
        )

    def contract(values, member):
        return lax.dot_general(values, member, (((1,), (1,)), ((), ())), preferred_element_type=jnp.float32)

    for t in range(CHUNKS):

        def gram_planes(h, carry, t=t):
            for side in range(2):
                r = 2 * h + side
                lanes = pl.ds(side * NODES, NODES)
                for pair in range(pairs):
                    parts = []
                    for k, b in BLOCKS[2 * (pairs * t + pair) : 2 * (pairs * t + pair) + 2]:
                        value = None
                        for c in range(3):
                            term = comb_ref[r, c * K + k : c * K + k + 1, :] * comb_ref[r, pl.ds(c * K + 8 * b, 8), :]
                            value = term if value is None else value + term
                        parts.append(value)
                    for piece, values in enumerate(split3(jnp.concatenate(parts, axis=0))):
                        outer[piece, pl.ds(16 * pair, 16), lanes] = values
            total = None
            for side in range(2):
                member = members[2 * h + side]
                lanes = pl.ds(side * NODES, NODES)
                for piece in range(3):
                    term = contract(outer[piece, :, lanes], member)
                    total = term if total is None else total + term
            acc[pl.ds(rows_part * t, rows_part), :] += total
            if t + 1 == CHUNKS:
                ones = jnp.ones((16, NODES), jnp.bfloat16)
                acc[TRI:GRAM_ROWS] += contract(ones, members[2 * h]) + contract(ones, members[2 * h + 1])
            return carry

        lax.fori_loop(0, PLANES // 2, gram_planes, 0)
        gram_copy(t).start()

    for t in range(CHUNKS):
        gram_copy(t).wait()
    gram_ref[...] = acc[...] + gram_in[...]


def slot_table(owner_ref, slots_total):
    count = owner_ref.shape[1]
    owners = owner_ref[...].astype(jnp.float32)
    across = jnp.broadcast_to(owners, (count, count))
    row = lax.broadcasted_iota(jnp.int32, (count, count), 0)
    column = lax.broadcasted_iota(jnp.int32, (count, count), 1)
    down = jnp.sum(jnp.where(row == column, across, 0.0), axis=1, keepdims=True)
    earlier = jnp.where(jnp.logical_and(down == across, row < column), 1.0, 0.0)
    target = owners * SLOT + jnp.sum(earlier, axis=0, keepdims=True)
    none = jnp.full_like(target, -1.0)
    is_low = lax.axis_index("narrow") == 0
    lanes = join_rows([jnp.where(is_low, target, none), jnp.where(is_low, none, target)])
    slots = lax.broadcasted_iota(jnp.int32, (slots_total, WIDTH), 0).astype(jnp.float32)
    return jnp.where(slots == lanes, 1.0, 0.0).astype(jnp.bfloat16)


def factor_kernel(gram_ref, owner_ref, packed_ref, inverse_ref, lower, inv):
    scale = 1.0 / (3.0 * gram_ref[TRI : TRI + 1, :])
    row = lax.broadcasted_iota(jnp.int32, (K, WIDTH), 0)
    columns = []
    for k in range(K):
        first = 8 * (k // 8)
        height = K - first
        column = gram_ref[pl.ds(STARTS[k], height), :] * scale
        columns.append(column + jnp.where(row[first:] == k, RIDGE, 0.0))
    reciprocals = []
    for k in range(K):
        first = 8 * (k // 8)
        at = k - first
        pivot = jnp.sqrt(columns[k][at : at + 1])
        reciprocal = 1.0 / pivot
        reciprocals.append(reciprocal)
        column = jnp.where(row[first:] >= k, columns[k] * reciprocal, 0.0)
        columns[k] = column
        for m in range(k + 1, K):
            begin = 8 * (m // 8)
            columns[m] = columns[m] - column[m - first : m - first + 1] * column[begin - first :]
        lower[pl.ds(STARTS[k], K - first), :] = column
    for l in range(K):
        first = 8 * (l // 8)
        solved = jnp.where(row[first:] == l, 1.0, 0.0)
        for m in range(l, K):
            base = 8 * (m // 8)
            value = solved[m - first : m - first + 1] * reciprocals[m]
            here = solved[base - first :]
            here = jnp.where(row[base:] == m, value, jnp.where(row[base:] > m, here - columns[m] * value, here))
            solved = here if base == first else jnp.concatenate([solved[: base - first], here], axis=0)
        inv[pl.ds(STARTS[l], K - first), :] = solved
    for i, piece in enumerate(split3(inv[...])):
        inverse_ref[:, i * WIDTH : (i + 1) * WIDTH] = piece
    table = slot_table(owner_ref, packed_ref.shape[0])
    total = None
    for piece in split3(lower[...]):
        term = lax.dot_general(table, piece, (((1,), (1,)), ((), ())), preferred_element_type=jnp.float32)
        total = term if total is None else total + term
    packed_ref[...] = total


def project_kernel(
    n_wide, n_narrow, packed_ref, comb_ref, label_ref, inverse_ref, out_ref, received_ref, landing, look, spare,
    send_sem, recv_sem,
):
    count = n_wide * n_narrow
    w = lax.axis_index("wide")
    n = lax.axis_index("narrow")
    me = w * n_narrow + n
    barrier = pltpu.get_barrier_semaphore()

    def peer(i):
        index = lax.rem(me + i, count)
        return index, (index // n_narrow, lax.rem(index, n_narrow))

    def greet(i, carry):
        pl.semaphore_signal(barrier, inc=1, device_id=peer(i)[1], device_id_type=MESH)
        return carry

    lax.fori_loop(1, count, greet, 0)
    own_span = pl.ds(SLOT * me, SLOT)
    pltpu.make_async_copy(packed_ref.at[own_span], landing.at[own_span], recv_sem).start()
    pltpu.make_async_copy(packed_ref.at[own_span], spare, send_sem).start()

    groups = lax.broadcasted_iota(jnp.int32, (WIDTH, NODES), 0)

    def project_plane(r, carry):
        label = join_rows([label_ref[pl.ds(4 * r + y, 1), :] for y in range(4)])
        member = jnp.where(groups == label, 1.0, 0.0).astype(jnp.bfloat16)
        look[...] = jnp.dot(
            inverse_ref[...], jnp.concatenate([member, member, member], axis=0), preferred_element_type=jnp.float32
        )
        for b in range(K // 8):
            totals = [None] * 3
            for l in range(8 * (b + 1)):
                weight = look[pl.ds(STARTS[l] + 8 * (b - l // 8), 8), :]
                for c in range(3):
                    term = weight * comb_ref[r, c * K + l : c * K + l + 1, :]
                    totals[c] = term if totals[c] is None else totals[c] + term
            for c in range(3):
                for y in range(4):
                    out_ref[r, pl.ds(96 * b + 4 * c + y, 8, stride=12), :] = totals[c][:, 64 * y : 64 * (y + 1)]
        return carry

    lax.fori_loop(0, PART, project_plane, 0)
    pl.semaphore_wait(barrier, count - 1)

    def send(i, carry):
        index, device = peer(i)
        pltpu.make_async_remote_copy(
            src_ref=packed_ref.at[pl.ds(SLOT * index, SLOT)], dst_ref=landing.at[own_span], send_sem=send_sem,
            recv_sem=recv_sem, device_id=device, device_id_type=MESH,
        ).start()
        return carry

    lax.fori_loop(1, count, send, 0)
    lax.fori_loop(PART, PLANES, project_plane, 0)
    everything = pltpu.make_async_remote_copy(
        src_ref=packed_ref, dst_ref=landing, send_sem=send_sem, recv_sem=recv_sem, device_id=peer(1)[1],
        device_id_type=MESH,
    )
    everything.wait_send()
    everything.wait_recv()
    received_ref[...] = landing[...]


def widen_kernel(received_ref, prolong_in, basis_ref, prolong_out, sem):
    copy = pltpu.make_async_copy(prolong_in, prolong_out, sem)
    copy.start()
    pieces = split3(received_ref[...])
    for m in range(K * K // WIDTH):
        group = m // 2
        width = K - 8 * group
        start = STARTS[8 * group]
        first = STARTS[4 * m] // WIDTH * WIDTH
        last = -(-(STARTS[4 * m] + 4 * width) // WIDTH) * WIDTH
        if group == 0:
            basis_ref[0, :, WIDTH * m : WIDTH * (m + 1)] = received_ref[:, first:last]
            continue
        source = lax.broadcasted_iota(jnp.int32, (last - first, WIDTH), 0) + first
        column = lax.broadcasted_iota(jnp.int32, (last - first, WIDTH), 1) + WIDTH * m
        k, l = column // K, lax.rem(column, K)
        wanted = start + (k - 8 * group) * width + l - 8 * group
        place = jnp.where(jnp.logical_and(source == wanted, l >= 8 * group), 1.0, 0.0).astype(jnp.bfloat16)
        total = None
        for piece in pieces:
            term = jnp.dot(piece[:, first:last], place, preferred_element_type=jnp.float32)
            total = term if total is None else total + term
        basis_ref[0, :, WIDTH * m : WIDTH * (m + 1)] = total
    copy.wait()


def vmem(shape, dtype=jnp.float32):
    return pltpu.VMEM(shape, dtype)


def shards(n_wide, n_narrow, tests, block_inverse, face_weight, mixing, far_tiles, far_column, aggregate, owner_map):
    bf16 = jnp.bfloat16
    whole = pl.BlockSpec(memory_space=pltpu.VMEM)
    any_spec = pl.BlockSpec(memory_space=pl.ANY)
    smem = pl.BlockSpec(memory_space=pltpu.SMEM)
    labels = aggregate.reshape(PLANES * 4, 64)

    slots_total = n_wide * n_narrow * SLOT
    combined, gram = pl.pallas_call(
        functools.partial(relax_kernel, n_wide),
        out_shape=(
            jax.ShapeDtypeStruct((PLANES, ROWS, NODES), jnp.float32),
            jax.ShapeDtypeStruct((GRAM_ROWS, WIDTH), jnp.float32),
        ),
        in_specs=[any_spec, whole, whole, smem, any_spec, smem, whole],
        out_specs=(whole, whole),
        scratch_shapes=[
            vmem((PLANES, 4 * ROWS, 64)),
            vmem((PLANES + 2, ROWS, NODES)),
            vmem((PLANES + 2, ROWS, NODES)),
            vmem((PLANES + 2, ROWS, NODES)),
            vmem((PLANES, 54, 8, NODES)),
            vmem((SWEEPS, PLANES, 48, WIDTH), bf16),
            vmem((SWEEPS, PLANES, 48, WIDTH), bf16),
            vmem((ROWS, WIDTH)),
            vmem((PLANES, ROWS, NODES), bf16),
            vmem((PLANES, ROWS, NODES), bf16),
            vmem((PLANES, ROWS, NODES), bf16),
            vmem((PLANES, 3, NODES, NODES), bf16),
            vmem((PLANES, WIDTH, NODES), bf16),
            vmem((3, TRI // CHUNKS, 2 * NODES), bf16),
            vmem((GRAM_ROWS, WIDTH)),
            vmem((GRAM_ROWS, WIDTH)),
            pltpu.SemaphoreType.DMA((2 * CHUNKS,)),
            pltpu.SemaphoreType.DMA((1,)),
            pltpu.SemaphoreType.DMA((2 * SWEEPS,)),
            pltpu.SemaphoreType.DMA((2 * SWEEPS,)),
            pltpu.SemaphoreType.DMA((SWEEPS * CHUNKS,)),
            pltpu.SemaphoreType.DMA((SWEEPS * CHUNKS,)),
            pltpu.SemaphoreType.DMA((4 * CHUNKS,)),
            pltpu.SemaphoreType.DMA((4 * CHUNKS,)),
            pltpu.SemaphoreType.DMA((CHUNKS,)),
            pltpu.SemaphoreType.DMA((CHUNKS,)),
        ],
        compiler_params=pltpu.CompilerParams(
            collective_id=0, has_side_effects=True, vmem_limit_bytes=56 * 1024 * 1024
        ),
        name="relax_far_gram",
    )(
        tests.reshape(PLANES, 4 * ROWS, 64),
        block_inverse.reshape(PLANES * 36, 64),
        face_weight.reshape(PLANES * 24, 64),
        mixing.transpose(1, 2, 0),
        far_tiles.reshape(PLANES, 3, NODES, NODES),
        far_column.transpose(2, 1, 0),
        labels,
    )

    packed, inverse = pl.pallas_call(
        factor_kernel,
        out_shape=(
            jax.ShapeDtypeStruct((slots_total, TRI), jnp.float32),
            jax.ShapeDtypeStruct((TRI, 3 * WIDTH), bf16),
        ),
        in_specs=[whole, whole],
        out_specs=(whole, whole),
        scratch_shapes=[vmem((TRI, WIDTH)), vmem((TRI, WIDTH))],
        compiler_params=pltpu.CompilerParams(vmem_limit_bytes=32 * 1024 * 1024),
        name="factor",
    )(gram, owner_map.reshape(1, owner_map.shape[0]))

    projected, received = pl.pallas_call(
        functools.partial(project_kernel, n_wide, n_narrow),
        out_shape=(
            jax.ShapeDtypeStruct((PLANES, 4 * ROWS, 64), jnp.float32),
            jax.ShapeDtypeStruct((slots_total, TRI), jnp.float32),
        ),
        in_specs=[whole, whole, whole, whole],
        out_specs=(whole, whole),
        scratch_shapes=[
            vmem((slots_total, TRI)),
            vmem((TRI, NODES)),
            vmem((SLOT, TRI)),
            pltpu.SemaphoreType.DMA,
            pltpu.SemaphoreType.DMA,
        ],
        compiler_params=pltpu.CompilerParams(
            collective_id=1, has_side_effects=True, vmem_limit_bytes=40 * 1024 * 1024
        ),
        name="project",
    )(packed, combined, labels, inverse)

    basis, prolong = pl.pallas_call(
        widen_kernel,
        out_shape=(
            jax.ShapeDtypeStruct((1, slots_total, K * K), jnp.float32),
            jax.ShapeDtypeStruct((PLANES, 4 * ROWS, 64), jnp.float32),
        ),
        in_specs=[whole, any_spec],
        out_specs=(whole, any_spec),
        scratch_shapes=[pltpu.SemaphoreType.DMA],
        compiler_params=pltpu.CompilerParams(vmem_limit_bytes=32 * 1024 * 1024),
        name="widen",
    )(received, projected)
    return prolong.reshape(tests.shape), basis


def solution(mesh):
    in_specs = (
        P("wide", None, None, "narrow", None),
        P("wide", None, None, "narrow", None),
        P("wide", None, "narrow", None),
        P(),
        P("wide", "narrow", None, None, None),
        P("wide", "narrow", None),
        P("wide", "narrow", None),
        P(("wide", "narrow")),
    )
    out_specs = (P("wide", None, None, "narrow", None), P(("wide", "narrow"), None, None))
    body = functools.partial(shards, mesh.shape["wide"], mesh.shape["narrow"])
    return jax.shard_map(body, mesh=mesh, in_specs=in_specs, out_specs=out_specs, check_vma=False)
```

```python
import functools

import jax
import jax.numpy as jnp
from jax import lax
from jax.experimental import pallas as pl
from jax.experimental.pallas import tpu as pltpu
from jax.sharding import PartitionSpec as P

MESH = pl.DeviceIdType.MESH
SWEEPS = 3
SLOT = 2
K = 32
ROWS = 3 * K
PLANES = 16
NODES = 256
WIDTH = 128
RIDGE = 0.001

BLOCKS = [(k, b) for k in range(K) for b in range(k // 8, K // 8)]
TRI = 8 * len(BLOCKS)
STARTS = {}
for place, (block_k, block_b) in enumerate(BLOCKS):
    STARTS.setdefault(block_k, 8 * place)
GRAM_ROWS = TRI + 16
CHUNKS = 8
PART = PLANES // CHUNKS
GRAM_PARTS = 4
EARLY = 4


def split3(x):
    hi = x.astype(jnp.bfloat16)
    rest = x - hi.astype(jnp.float32)
    mid = rest.astype(jnp.bfloat16)
    low = (rest - mid.astype(jnp.float32)).astype(jnp.bfloat16)
    return hi, mid, low


def join_rows(rows):
    return jnp.concatenate(rows, axis=1)


def relax_kernel(
    n_wide,
    tests_hbm, bi_ref, fw_ref, mix_ref, tiles_hbm, col_ref, label_ref,
    comb_ref, gram_ref,
    raw, x0, x1, x2, coef, ysend, yrecv, ydup, from_left, planes, from_right, tiles, members, outer, acc, gram_in,
    tests_sems, tiles_sem, xsend_sems, xrecv_sems, ysend_sems, yrecv_sems, psend_sems, precv_sems, gsend_sems,
    grecv_sems,
):
    w = lax.axis_index("wide")
    n = lax.axis_index("narrow")
    right = lax.rem(w + 1, n_wide)
    left = lax.rem(w + n_wide - 1, n_wide)
    other = 1 - n
    fields = [x0, x1, x2]

    def plane_at(i):
        half = i // 2
        return jnp.where(lax.rem(i, 2) == 0, PLANES // 2 - 1 - half, PLANES // 2 + half)

    tests_copies = []
    for q in range(CHUNKS):
        for j, start in enumerate((PLANES // 2 - 1 - q, PLANES // 2 + q)):
            span = pl.ds(start, 1)
            copy = pltpu.make_async_copy(tests_hbm.at[span], raw.at[span], tests_sems.at[2 * q + j])
            copy.start()
            tests_copies.append(copy)
    tiles_copy = pltpu.make_async_copy(tiles_hbm, tiles, tiles_sem.at[0])
    tiles_copy.start()

    barrier = pltpu.get_barrier_semaphore()
    for target in ((left, n), (right, n), (w, other)):
        pl.semaphore_signal(barrier, inc=1, device_id=target, device_id_type=MESH)

    lane = lax.broadcasted_iota(jnp.int32, (K + 16, WIDTH), 1)
    low_half = lane < 64
    low8 = low_half[0:8]
    is_low = n == 0

    def pack_row(first, second):
        chosen = jnp.where(is_low, second, first)
        turned = pltpu.roll(chosen, 64, 1)
        a = jnp.where(is_low, turned, chosen)[0:48]
        b = jnp.where(is_low, chosen, turned)[48:96]
        return jnp.where(low_half, a, b).astype(jnp.bfloat16)

    def y_copy(s, q):
        span = pl.ds(q * PART, PART)
        return pltpu.make_async_remote_copy(
            src_ref=ysend.at[s, span], dst_ref=yrecv.at[s, span], send_sem=ysend_sems.at[s * CHUNKS + q],
            recv_sem=yrecv_sems.at[s * CHUNKS + q], device_id=(w, other), device_id_type=MESH,
        )

    def x_copies(s):
        up = pltpu.make_async_remote_copy(
            src_ref=fields[s].at[PLANES], dst_ref=fields[s].at[0], send_sem=xsend_sems.at[2 * s],
            recv_sem=xrecv_sems.at[2 * s], device_id=(right, n), device_id_type=MESH,
        )
        down = pltpu.make_async_remote_copy(
            src_ref=fields[s].at[1], dst_ref=fields[s].at[PLANES + 1], send_sem=xsend_sems.at[2 * s + 1],
            recv_sem=xrecv_sems.at[2 * s + 1], device_id=(left, n), device_id_type=MESH,
        )
        return up, down

    has_right = w < n_wide - 1
    has_left = w > 0

    def start_x(s):
        up, down = x_copies(s)
        pl.when(has_right)(up.start)
        pl.when(has_left)(down.start)

    def wait_x(s):
        up, down = x_copies(s)
        pl.when(has_right)(up.wait_send)
        pl.when(has_left)(up.wait_recv)
        pl.when(has_left)(down.wait_send)
        pl.when(has_right)(down.wait_recv)

    @pl.when(jnp.logical_not(has_left))
    def clear_left():
        for field in fields:
            field[0] = jnp.zeros((ROWS, NODES), jnp.float32)

    @pl.when(jnp.logical_not(has_right))
    def clear_right():
        for field in fields:
            field[PLANES + 1] = jnp.zeros((ROWS, NODES), jnp.float32)

    def unpack_tests(i, carry):
        p = plane_at(i)
        for c in range(3):
            for kb in range(K // 8):
                pieces = [raw[p, pl.ds(96 * kb + 4 * c + y, 8, stride=12), :] for y in range(4)]
                x0[p + 1, pl.ds(c * K + 8 * kb, 8), :] = join_rows(pieces)
        ysend[0, i] = pack_row(x0[p + 1, :, 0:128], x0[p + 1, :, 128:256])
        return carry

    for q in range(CHUNKS):
        tests_copies[2 * q].wait()
        tests_copies[2 * q + 1].wait()
        lax.fori_loop(q * PART, (q + 1) * PART, unpack_tests, 0)
        if q == 0:
            pl.semaphore_wait(barrier, 3)
        y_copy(0, q).start()
    start_x(0)

    lane_wide = lax.broadcasted_iota(jnp.int32, (8, NODES), 1)
    z_place = lax.rem(lane_wide, 64)

    def make_coef(p, carry):
        def wide_row(ref, first):
            row = join_rows([ref[pl.ds(first + y, 1), :] for y in range(4)])
            return jnp.broadcast_to(row, (8, NODES))

        inv_rows = [wide_row(bi_ref, 36 * p + 4 * i) for i in range(9)]
        edges = [
            jnp.logical_and(p == PLANES - 1, w == n_wide - 1),
            jnp.logical_and(p == 0, w == 0),
            jnp.logical_and(lane_wide >= 192, n == 1),
            jnp.logical_and(lane_wide < 64, n == 0),
            z_place == 63,
            z_place == 0,
        ]
        for d in range(6):
            weight = jnp.where(edges[d], 0.0, 0.5 * wide_row(fw_ref, 24 * p + 4 * d))
            for a in range(3):
                for b in range(3):
                    total = inv_rows[3 * a] * mix_ref[0, b, d]
                    total += inv_rows[3 * a + 1] * mix_ref[1, b, d]
                    total += inv_rows[3 * a + 2] * mix_ref[2, b, d]
                    coef[p, 9 * d + 3 * a + b] = total * weight
        label = join_rows([label_ref[pl.ds(4 * p + y, 1), :] for y in range(4)])
        groups = lax.broadcasted_iota(jnp.int32, (WIDTH, NODES), 0)
        members[p] = jnp.where(groups == label, 1.0, 0.0).astype(jnp.bfloat16)
        return carry

    lax.fori_loop(0, PLANES, make_coef, 0)

    def sweep_plane(s, i):
        p = plane_at(i)
        src = fields[s]
        packed = yrecv[s, i].astype(jnp.float32)
        turned = pltpu.roll(packed, 64, 1)
        ydup[0:48] = jnp.where(low_half, packed, turned)
        ydup[48:96] = jnp.where(low_half, turned, packed)
        for kb in range(K // 8):
            near = []
            own = []
            for c in range(3):
                rows = pl.ds(c * K + kb * 8, 8)
                mid = src[p + 1, rows, :]
                own.append(mid)
                c0, c1 = mid[:, 0:128], mid[:, 128:256]
                r0, r1 = pltpu.roll(c0, 64, 1), pltpu.roll(c1, 64, 1)
                dup = ydup[rows]
                between = jnp.where(low8, r0, r1)
                y_up = jnp.concatenate([between, jnp.where(low8, r1, dup)], axis=1)
                y_down = jnp.concatenate([jnp.where(low8, dup, r0), between], axis=1)
                z_up = jnp.concatenate([pltpu.roll(c0, 127, 1), pltpu.roll(c1, 127, 1)], axis=1)
                z_down = jnp.concatenate([pltpu.roll(c0, 1, 1), pltpu.roll(c1, 1, 1)], axis=1)
                near.append([src[p + 2, rows, :], src[p, rows, :], y_up, y_down, z_up, z_down])
            for a in range(3):
                total = 0.5 * own[a]
                for d in range(6):
                    for b in range(3):
                        total += coef[p, 9 * d + 3 * a + b] * near[b][d]
                rows = pl.ds(a * K + kb * 8, 8)
                if s + 1 < SWEEPS:
                    fields[s + 1][p + 1, rows, :] = total
                else:
                    comb_ref[p, rows, :] = total
        if s + 1 < SWEEPS:
            ysend[s + 1, i] = pack_row(fields[s + 1][p + 1, :, 0:128], fields[s + 1][p + 1, :, 128:256])
        else:
            planes[p] = comb_ref[p].astype(jnp.bfloat16)

    def plane_copies(q):
        copies = []
        for j, start in enumerate((PLANES // 2 - 1 - q, PLANES // 2 + q)):
            span = pl.ds(start, 1)
            for side, (target, landing) in enumerate(((right, from_left), (left, from_right))):
                at = 4 * q + 2 * j + side
                copies.append(
                    pltpu.make_async_remote_copy(
                        src_ref=planes.at[span], dst_ref=landing.at[span], send_sem=psend_sems.at[at],
                        recv_sem=precv_sems.at[at], device_id=(target, n), device_id_type=MESH,
                    )
                )
        return copies

    for s in range(SWEEPS):

        def one_chunk(q, carry, s=s):
            y_copy(s, q).wait()
            pl.when(q == CHUNKS - 1)(lambda: wait_x(s))

            def one_plane(j, inner):
                sweep_plane(s, q * PART + j)
                return inner

            lax.fori_loop(0, PART, one_plane, 0)
            if s + 1 < SWEEPS:
                y_copy(s + 1, q).start()
            else:
                for copy in plane_copies(q):
                    copy.start()
            return carry

        lax.fori_loop(0, CHUNKS, one_chunk, 0)
        if s + 1 < SWEEPS:
            start_x(s + 1)

    tiles_copy.wait()
    sources = [from_left, planes, from_right]

    def far_product(r, slot):
        return jnp.dot(
            sources[slot][col_ref[slot, 0, r]], tiles[r, slot], preferred_element_type=jnp.float32
        )

    def near_far(r, carry):
        comb_ref[r] = comb_ref[r] + far_product(r, 1)
        return carry

    lax.fori_loop(0, PLANES, near_far, 0)

    acc[...] = jnp.zeros_like(acc)
    for q in range(CHUNKS):
        for copy in plane_copies(q):
            copy.wait()

    def side_far(r, carry):
        comb_ref[r] = comb_ref[r] + (far_product(r, 0) + far_product(r, 2))
        return carry

    lax.fori_loop(0, PLANES, side_far, 0)

    pairs = len(BLOCKS) // 2 // GRAM_PARTS
    rows_part = 16 * pairs

    def gram_copy(t):
        height = rows_part if t + 1 < GRAM_PARTS else GRAM_ROWS - rows_part * t
        span = pl.ds(rows_part * t, height)
        return pltpu.make_async_remote_copy(
            src_ref=acc.at[span], dst_ref=gram_in.at[span], send_sem=gsend_sems.at[t], recv_sem=grecv_sems.at[t],
            device_id=(w, other), device_id_type=MESH,
        )

    def contract(values, member):
        return lax.dot_general(values, member, (((1,), (1,)), ((), ())), preferred_element_type=jnp.float32)

    for t in range(GRAM_PARTS):

        def gram_planes(h, carry, t=t):
            for side in range(2):
                r = 2 * h + side
                lanes = pl.ds(side * NODES, NODES)
                for pair in range(pairs):
                    parts = []
                    for k, b in BLOCKS[2 * (pairs * t + pair) : 2 * (pairs * t + pair) + 2]:
                        value = None
                        for c in range(3):
                            term = comb_ref[r, c * K + k : c * K + k + 1, :] * comb_ref[r, pl.ds(c * K + 8 * b, 8), :]
                            value = term if value is None else value + term
                        parts.append(value)
                    for piece, values in enumerate(split3(jnp.concatenate(parts, axis=0))):
                        outer[piece, pl.ds(16 * pair, 16), lanes] = values
            total = None
            for side in range(2):
                member = members[2 * h + side]
                lanes = pl.ds(side * NODES, NODES)
                for piece in range(3):
                    term = contract(outer[piece, :, lanes], member)
                    total = term if total is None else total + term
            acc[pl.ds(rows_part * t, rows_part), :] += total
            if t + 1 == GRAM_PARTS:
                ones = jnp.ones((16, NODES), jnp.bfloat16)
                acc[TRI:GRAM_ROWS] += contract(ones, members[2 * h]) + contract(ones, members[2 * h + 1])
            return carry

        lax.fori_loop(0, PLANES // 2, gram_planes, 0)
        gram_copy(t).start()

    for t in range(GRAM_PARTS):
        gram_copy(t).wait()
    gram_ref[...] = acc[...] + gram_in[...]


def slot_table(owner_ref, slots_total):
    count = owner_ref.shape[1]
    owners = owner_ref[...].astype(jnp.float32)
    across = jnp.broadcast_to(owners, (count, count))
    row = lax.broadcasted_iota(jnp.int32, (count, count), 0)
    column = lax.broadcasted_iota(jnp.int32, (count, count), 1)
    down = jnp.sum(jnp.where(row == column, across, 0.0), axis=1, keepdims=True)
    earlier = jnp.where(jnp.logical_and(down == across, row < column), 1.0, 0.0)
    target = owners * SLOT + jnp.sum(earlier, axis=0, keepdims=True)
    none = jnp.full_like(target, -1.0)
    is_low = lax.axis_index("narrow") == 0
    lanes = join_rows([jnp.where(is_low, target, none), jnp.where(is_low, none, target)])
    slots = lax.broadcasted_iota(jnp.int32, (slots_total, WIDTH), 0).astype(jnp.float32)
    return jnp.where(slots == lanes, 1.0, 0.0).astype(jnp.bfloat16)


def factor_kernel(gram_ref, owner_ref, packed_ref, inverse_ref, lower, inv):
    scale = 1.0 / (3.0 * gram_ref[TRI : TRI + 1, :])
    row = lax.broadcasted_iota(jnp.int32, (K, WIDTH), 0)
    columns = []
    for k in range(K):
        first = 8 * (k // 8)
        height = K - first
        column = gram_ref[pl.ds(STARTS[k], height), :] * scale
        columns.append(column + jnp.where(row[first:] == k, RIDGE, 0.0))
    reciprocals = []
    for k in range(K):
        first = 8 * (k // 8)
        at = k - first
        pivot = jnp.sqrt(columns[k][at : at + 1])
        reciprocal = 1.0 / pivot
        reciprocals.append(reciprocal)
        column = jnp.where(row[first:] >= k, columns[k] * reciprocal, 0.0)
        columns[k] = column
        for m in range(k + 1, K):
            begin = 8 * (m // 8)
            columns[m] = columns[m] - column[m - first : m - first + 1] * column[begin - first :]
        lower[pl.ds(STARTS[k], K - first), :] = column
    for l in range(K):
        first = 8 * (l // 8)
        solved = jnp.where(row[first:] == l, 1.0, 0.0)
        for m in range(l, K):
            base = 8 * (m // 8)
            value = solved[m - first : m - first + 1] * reciprocals[m]
            here = solved[base - first :]
            here = jnp.where(row[base:] == m, value, jnp.where(row[base:] > m, here - columns[m] * value, here))
            solved = here if base == first else jnp.concatenate([solved[: base - first], here], axis=0)
        inv[pl.ds(STARTS[l], K - first), :] = solved
    for i, piece in enumerate(split3(inv[...])):
        inverse_ref[:, i * WIDTH : (i + 1) * WIDTH] = piece
    table = slot_table(owner_ref, packed_ref.shape[0])
    total = None
    for piece in split3(lower[...]):
        term = lax.dot_general(table, piece, (((1,), (1,)), ((), ())), preferred_element_type=jnp.float32)
        total = term if total is None else total + term
    packed_ref[...] = total


def project_kernel(
    n_wide, n_narrow, packed_ref, comb_ref, label_ref, inverse_ref, out_ref, received_ref, landing, look, spare,
    send_sem, recv_sem,
):
    count = n_wide * n_narrow
    w = lax.axis_index("wide")
    n = lax.axis_index("narrow")
    me = w * n_narrow + n
    barrier = pltpu.get_barrier_semaphore()

    def peer(i):
        index = lax.rem(me + i, count)
        return index, (index // n_narrow, lax.rem(index, n_narrow))

    def greet(i, carry):
        pl.semaphore_signal(barrier, inc=1, device_id=peer(i)[1], device_id_type=MESH)
        return carry

    lax.fori_loop(1, count, greet, 0)
    own_span = pl.ds(SLOT * me, SLOT)
    pltpu.make_async_copy(packed_ref.at[own_span], landing.at[own_span], recv_sem).start()
    pltpu.make_async_copy(packed_ref.at[own_span], spare, send_sem).start()

    groups = lax.broadcasted_iota(jnp.int32, (WIDTH, NODES), 0)

    def project_plane(r, carry):
        label = join_rows([label_ref[pl.ds(4 * r + y, 1), :] for y in range(4)])
        member = jnp.where(groups == label, 1.0, 0.0).astype(jnp.bfloat16)
        look[...] = jnp.dot(
            inverse_ref[...], jnp.concatenate([member, member, member], axis=0), preferred_element_type=jnp.float32
        )
        for b in range(K // 8):
            totals = [None] * 3
            for l in range(8 * (b + 1)):
                weight = look[pl.ds(STARTS[l] + 8 * (b - l // 8), 8), :]
                for c in range(3):
                    term = weight * comb_ref[r, c * K + l : c * K + l + 1, :]
                    totals[c] = term if totals[c] is None else totals[c] + term
            for c in range(3):
                for y in range(4):
                    out_ref[r, pl.ds(96 * b + 4 * c + y, 8, stride=12), :] = totals[c][:, 64 * y : 64 * (y + 1)]
        return carry

    lax.fori_loop(0, EARLY, project_plane, 0)
    pl.semaphore_wait(barrier, count - 1)

    def send(i, carry):
        index, device = peer(i)
        pltpu.make_async_remote_copy(
            src_ref=packed_ref.at[pl.ds(SLOT * index, SLOT)], dst_ref=landing.at[own_span], send_sem=send_sem,
            recv_sem=recv_sem, device_id=device, device_id_type=MESH,
        ).start()
        return carry

    lax.fori_loop(1, count, send, 0)
    lax.fori_loop(EARLY, PLANES, project_plane, 0)
    everything = pltpu.make_async_remote_copy(
        src_ref=packed_ref, dst_ref=landing, send_sem=send_sem, recv_sem=recv_sem, device_id=peer(1)[1],
        device_id_type=MESH,
    )
    everything.wait_send()
    everything.wait_recv()
    received_ref[...] = landing[...]


def widen_kernel(received_ref, prolong_in, basis_ref, prolong_out, sem):
    copy = pltpu.make_async_copy(prolong_in, prolong_out, sem)
    copy.start()
    pieces = split3(received_ref[...])
    for m in range(K * K // WIDTH):
        group = m // 2
        width = K - 8 * group
        start = STARTS[8 * group]
        first = STARTS[4 * m] // WIDTH * WIDTH
        last = -(-(STARTS[4 * m] + 4 * width) // WIDTH) * WIDTH
        if group == 0:
            basis_ref[0, :, WIDTH * m : WIDTH * (m + 1)] = received_ref[:, first:last]
            continue
        source = lax.broadcasted_iota(jnp.int32, (last - first, WIDTH), 0) + first
        column = lax.broadcasted_iota(jnp.int32, (last - first, WIDTH), 1) + WIDTH * m
        k, l = column // K, lax.rem(column, K)
        wanted = start + (k - 8 * group) * width + l - 8 * group
        place = jnp.where(jnp.logical_and(source == wanted, l >= 8 * group), 1.0, 0.0).astype(jnp.bfloat16)
        total = None
        for piece in pieces:
            term = jnp.dot(piece[:, first:last], place, preferred_element_type=jnp.float32)
            total = term if total is None else total + term
        basis_ref[0, :, WIDTH * m : WIDTH * (m + 1)] = total
    copy.wait()


def vmem(shape, dtype=jnp.float32):
    return pltpu.VMEM(shape, dtype)


def shards(n_wide, n_narrow, tests, block_inverse, face_weight, mixing, far_tiles, far_column, aggregate, owner_map):
    bf16 = jnp.bfloat16
    whole = pl.BlockSpec(memory_space=pltpu.VMEM)
    any_spec = pl.BlockSpec(memory_space=pl.ANY)
    smem = pl.BlockSpec(memory_space=pltpu.SMEM)
    labels = aggregate.reshape(PLANES * 4, 64)

    slots_total = n_wide * n_narrow * SLOT
    combined, gram = pl.pallas_call(
        functools.partial(relax_kernel, n_wide),
        out_shape=(
            jax.ShapeDtypeStruct((PLANES, ROWS, NODES), jnp.float32),
            jax.ShapeDtypeStruct((GRAM_ROWS, WIDTH), jnp.float32),
        ),
        in_specs=[any_spec, whole, whole, smem, any_spec, smem, whole],
        out_specs=(whole, whole),
        scratch_shapes=[
            vmem((PLANES, 4 * ROWS, 64)),
            vmem((PLANES + 2, ROWS, NODES)),
            vmem((PLANES + 2, ROWS, NODES)),
            vmem((PLANES + 2, ROWS, NODES)),
            vmem((PLANES, 54, 8, NODES)),
            vmem((SWEEPS, PLANES, 48, WIDTH), bf16),
            vmem((SWEEPS, PLANES, 48, WIDTH), bf16),
            vmem((ROWS, WIDTH)),
            vmem((PLANES, ROWS, NODES), bf16),
            vmem((PLANES, ROWS, NODES), bf16),
            vmem((PLANES, ROWS, NODES), bf16),
            vmem((PLANES, 3, NODES, NODES), bf16),
            vmem((PLANES, WIDTH, NODES), bf16),
            vmem((3, TRI // GRAM_PARTS, 2 * NODES), bf16),
            vmem((GRAM_ROWS, WIDTH)),
            vmem((GRAM_ROWS, WIDTH)),
            pltpu.SemaphoreType.DMA((2 * CHUNKS,)),
            pltpu.SemaphoreType.DMA((1,)),
            pltpu.SemaphoreType.DMA((2 * SWEEPS,)),
            pltpu.SemaphoreType.DMA((2 * SWEEPS,)),
            pltpu.SemaphoreType.DMA((SWEEPS * CHUNKS,)),
            pltpu.SemaphoreType.DMA((SWEEPS * CHUNKS,)),
            pltpu.SemaphoreType.DMA((4 * CHUNKS,)),
            pltpu.SemaphoreType.DMA((4 * CHUNKS,)),
            pltpu.SemaphoreType.DMA((GRAM_PARTS,)),
            pltpu.SemaphoreType.DMA((GRAM_PARTS,)),
        ],
        compiler_params=pltpu.CompilerParams(
            collective_id=0, has_side_effects=True, vmem_limit_bytes=56 * 1024 * 1024
        ),
        name="relax_far_gram",
    )(
        tests.reshape(PLANES, 4 * ROWS, 64),
        block_inverse.reshape(PLANES * 36, 64),
        face_weight.reshape(PLANES * 24, 64),
        mixing.transpose(1, 2, 0),
        far_tiles.reshape(PLANES, 3, NODES, NODES),
        far_column.transpose(2, 1, 0),
        labels,
    )

    packed, inverse = pl.pallas_call(
        factor_kernel,
        out_shape=(
            jax.ShapeDtypeStruct((slots_total, TRI), jnp.float32),
            jax.ShapeDtypeStruct((TRI, 3 * WIDTH), bf16),
        ),
        in_specs=[whole, whole],
        out_specs=(whole, whole),
        scratch_shapes=[vmem((TRI, WIDTH)), vmem((TRI, WIDTH))],
        compiler_params=pltpu.CompilerParams(vmem_limit_bytes=32 * 1024 * 1024),
        name="factor",
    )(gram, owner_map.reshape(1, owner_map.shape[0]))

    projected, received = pl.pallas_call(
        functools.partial(project_kernel, n_wide, n_narrow),
        out_shape=(
            jax.ShapeDtypeStruct((PLANES, 4 * ROWS, 64), jnp.float32),
            jax.ShapeDtypeStruct((slots_total, TRI), jnp.float32),
        ),
        in_specs=[whole, whole, whole, whole],
        out_specs=(whole, whole),
        scratch_shapes=[
            vmem((slots_total, TRI)),
            vmem((TRI, NODES)),
            vmem((SLOT, TRI)),
            pltpu.SemaphoreType.DMA,
            pltpu.SemaphoreType.DMA,
        ],
        compiler_params=pltpu.CompilerParams(
            collective_id=1, has_side_effects=True, vmem_limit_bytes=40 * 1024 * 1024
        ),
        name="project",
    )(packed, combined, labels, inverse)

    basis, prolong = pl.pallas_call(
        widen_kernel,
        out_shape=(
            jax.ShapeDtypeStruct((1, slots_total, K * K), jnp.float32),
            jax.ShapeDtypeStruct((PLANES, 4 * ROWS, 64), jnp.float32),
        ),
        in_specs=[whole, any_spec],
        out_specs=(whole, any_spec),
        scratch_shapes=[pltpu.SemaphoreType.DMA],
        compiler_params=pltpu.CompilerParams(vmem_limit_bytes=32 * 1024 * 1024),
        name="widen",
    )(received, projected)
    return prolong.reshape(tests.shape), basis


def solution(mesh):
    in_specs = (
        P("wide", None, None, "narrow", None),
        P("wide", None, None, "narrow", None),
        P("wide", None, "narrow", None),
        P(),
        P("wide", "narrow", None, None, None),
        P("wide", "narrow", None),
        P("wide", "narrow", None),
        P(("wide", "narrow")),
    )
    out_specs = (P("wide", None, None, "narrow", None), P(("wide", "narrow"), None, None))
    body = functools.partial(shards, mesh.shape["wide"], mesh.shape["narrow"])
    return jax.shard_map(body, mesh=mesh, in_specs=in_specs, out_specs=out_specs, check_vma=False)
```

```python
import functools

import jax
import jax.numpy as jnp
from jax import lax
from jax.experimental import pallas as pl
from jax.experimental.pallas import tpu as pltpu
from jax.sharding import PartitionSpec as P

MESH = pl.DeviceIdType.MESH
SWEEPS = 3
SLOT = 2
K = 32
ROWS = 3 * K
PLANES = 16
NODES = 256
WIDTH = 128
RIDGE = 0.001

BLOCKS = [(k, b) for k in range(K) for b in range(k // 8, K // 8)]
TRI = 8 * len(BLOCKS)
STARTS = {}
for place, (block_k, block_b) in enumerate(BLOCKS):
    STARTS.setdefault(block_k, 8 * place)
GRAM_ROWS = TRI + 16
CHUNKS = 8
PART = PLANES // CHUNKS
GRAM_PARTS = 4
EARLY = 4


def split3(x):
    hi = x.astype(jnp.bfloat16)
    rest = x - hi.astype(jnp.float32)
    mid = rest.astype(jnp.bfloat16)
    low = (rest - mid.astype(jnp.float32)).astype(jnp.bfloat16)
    return hi, mid, low


def join_rows(rows):
    return jnp.concatenate(rows, axis=1)


def setup_kernel(
    n_wide, n_narrow,
    tests_hbm, bi_ref, fw_ref, mix_ref, tiles_hbm, col_ref, label_ref, owner_ref,
    out_ref, received_ref,
    comb_ref, lower, inv, inverse_ref, packed_ref, landing, look, spare,
    raw, x0, x1, x2, coef, ysend, yrecv, ydup, from_left, planes, from_right, tiles, members, outer, acc, gram_in,
    tests_sems, tiles_sem, xsend_sems, xrecv_sems, ysend_sems, yrecv_sems, psend_sems, precv_sems, gsend_sems,
    grecv_sems, send_sem, recv_sem,
):
    w = lax.axis_index("wide")
    n = lax.axis_index("narrow")
    right = lax.rem(w + 1, n_wide)
    left = lax.rem(w + n_wide - 1, n_wide)
    other = 1 - n
    fields = [x0, x1, x2]

    def plane_at(i):
        half = i // 2
        return jnp.where(lax.rem(i, 2) == 0, PLANES // 2 - 1 - half, PLANES // 2 + half)

    tests_copies = []
    for q in range(CHUNKS):
        for j, start in enumerate((PLANES // 2 - 1 - q, PLANES // 2 + q)):
            span = pl.ds(start, 1)
            copy = pltpu.make_async_copy(tests_hbm.at[span], raw.at[span], tests_sems.at[2 * q + j])
            copy.start()
            tests_copies.append(copy)
    tiles_copy = pltpu.make_async_copy(tiles_hbm, tiles, tiles_sem.at[0])
    tiles_copy.start()

    barrier = pltpu.get_barrier_semaphore()
    count = n_wide * n_narrow
    me = w * n_narrow + n

    def peer(i):
        index = lax.rem(me + i, count)
        return index, (index // n_narrow, lax.rem(index, n_narrow))

    def greet(i, carry):
        pl.semaphore_signal(barrier, inc=1, device_id=peer(i)[1], device_id_type=MESH)
        return carry

    lax.fori_loop(1, count, greet, 0)

    lane = lax.broadcasted_iota(jnp.int32, (K + 16, WIDTH), 1)
    low_half = lane < 64
    low8 = low_half[0:8]
    is_low = n == 0

    def pack_row(first, second):
        chosen = jnp.where(is_low, second, first)
        turned = pltpu.roll(chosen, 64, 1)
        a = jnp.where(is_low, turned, chosen)[0:48]
        b = jnp.where(is_low, chosen, turned)[48:96]
        return jnp.where(low_half, a, b).astype(jnp.bfloat16)

    def y_copy(s, q):
        span = pl.ds(q * PART, PART)
        return pltpu.make_async_remote_copy(
            src_ref=ysend.at[s, span], dst_ref=yrecv.at[s, span], send_sem=ysend_sems.at[s * CHUNKS + q],
            recv_sem=yrecv_sems.at[s * CHUNKS + q], device_id=(w, other), device_id_type=MESH,
        )

    def x_copies(s):
        up = pltpu.make_async_remote_copy(
            src_ref=fields[s].at[PLANES], dst_ref=fields[s].at[0], send_sem=xsend_sems.at[2 * s],
            recv_sem=xrecv_sems.at[2 * s], device_id=(right, n), device_id_type=MESH,
        )
        down = pltpu.make_async_remote_copy(
            src_ref=fields[s].at[1], dst_ref=fields[s].at[PLANES + 1], send_sem=xsend_sems.at[2 * s + 1],
            recv_sem=xrecv_sems.at[2 * s + 1], device_id=(left, n), device_id_type=MESH,
        )
        return up, down

    has_right = w < n_wide - 1
    has_left = w > 0

    def start_x(s):
        up, down = x_copies(s)
        pl.when(has_right)(up.start)
        pl.when(has_left)(down.start)

    def wait_x(s):
        up, down = x_copies(s)
        pl.when(has_right)(up.wait_send)
        pl.when(has_left)(up.wait_recv)
        pl.when(has_left)(down.wait_send)
        pl.when(has_right)(down.wait_recv)

    @pl.when(jnp.logical_not(has_left))
    def clear_left():
        for field in fields:
            field[0] = jnp.zeros((ROWS, NODES), jnp.float32)

    @pl.when(jnp.logical_not(has_right))
    def clear_right():
        for field in fields:
            field[PLANES + 1] = jnp.zeros((ROWS, NODES), jnp.float32)

    def unpack_tests(i, carry):
        p = plane_at(i)
        for c in range(3):
            for kb in range(K // 8):
                pieces = [raw[p, pl.ds(96 * kb + 4 * c + y, 8, stride=12), :] for y in range(4)]
                x0[p + 1, pl.ds(c * K + 8 * kb, 8), :] = join_rows(pieces)
        ysend[0, i] = pack_row(x0[p + 1, :, 0:128], x0[p + 1, :, 128:256])
        return carry

    for q in range(CHUNKS):
        tests_copies[2 * q].wait()
        tests_copies[2 * q + 1].wait()
        lax.fori_loop(q * PART, (q + 1) * PART, unpack_tests, 0)

    lane_wide = lax.broadcasted_iota(jnp.int32, (8, NODES), 1)
    z_place = lax.rem(lane_wide, 64)

    def make_coef(p, carry):
        def wide_row(ref, first):
            row = join_rows([ref[pl.ds(first + y, 1), :] for y in range(4)])
            return jnp.broadcast_to(row, (8, NODES))

        inv_rows = [wide_row(bi_ref, 36 * p + 4 * i) for i in range(9)]
        edges = [
            jnp.logical_and(p == PLANES - 1, w == n_wide - 1),
            jnp.logical_and(p == 0, w == 0),
            jnp.logical_and(lane_wide >= 192, n == 1),
            jnp.logical_and(lane_wide < 64, n == 0),
            z_place == 63,
            z_place == 0,
        ]
        for d in range(6):
            weight = jnp.where(edges[d], 0.0, 0.5 * wide_row(fw_ref, 24 * p + 4 * d))
            for a in range(3):
                for b in range(3):
                    total = inv_rows[3 * a] * mix_ref[0, b, d]
                    total += inv_rows[3 * a + 1] * mix_ref[1, b, d]
                    total += inv_rows[3 * a + 2] * mix_ref[2, b, d]
                    coef[p, 9 * d + 3 * a + b] = total * weight
        label = join_rows([label_ref[pl.ds(4 * p + y, 1), :] for y in range(4)])
        groups = lax.broadcasted_iota(jnp.int32, (WIDTH, NODES), 0)
        members[p] = jnp.where(groups == label, 1.0, 0.0).astype(jnp.bfloat16)
        return carry

    lax.fori_loop(0, EARLY, make_coef, 0)
    pl.semaphore_wait(barrier, count - 1)
    for q in range(CHUNKS):
        y_copy(0, q).start()
    start_x(0)
    lax.fori_loop(EARLY, PLANES, make_coef, 0)

    def sweep_plane(s, i):
        p = plane_at(i)
        src = fields[s]
        packed = yrecv[s, i].astype(jnp.float32)
        turned = pltpu.roll(packed, 64, 1)
        ydup[0:48] = jnp.where(low_half, packed, turned)
        ydup[48:96] = jnp.where(low_half, turned, packed)
        for kb in range(K // 8):
            near = []
            own = []
            for c in range(3):
                rows = pl.ds(c * K + kb * 8, 8)
                mid = src[p + 1, rows, :]
                own.append(mid)
                c0, c1 = mid[:, 0:128], mid[:, 128:256]
                r0, r1 = pltpu.roll(c0, 64, 1), pltpu.roll(c1, 64, 1)
                dup = ydup[rows]
                between = jnp.where(low8, r0, r1)
                y_up = jnp.concatenate([between, jnp.where(low8, r1, dup)], axis=1)
                y_down = jnp.concatenate([jnp.where(low8, dup, r0), between], axis=1)
                z_up = jnp.concatenate([pltpu.roll(c0, 127, 1), pltpu.roll(c1, 127, 1)], axis=1)
                z_down = jnp.concatenate([pltpu.roll(c0, 1, 1), pltpu.roll(c1, 1, 1)], axis=1)
                near.append([src[p + 2, rows, :], src[p, rows, :], y_up, y_down, z_up, z_down])
            for a in range(3):
                total = 0.5 * own[a]
                for d in range(6):
                    for b in range(3):
                        total += coef[p, 9 * d + 3 * a + b] * near[b][d]
                rows = pl.ds(a * K + kb * 8, 8)
                if s + 1 < SWEEPS:
                    fields[s + 1][p + 1, rows, :] = total
                else:
                    comb_ref[p, rows, :] = total
        if s + 1 < SWEEPS:
            ysend[s + 1, i] = pack_row(fields[s + 1][p + 1, :, 0:128], fields[s + 1][p + 1, :, 128:256])
        else:
            planes[p] = comb_ref[p].astype(jnp.bfloat16)

    def plane_copies(q):
        copies = []
        for j, start in enumerate((PLANES // 2 - 1 - q, PLANES // 2 + q)):
            span = pl.ds(start, 1)
            for side, (target, landing) in enumerate(((right, from_left), (left, from_right))):
                at = 4 * q + 2 * j + side
                copies.append(
                    pltpu.make_async_remote_copy(
                        src_ref=planes.at[span], dst_ref=landing.at[span], send_sem=psend_sems.at[at],
                        recv_sem=precv_sems.at[at], device_id=(target, n), device_id_type=MESH,
                    )
                )
        return copies

    for s in range(SWEEPS):

        def one_chunk(q, carry, s=s):
            y_copy(s, q).wait()
            pl.when(q == CHUNKS - 1)(lambda: wait_x(s))

            def one_plane(j, inner):
                sweep_plane(s, q * PART + j)
                return inner

            lax.fori_loop(0, PART, one_plane, 0)
            if s + 1 < SWEEPS:
                y_copy(s + 1, q).start()
            else:
                for copy in plane_copies(q):
                    copy.start()
            return carry

        lax.fori_loop(0, CHUNKS, one_chunk, 0)
        if s + 1 < SWEEPS:
            start_x(s + 1)

    tiles_copy.wait()
    sources = [from_left, planes, from_right]

    def far_product(r, slot):
        return jnp.dot(
            sources[slot][col_ref[slot, 0, r]], tiles[r, slot], preferred_element_type=jnp.float32
        )

    def near_far(r, carry):
        comb_ref[r] = comb_ref[r] + far_product(r, 1)
        return carry

    lax.fori_loop(0, PLANES, near_far, 0)

    acc[...] = jnp.zeros_like(acc)
    for q in range(CHUNKS):
        for copy in plane_copies(q):
            copy.wait()

    def side_far(r, carry):
        comb_ref[r] = comb_ref[r] + (far_product(r, 0) + far_product(r, 2))
        return carry

    lax.fori_loop(0, PLANES, side_far, 0)

    pairs = len(BLOCKS) // 2 // GRAM_PARTS
    rows_part = 16 * pairs

    def gram_copy(t):
        height = rows_part if t + 1 < GRAM_PARTS else GRAM_ROWS - rows_part * t
        span = pl.ds(rows_part * t, height)
        return pltpu.make_async_remote_copy(
            src_ref=acc.at[span], dst_ref=gram_in.at[span], send_sem=gsend_sems.at[t], recv_sem=grecv_sems.at[t],
            device_id=(w, other), device_id_type=MESH,
        )

    def contract(values, member):
        return lax.dot_general(values, member, (((1,), (1,)), ((), ())), preferred_element_type=jnp.float32)

    for t in range(GRAM_PARTS):

        def gram_planes(h, carry, t=t):
            for side in range(2):
                r = 2 * h + side
                lanes = pl.ds(side * NODES, NODES)
                for pair in range(pairs):
                    parts = []
                    for k, b in BLOCKS[2 * (pairs * t + pair) : 2 * (pairs * t + pair) + 2]:
                        value = None
                        for c in range(3):
                            term = comb_ref[r, c * K + k : c * K + k + 1, :] * comb_ref[r, pl.ds(c * K + 8 * b, 8), :]
                            value = term if value is None else value + term
                        parts.append(value)
                    for piece, values in enumerate(split3(jnp.concatenate(parts, axis=0))):
                        outer[piece, pl.ds(16 * pair, 16), lanes] = values
            total = None
            for side in range(2):
                member = members[2 * h + side]
                lanes = pl.ds(side * NODES, NODES)
                for piece in range(3):
                    term = contract(outer[piece, :, lanes], member)
                    total = term if total is None else total + term
            acc[pl.ds(rows_part * t, rows_part), :] += total
            if t + 1 == GRAM_PARTS:
                ones = jnp.ones((16, NODES), jnp.bfloat16)
                acc[TRI:GRAM_ROWS] += contract(ones, members[2 * h]) + contract(ones, members[2 * h + 1])
            return carry

        lax.fori_loop(0, PLANES // 2, gram_planes, 0)
        gram_copy(t).start()

    for t in range(GRAM_PARTS):
        gram_copy(t).wait()

    def gram_rows(first, height):
        span = pl.ds(first, height)
        return acc[span, :] + gram_in[span, :]

    factorize(gram_rows, owner_ref, packed_ref, inverse_ref, lower, inv)

    own_span = pl.ds(SLOT * me, SLOT)
    pltpu.make_async_copy(packed_ref.at[own_span], landing.at[own_span], recv_sem).start()
    pltpu.make_async_copy(packed_ref.at[own_span], spare, send_sem).start()

    def send(i, carry):
        index, device = peer(i)
        pltpu.make_async_remote_copy(
            src_ref=packed_ref.at[pl.ds(SLOT * index, SLOT)], dst_ref=landing.at[own_span], send_sem=send_sem,
            recv_sem=recv_sem, device_id=device, device_id_type=MESH,
        ).start()
        return carry

    lax.fori_loop(1, count, send, 0)

    def project_plane(r, carry):
        member = members[r]
        look[...] = jnp.dot(
            inverse_ref[...], jnp.concatenate([member, member, member], axis=0), preferred_element_type=jnp.float32
        )
        for b in range(K // 8):
            totals = [None] * 3
            for l in range(8 * (b + 1)):
                weight = look[pl.ds(STARTS[l] + 8 * (b - l // 8), 8), :]
                for c in range(3):
                    term = weight * comb_ref[r, c * K + l : c * K + l + 1, :]
                    totals[c] = term if totals[c] is None else totals[c] + term
            for c in range(3):
                for y in range(4):
                    out_ref[r, pl.ds(96 * b + 4 * c + y, 8, stride=12), :] = totals[c][:, 64 * y : 64 * (y + 1)]
        return carry

    lax.fori_loop(0, PLANES, project_plane, 0)
    everything = pltpu.make_async_remote_copy(
        src_ref=packed_ref, dst_ref=landing, send_sem=send_sem, recv_sem=recv_sem, device_id=peer(1)[1],
        device_id_type=MESH,
    )
    everything.wait_send()
    everything.wait_recv()
    received_ref[...] = landing[...]


def slot_table(owner_ref, slots_total):
    count = owner_ref.shape[1]
    owners = owner_ref[...].astype(jnp.float32)
    across = jnp.broadcast_to(owners, (count, count))
    row = lax.broadcasted_iota(jnp.int32, (count, count), 0)
    column = lax.broadcasted_iota(jnp.int32, (count, count), 1)
    down = jnp.sum(jnp.where(row == column, across, 0.0), axis=1, keepdims=True)
    earlier = jnp.where(jnp.logical_and(down == across, row < column), 1.0, 0.0)
    target = owners * SLOT + jnp.sum(earlier, axis=0, keepdims=True)
    none = jnp.full_like(target, -1.0)
    is_low = lax.axis_index("narrow") == 0
    lanes = join_rows([jnp.where(is_low, target, none), jnp.where(is_low, none, target)])
    slots = lax.broadcasted_iota(jnp.int32, (slots_total, WIDTH), 0).astype(jnp.float32)
    return jnp.where(slots == lanes, 1.0, 0.0).astype(jnp.bfloat16)


def factorize(gram_rows, owner_ref, packed_ref, inverse_ref, lower, inv):
    scale = 1.0 / (3.0 * gram_rows(TRI, 1))
    row = lax.broadcasted_iota(jnp.int32, (K, WIDTH), 0)
    columns = []
    for k in range(K):
        first = 8 * (k // 8)
        height = K - first
        column = gram_rows(STARTS[k], height) * scale
        columns.append(column + jnp.where(row[first:] == k, RIDGE, 0.0))
    reciprocals = []
    for k in range(K):
        first = 8 * (k // 8)
        at = k - first
        pivot = jnp.sqrt(columns[k][at : at + 1])
        reciprocal = 1.0 / pivot
        reciprocals.append(reciprocal)
        column = jnp.where(row[first:] >= k, columns[k] * reciprocal, 0.0)
        columns[k] = column
        for m in range(k + 1, K):
            begin = 8 * (m // 8)
            columns[m] = columns[m] - column[m - first : m - first + 1] * column[begin - first :]
        lower[pl.ds(STARTS[k], K - first), :] = column
    for l in range(K):
        first = 8 * (l // 8)
        solved = jnp.where(row[first:] == l, 1.0, 0.0)
        for m in range(l, K):
            base = 8 * (m // 8)
            value = solved[m - first : m - first + 1] * reciprocals[m]
            here = solved[base - first :]
            here = jnp.where(row[base:] == m, value, jnp.where(row[base:] > m, here - columns[m] * value, here))
            solved = here if base == first else jnp.concatenate([solved[: base - first], here], axis=0)
        inv[pl.ds(STARTS[l], K - first), :] = solved
    for i, piece in enumerate(split3(inv[...])):
        inverse_ref[:, i * WIDTH : (i + 1) * WIDTH] = piece
    table = slot_table(owner_ref, packed_ref.shape[0])
    total = None
    for piece in split3(lower[...]):
        term = lax.dot_general(table, piece, (((1,), (1,)), ((), ())), preferred_element_type=jnp.float32)
        total = term if total is None else total + term
    packed_ref[...] = total


def widen_kernel(received_ref, prolong_in, basis_ref, prolong_out, sem):
    copy = pltpu.make_async_copy(prolong_in, prolong_out, sem)
    copy.start()
    pieces = split3(received_ref[...])
    for m in range(K * K // WIDTH):
        group = m // 2
        width = K - 8 * group
        start = STARTS[8 * group]
        first = STARTS[4 * m] // WIDTH * WIDTH
        last = -(-(STARTS[4 * m] + 4 * width) // WIDTH) * WIDTH
        if group == 0:
            basis_ref[0, :, WIDTH * m : WIDTH * (m + 1)] = received_ref[:, first:last]
            continue
        source = lax.broadcasted_iota(jnp.int32, (last - first, WIDTH), 0) + first
        column = lax.broadcasted_iota(jnp.int32, (last - first, WIDTH), 1) + WIDTH * m
        k, l = column // K, lax.rem(column, K)
        wanted = start + (k - 8 * group) * width + l - 8 * group
        place = jnp.where(jnp.logical_and(source == wanted, l >= 8 * group), 1.0, 0.0).astype(jnp.bfloat16)
        total = None
        for piece in pieces:
            term = jnp.dot(piece[:, first:last], place, preferred_element_type=jnp.float32)
            total = term if total is None else total + term
        basis_ref[0, :, WIDTH * m : WIDTH * (m + 1)] = total
    copy.wait()


def vmem(shape, dtype=jnp.float32):
    return pltpu.VMEM(shape, dtype)


def shards(n_wide, n_narrow, tests, block_inverse, face_weight, mixing, far_tiles, far_column, aggregate, owner_map):
    bf16 = jnp.bfloat16
    whole = pl.BlockSpec(memory_space=pltpu.VMEM)
    any_spec = pl.BlockSpec(memory_space=pl.ANY)
    hbm = pl.BlockSpec(memory_space=pltpu.HBM)
    smem = pl.BlockSpec(memory_space=pltpu.SMEM)
    labels = aggregate.reshape(PLANES * 4, 64)

    slots_total = n_wide * n_narrow * SLOT
    projected, received = pl.pallas_call(
        functools.partial(setup_kernel, n_wide, n_narrow),
        out_shape=(
            jax.ShapeDtypeStruct((PLANES, 4 * ROWS, 64), jnp.float32),
            jax.ShapeDtypeStruct((slots_total, TRI), jnp.float32),
        ),
        in_specs=[hbm, whole, whole, smem, hbm, smem, whole, whole],
        out_specs=(whole, whole),
        scratch_shapes=[
            vmem((PLANES, ROWS, NODES)),
            vmem((TRI, WIDTH)),
            vmem((TRI, WIDTH)),
            vmem((TRI, 3 * WIDTH), bf16),
            vmem((slots_total, TRI)),
            vmem((slots_total, TRI)),
            vmem((TRI, NODES)),
            vmem((SLOT, TRI)),
            vmem((PLANES, 4 * ROWS, 64)),
            vmem((PLANES + 2, ROWS, NODES)),
            vmem((PLANES + 2, ROWS, NODES)),
            vmem((PLANES + 2, ROWS, NODES)),
            vmem((PLANES, 54, 8, NODES)),
            vmem((SWEEPS, PLANES, 48, WIDTH), bf16),
            vmem((SWEEPS, PLANES, 48, WIDTH), bf16),
            vmem((ROWS, WIDTH)),
            vmem((PLANES, ROWS, NODES), bf16),
            vmem((PLANES, ROWS, NODES), bf16),
            vmem((PLANES, ROWS, NODES), bf16),
            vmem((PLANES, 3, NODES, NODES), bf16),
            vmem((PLANES, WIDTH, NODES), bf16),
            vmem((3, TRI // GRAM_PARTS, 2 * NODES), bf16),
            vmem((GRAM_ROWS, WIDTH)),
            vmem((GRAM_ROWS, WIDTH)),
            pltpu.SemaphoreType.DMA((2 * CHUNKS,)),
            pltpu.SemaphoreType.DMA((1,)),
            pltpu.SemaphoreType.DMA((2 * SWEEPS,)),
            pltpu.SemaphoreType.DMA((2 * SWEEPS,)),
            pltpu.SemaphoreType.DMA((SWEEPS * CHUNKS,)),
            pltpu.SemaphoreType.DMA((SWEEPS * CHUNKS,)),
            pltpu.SemaphoreType.DMA((4 * CHUNKS,)),
            pltpu.SemaphoreType.DMA((4 * CHUNKS,)),
            pltpu.SemaphoreType.DMA((GRAM_PARTS,)),
            pltpu.SemaphoreType.DMA((GRAM_PARTS,)),
            pltpu.SemaphoreType.DMA,
            pltpu.SemaphoreType.DMA,
        ],
        compiler_params=pltpu.CompilerParams(
            collective_id=0, has_side_effects=True, vmem_limit_bytes=48 * 1024 * 1024
        ),
        name="setup",
    )(
        tests.reshape(PLANES, 4 * ROWS, 64),
        block_inverse.reshape(PLANES * 36, 64),
        face_weight.reshape(PLANES * 24, 64),
        mixing.transpose(1, 2, 0),
        far_tiles.reshape(PLANES, 3, NODES, NODES),
        far_column.transpose(2, 1, 0),
        labels,
        owner_map.reshape(1, owner_map.shape[0]),
    )

    basis, prolong = pl.pallas_call(
        widen_kernel,
        out_shape=(
            jax.ShapeDtypeStruct((1, slots_total, K * K), jnp.float32),
            jax.ShapeDtypeStruct((PLANES, 4 * ROWS, 64), jnp.float32),
        ),
        in_specs=[whole, any_spec],
        out_specs=(whole, any_spec),
        scratch_shapes=[pltpu.SemaphoreType.DMA],
        compiler_params=pltpu.CompilerParams(vmem_limit_bytes=32 * 1024 * 1024),
        name="widen",
    )(received, projected)
    return prolong.reshape(tests.shape), basis


def solution(mesh):
    in_specs = (
        P("wide", None, None, "narrow", None),
        P("wide", None, None, "narrow", None),
        P("wide", None, "narrow", None),
        P(),
        P("wide", "narrow", None, None, None),
        P("wide", "narrow", None),
        P("wide", "narrow", None),
        P(("wide", "narrow")),
    )
    out_specs = (P("wide", None, None, "narrow", None), P(("wide", "narrow"), None, None))
    body = functools.partial(shards, mesh.shape["wide"], mesh.shape["narrow"])
    return jax.shard_map(body, mesh=mesh, in_specs=in_specs, out_specs=out_specs, check_vma=False)
```

```python
import functools

import jax
import jax.numpy as jnp
from jax import lax
from jax.experimental import pallas as pl
from jax.experimental.pallas import tpu as pltpu
from jax.sharding import PartitionSpec as P

MESH = pl.DeviceIdType.MESH
SWEEPS = 3
SLOT = 2
K = 32
ROWS = 3 * K
PLANES = 16
NODES = 256
WIDTH = 128
RIDGE = 0.001

BLOCKS = [(k, b) for k in range(K) for b in range(k // 8, K // 8)]
TRI = 8 * len(BLOCKS)
STARTS = {}
for place, (block_k, block_b) in enumerate(BLOCKS):
    STARTS.setdefault(block_k, 8 * place)
GRAM_ROWS = TRI + 16
CHUNKS = 8
PART = PLANES // CHUNKS
GRAM_PARTS = 4
EARLY = 4
LAG = 5
PASSES = 4


def split3(x):
    hi = x.astype(jnp.bfloat16)
    rest = x - hi.astype(jnp.float32)
    mid = rest.astype(jnp.bfloat16)
    low = (rest - mid.astype(jnp.float32)).astype(jnp.bfloat16)
    return hi, mid, low


def join_rows(rows):
    return jnp.concatenate(rows, axis=1)


def setup_kernel(
    n_wide, n_narrow,
    tests_hbm, bi_ref, fw_ref, mix_ref, tiles_hbm, col_ref, label_ref, owner_ref,
    out_hbm, received_ref,
    comb_ref, lower, inv, inverse_ref, packed_ref, landing, look, spare,
    raw, x0, x1, x2, coef, xsend, xrecv, ysend, yrecv, ydup, from_left, planes, from_right, tiles, members, outer, acc, gram_in,
    tests_sems, tiles_sem, xsend_sems, xrecv_sems, ysend_sems, yrecv_sems, psend_sems, precv_sems, gsend_sems,
    grecv_sems, send_sem, recv_sem, out_sems,
):
    w = lax.axis_index("wide")
    n = lax.axis_index("narrow")
    right = lax.rem(w + 1, n_wide)
    left = lax.rem(w + n_wide - 1, n_wide)
    other = 1 - n
    fields = [x0, x1, x2]

    def plane_at(i):
        half = i // 2
        return jnp.where(lax.rem(i, 2) == 0, PLANES // 2 - 1 - half, PLANES // 2 + half)

    tests_copies = []
    for q in range(CHUNKS):
        for j, start in enumerate((PLANES // 2 - 1 - q, PLANES // 2 + q)):
            span = pl.ds(start, 1)
            copy = pltpu.make_async_copy(tests_hbm.at[span], raw.at[span], tests_sems.at[2 * q + j])
            copy.start()
            tests_copies.append(copy)
    tiles_copy = pltpu.make_async_copy(tiles_hbm, tiles, tiles_sem.at[0])
    tiles_copy.start()

    barrier = pltpu.get_barrier_semaphore()
    count = n_wide * n_narrow
    me = w * n_narrow + n

    def peer(i):
        index = lax.rem(me + i, count)
        return index, (index // n_narrow, lax.rem(index, n_narrow))

    def greet(i, carry):
        pl.semaphore_signal(barrier, inc=1, device_id=peer(i)[1], device_id_type=MESH)
        return carry

    lax.fori_loop(1, count, greet, 0)

    lane = lax.broadcasted_iota(jnp.int32, (K + 16, WIDTH), 1)
    low_half = lane < 64
    low8 = low_half[0:8]
    is_low = n == 0

    def pack_row(first, second):
        chosen = jnp.where(is_low, second, first)
        turned = pltpu.roll(chosen, 64, 1)
        a = jnp.where(is_low, turned, chosen)[0:48]
        b = jnp.where(is_low, chosen, turned)[48:96]
        return jnp.where(low_half, a, b).astype(jnp.bfloat16)

    def y_copy(s, q):
        span = pl.ds(q * PART, PART)
        return pltpu.make_async_remote_copy(
            src_ref=ysend.at[s, span], dst_ref=yrecv.at[s, span], send_sem=ysend_sems.at[s * CHUNKS + q],
            recv_sem=yrecv_sems.at[s * CHUNKS + q], device_id=(w, other), device_id_type=MESH,
        )

    def x_copies(s):
        up = pltpu.make_async_remote_copy(
            src_ref=xsend.at[s, 0], dst_ref=xrecv.at[s, 0], send_sem=xsend_sems.at[2 * s],
            recv_sem=xrecv_sems.at[2 * s], device_id=(right, n), device_id_type=MESH,
        )
        down = pltpu.make_async_remote_copy(
            src_ref=xsend.at[s, 1], dst_ref=xrecv.at[s, 1], send_sem=xsend_sems.at[2 * s + 1],
            recv_sem=xrecv_sems.at[2 * s + 1], device_id=(left, n), device_id_type=MESH,
        )
        return up, down

    has_right = w < n_wide - 1
    has_left = w > 0

    def start_x(s):
        up, down = x_copies(s)
        xsend[s, 0] = fields[s][PLANES].astype(jnp.bfloat16)
        xsend[s, 1] = fields[s][1].astype(jnp.bfloat16)
        pl.when(has_right)(up.start)
        pl.when(has_left)(down.start)

    def wait_x(s):
        up, down = x_copies(s)
        pl.when(has_right)(up.wait_send)
        pl.when(has_left)(up.wait_recv)
        pl.when(has_left)(down.wait_send)
        pl.when(has_right)(down.wait_recv)

        def widen_left():
            fields[s][0] = xrecv[s, 0].astype(jnp.float32)

        def widen_right():
            fields[s][PLANES + 1] = xrecv[s, 1].astype(jnp.float32)

        pl.when(has_left)(widen_left)
        pl.when(has_right)(widen_right)

    @pl.when(jnp.logical_not(has_left))
    def clear_left():
        for field in fields:
            field[0] = jnp.zeros((ROWS, NODES), jnp.float32)

    @pl.when(jnp.logical_not(has_right))
    def clear_right():
        for field in fields:
            field[PLANES + 1] = jnp.zeros((ROWS, NODES), jnp.float32)

    def unpack_tests(i, carry):
        p = plane_at(i)
        for c in range(3):
            for kb in range(K // 8):
                pieces = [raw[p, pl.ds(96 * kb + 4 * c + y, 8, stride=12), :] for y in range(4)]
                x0[p + 1, pl.ds(c * K + 8 * kb, 8), :] = join_rows(pieces)
        ysend[0, i] = pack_row(x0[p + 1, :, 0:128], x0[p + 1, :, 128:256])
        return carry

    for q in range(CHUNKS):
        tests_copies[2 * q].wait()
        tests_copies[2 * q + 1].wait()
        lax.fori_loop(q * PART, (q + 1) * PART, unpack_tests, 0)

    lane_wide = lax.broadcasted_iota(jnp.int32, (8, NODES), 1)
    z_place = lax.rem(lane_wide, 64)

    def make_coef(p, carry):
        def wide_row(ref, first):
            row = join_rows([ref[pl.ds(first + y, 1), :] for y in range(4)])
            return jnp.broadcast_to(row, (8, NODES))

        inv_rows = [wide_row(bi_ref, 36 * p + 4 * i) for i in range(9)]
        edges = [
            jnp.logical_and(p == PLANES - 1, w == n_wide - 1),
            jnp.logical_and(p == 0, w == 0),
            jnp.logical_and(lane_wide >= 192, n == 1),
            jnp.logical_and(lane_wide < 64, n == 0),
            z_place == 63,
            z_place == 0,
        ]
        for d in range(6):
            weight = jnp.where(edges[d], 0.0, 0.5 * wide_row(fw_ref, 24 * p + 4 * d))
            for a in range(3):
                for b in range(3):
                    total = inv_rows[3 * a] * mix_ref[0, b, d]
                    total += inv_rows[3 * a + 1] * mix_ref[1, b, d]
                    total += inv_rows[3 * a + 2] * mix_ref[2, b, d]
                    coef[p, 9 * d + 3 * a + b] = total * weight
        label = join_rows([label_ref[pl.ds(4 * p + y, 1), :] for y in range(4)])
        groups = lax.broadcasted_iota(jnp.int32, (WIDTH, NODES), 0)
        members[p] = jnp.where(groups == label, 1.0, 0.0).astype(jnp.bfloat16)
        return carry

    lax.fori_loop(0, EARLY, make_coef, 0)
    pl.semaphore_wait(barrier, count - 1)
    for q in range(CHUNKS):
        y_copy(0, q).start()
    start_x(0)
    lax.fori_loop(EARLY, PLANES, make_coef, 0)

    def sweep_plane(s, i):
        p = plane_at(i)
        src = fields[s]
        packed = yrecv[s, i].astype(jnp.float32)
        turned = pltpu.roll(packed, 64, 1)
        ydup[0:48] = jnp.where(low_half, packed, turned)
        ydup[48:96] = jnp.where(low_half, turned, packed)
        for kb in range(K // 8):
            near = []
            own = []
            for c in range(3):
                rows = pl.ds(c * K + kb * 8, 8)
                mid = src[p + 1, rows, :]
                own.append(mid)
                c0, c1 = mid[:, 0:128], mid[:, 128:256]
                r0, r1 = pltpu.roll(c0, 64, 1), pltpu.roll(c1, 64, 1)
                dup = ydup[rows]
                between = jnp.where(low8, r0, r1)
                y_up = jnp.concatenate([between, jnp.where(low8, r1, dup)], axis=1)
                y_down = jnp.concatenate([jnp.where(low8, dup, r0), between], axis=1)
                z_up = jnp.concatenate([pltpu.roll(c0, 127, 1), pltpu.roll(c1, 127, 1)], axis=1)
                z_down = jnp.concatenate([pltpu.roll(c0, 1, 1), pltpu.roll(c1, 1, 1)], axis=1)
                near.append([src[p + 2, rows, :], src[p, rows, :], y_up, y_down, z_up, z_down])
            for a in range(3):
                total = 0.5 * own[a]
                for d in range(6):
                    for b in range(3):
                        total += coef[p, 9 * d + 3 * a + b] * near[b][d]
                rows = pl.ds(a * K + kb * 8, 8)
                if s + 1 < SWEEPS:
                    fields[s + 1][p + 1, rows, :] = total
                else:
                    comb_ref[p, rows, :] = total
        if s + 1 < SWEEPS:
            ysend[s + 1, i] = pack_row(fields[s + 1][p + 1, :, 0:128], fields[s + 1][p + 1, :, 128:256])
        else:
            planes[p] = comb_ref[p].astype(jnp.bfloat16)

    def plane_copies(q):
        copies = []
        for j, start in enumerate((PLANES // 2 - 1 - q, PLANES // 2 + q)):
            span = pl.ds(start, 1)
            for side, (target, landing) in enumerate(((right, from_left), (left, from_right))):
                at = 4 * q + 2 * j + side
                copies.append(
                    pltpu.make_async_remote_copy(
                        src_ref=planes.at[span], dst_ref=landing.at[span], send_sem=psend_sems.at[at],
                        recv_sem=precv_sems.at[at], device_id=(target, n), device_id_type=MESH,
                    )
                )
        return copies

    def do_chunk(s, q):
        y_copy(s, q).wait()
        pl.when(q == CHUNKS - 1)(lambda: wait_x(s))

        def one_plane(j, inner):
            sweep_plane(s, q * PART + j)
            return inner

        lax.fori_loop(0, PART, one_plane, 0)
        if s + 1 < SWEEPS:
            y_copy(s + 1, q).start()
            pl.when(q == CHUNKS - 1)(lambda: start_x(s + 1))
        else:
            for copy in plane_copies(q):
                copy.start()

    def wave_step(t, carry):
        for s in range(SWEEPS):
            q = t - LAG * s
            pl.when(jnp.logical_and(q >= 0, q < CHUNKS))(functools.partial(do_chunk, s, q))
        return carry

    lax.fori_loop(0, CHUNKS + LAG * (SWEEPS - 1), wave_step, 0)

    tiles_copy.wait()
    sources = [from_left, planes, from_right]

    def far_product(r, slot):
        return jnp.dot(
            sources[slot][col_ref[slot, 0, r]], tiles[r, slot], preferred_element_type=jnp.float32
        )

    def near_far(r, carry):
        comb_ref[r] = comb_ref[r] + far_product(r, 1)
        return carry

    lax.fori_loop(0, PLANES, near_far, 0)

    acc[...] = jnp.zeros_like(acc)
    for q in range(CHUNKS):
        for copy in plane_copies(q):
            copy.wait()

    def side_far(r, carry):
        comb_ref[r] = comb_ref[r] + (far_product(r, 0) + far_product(r, 2))
        return carry

    lax.fori_loop(0, PLANES, side_far, 0)

    pairs = len(BLOCKS) // 2 // GRAM_PARTS
    rows_part = 16 * pairs

    def gram_copy(t):
        height = rows_part if t + 1 < GRAM_PARTS else GRAM_ROWS - rows_part * t
        span = pl.ds(rows_part * t, height)
        return pltpu.make_async_remote_copy(
            src_ref=acc.at[span], dst_ref=gram_in.at[span], send_sem=gsend_sems.at[t], recv_sem=grecv_sems.at[t],
            device_id=(w, other), device_id_type=MESH,
        )

    def contract(values, member):
        return lax.dot_general(values, member, (((1,), (1,)), ((), ())), preferred_element_type=jnp.float32)

    for t in range(GRAM_PARTS):

        def gram_planes(h, carry, t=t):
            for side in range(2):
                r = 2 * h + side
                lanes = pl.ds(side * NODES, NODES)
                for pair in range(pairs):
                    parts = []
                    for k, b in BLOCKS[2 * (pairs * t + pair) : 2 * (pairs * t + pair) + 2]:
                        value = None
                        for c in range(3):
                            term = comb_ref[r, c * K + k : c * K + k + 1, :] * comb_ref[r, pl.ds(c * K + 8 * b, 8), :]
                            value = term if value is None else value + term
                        parts.append(value)
                    for piece, values in enumerate(split3(jnp.concatenate(parts, axis=0))):
                        outer[piece, pl.ds(16 * pair, 16), lanes] = values
            total = None
            for side in range(2):
                member = members[2 * h + side]
                lanes = pl.ds(side * NODES, NODES)
                for piece in range(3):
                    term = contract(outer[piece, :, lanes], member)
                    total = term if total is None else total + term
            acc[pl.ds(rows_part * t, rows_part), :] += total
            if t + 1 == GRAM_PARTS:
                ones = jnp.ones((16, NODES), jnp.bfloat16)
                acc[TRI:GRAM_ROWS] += contract(ones, members[2 * h]) + contract(ones, members[2 * h + 1])
            return carry

        lax.fori_loop(0, PLANES // 2, gram_planes, 0)
        gram_copy(t).start()

    for t in range(GRAM_PARTS):
        gram_copy(t).wait()

    def gram_rows(first, height):
        span = pl.ds(first, height)
        return acc[span, :] + gram_in[span, :]

    factorize(gram_rows, owner_ref, packed_ref, inverse_ref, lower, inv)

    own_span = pl.ds(SLOT * me, SLOT)
    pltpu.make_async_copy(packed_ref.at[own_span], landing.at[own_span], recv_sem).start()
    pltpu.make_async_copy(packed_ref.at[own_span], spare, send_sem).start()

    def send(i, carry):
        index, device = peer(i)
        pltpu.make_async_remote_copy(
            src_ref=packed_ref.at[pl.ds(SLOT * index, SLOT)], dst_ref=landing.at[own_span], send_sem=send_sem,
            recv_sem=recv_sem, device_id=device, device_id_type=MESH,
        ).start()
        return carry

    lax.fori_loop(1, count, send, 0)

    def project_plane(r, carry):
        member = members[r]
        look[...] = jnp.dot(
            inverse_ref[...], jnp.concatenate([member, member, member], axis=0), preferred_element_type=jnp.float32
        )
        for b in range(K // 8):
            totals = [None] * 3
            for l in range(8 * (b + 1)):
                weight = look[pl.ds(STARTS[l] + 8 * (b - l // 8), 8), :]
                for c in range(3):
                    term = weight * comb_ref[r, c * K + l : c * K + l + 1, :]
                    totals[c] = term if totals[c] is None else totals[c] + term
            for c in range(3):
                for y in range(4):
                    raw[r, pl.ds(96 * b + 4 * c + y, 8, stride=12), :] = totals[c][:, 64 * y : 64 * (y + 1)]
        return carry

    def out_copy(r):
        return pltpu.make_async_copy(raw.at[r], out_hbm.at[r], out_sems.at[r])

    def project_out(r, carry):
        project_plane(r, carry)
        out_copy(r).start()
        return carry

    def wait_out(r, carry):
        out_copy(r).wait()
        return carry

    lax.fori_loop(0, PLANES, project_out, 0)
    everything = pltpu.make_async_remote_copy(
        src_ref=packed_ref, dst_ref=landing, send_sem=send_sem, recv_sem=recv_sem, device_id=peer(1)[1],
        device_id_type=MESH,
    )
    everything.wait_send()
    everything.wait_recv()
    received_ref[...] = landing[...]
    lax.fori_loop(0, PLANES, wait_out, 0)


def slot_table(owner_ref, slots_total):
    count = owner_ref.shape[1]
    owners = owner_ref[...].astype(jnp.float32)
    across = jnp.broadcast_to(owners, (count, count))
    row = lax.broadcasted_iota(jnp.int32, (count, count), 0)
    column = lax.broadcasted_iota(jnp.int32, (count, count), 1)
    down = jnp.sum(jnp.where(row == column, across, 0.0), axis=1, keepdims=True)
    earlier = jnp.where(jnp.logical_and(down == across, row < column), 1.0, 0.0)
    target = owners * SLOT + jnp.sum(earlier, axis=0, keepdims=True)
    none = jnp.full_like(target, -1.0)
    is_low = lax.axis_index("narrow") == 0
    lanes = join_rows([jnp.where(is_low, target, none), jnp.where(is_low, none, target)])
    slots = lax.broadcasted_iota(jnp.int32, (slots_total, WIDTH), 0).astype(jnp.float32)
    return jnp.where(slots == lanes, 1.0, 0.0).astype(jnp.bfloat16)


def factorize(gram_rows, owner_ref, packed_ref, inverse_ref, lower, inv):
    scale = 1.0 / (3.0 * gram_rows(TRI, 1))
    row = lax.broadcasted_iota(jnp.int32, (K, WIDTH), 0)
    columns = []
    for k in range(K):
        first = 8 * (k // 8)
        height = K - first
        column = gram_rows(STARTS[k], height) * scale
        columns.append(column + jnp.where(row[first:] == k, RIDGE, 0.0))
    reciprocals = []
    for k in range(K):
        first = 8 * (k // 8)
        at = k - first
        pivot = jnp.sqrt(columns[k][at : at + 1])
        reciprocal = 1.0 / pivot
        reciprocals.append(reciprocal)
        column = jnp.where(row[first:] >= k, columns[k] * reciprocal, 0.0)
        columns[k] = column
        for m in range(k + 1, K):
            begin = 8 * (m // 8)
            columns[m] = columns[m] - column[m - first : m - first + 1] * column[begin - first :]
        lower[pl.ds(STARTS[k], K - first), :] = column
    for l in range(K):
        first = 8 * (l // 8)
        solved = jnp.where(row[first:] == l, 1.0, 0.0)
        for m in range(l, K):
            base = 8 * (m // 8)
            value = solved[m - first : m - first + 1] * reciprocals[m]
            here = solved[base - first :]
            here = jnp.where(row[base:] == m, value, jnp.where(row[base:] > m, here - columns[m] * value, here))
            solved = here if base == first else jnp.concatenate([solved[: base - first], here], axis=0)
        inv[pl.ds(STARTS[l], K - first), :] = solved
    for i, piece in enumerate(split3(inv[...])):
        inverse_ref[:, i * WIDTH : (i + 1) * WIDTH] = piece
    table = slot_table(owner_ref, packed_ref.shape[0])
    total = None
    for piece in split3(lower[...]):
        term = lax.dot_general(table, piece, (((1,), (1,)), ((), ())), preferred_element_type=jnp.float32)
        total = term if total is None else total + term
    packed_ref[...] = total


def widen_kernel(received_ref, prolong_in, basis_ref, prolong_out, passing, in_sems, out_sems):
    part = PLANES // PASSES
    inward, outward = [], []
    for i in range(PASSES):
        span = pl.ds(part * i, part)
        inward.append(pltpu.make_async_copy(prolong_in.at[span], passing.at[span], in_sems.at[i]))
        outward.append(pltpu.make_async_copy(passing.at[span], prolong_out.at[span], out_sems.at[i]))
    for copy in inward:
        copy.start()
    pieces = split3(received_ref[...])
    for m in range(K * K // WIDTH):
        if m >= 2 and m - 2 < PASSES:
            inward[m - 2].wait()
            outward[m - 2].start()
        group = m // 2
        width = K - 8 * group
        start = STARTS[8 * group]
        first = STARTS[4 * m] // WIDTH * WIDTH
        last = -(-(STARTS[4 * m] + 4 * width) // WIDTH) * WIDTH
        if group == 0:
            basis_ref[0, :, WIDTH * m : WIDTH * (m + 1)] = received_ref[:, first:last]
            continue
        source = lax.broadcasted_iota(jnp.int32, (last - first, WIDTH), 0) + first
        column = lax.broadcasted_iota(jnp.int32, (last - first, WIDTH), 1) + WIDTH * m
        k, l = column // K, lax.rem(column, K)
        wanted = start + (k - 8 * group) * width + l - 8 * group
        place = jnp.where(jnp.logical_and(source == wanted, l >= 8 * group), 1.0, 0.0).astype(jnp.bfloat16)
        total = None
        for piece in pieces:
            term = jnp.dot(piece[:, first:last], place, preferred_element_type=jnp.float32)
            total = term if total is None else total + term
        basis_ref[0, :, WIDTH * m : WIDTH * (m + 1)] = total
    for copy in outward:
        copy.wait()


def vmem(shape, dtype=jnp.float32):
    return pltpu.VMEM(shape, dtype)


def shards(n_wide, n_narrow, tests, block_inverse, face_weight, mixing, far_tiles, far_column, aggregate, owner_map):
    bf16 = jnp.bfloat16
    whole = pl.BlockSpec(memory_space=pltpu.VMEM)
    any_spec = pl.BlockSpec(memory_space=pl.ANY)
    hbm = pl.BlockSpec(memory_space=pltpu.HBM)
    smem = pl.BlockSpec(memory_space=pltpu.SMEM)
    labels = aggregate.reshape(PLANES * 4, 64)

    slots_total = n_wide * n_narrow * SLOT
    projected, received = pl.pallas_call(
        functools.partial(setup_kernel, n_wide, n_narrow),
        out_shape=(
            jax.ShapeDtypeStruct((PLANES, 4 * ROWS, 64), jnp.float32),
            jax.ShapeDtypeStruct((slots_total, TRI), jnp.float32),
        ),
        in_specs=[hbm, whole, whole, smem, hbm, smem, whole, whole],
        out_specs=(any_spec, whole),
        scratch_shapes=[
            vmem((PLANES, ROWS, NODES)),
            vmem((TRI, WIDTH)),
            vmem((TRI, WIDTH)),
            vmem((TRI, 3 * WIDTH), bf16),
            vmem((slots_total, TRI)),
            vmem((slots_total, TRI)),
            vmem((TRI, NODES)),
            vmem((SLOT, TRI)),
            vmem((PLANES, 4 * ROWS, 64)),
            vmem((PLANES + 2, ROWS, NODES)),
            vmem((PLANES + 2, ROWS, NODES)),
            vmem((PLANES + 2, ROWS, NODES)),
            vmem((PLANES, 54, 8, NODES)),
            vmem((SWEEPS, 2, ROWS, NODES), bf16),
            vmem((SWEEPS, 2, ROWS, NODES), bf16),
            vmem((SWEEPS, PLANES, 48, WIDTH), bf16),
            vmem((SWEEPS, PLANES, 48, WIDTH), bf16),
            vmem((ROWS, WIDTH)),
            vmem((PLANES, ROWS, NODES), bf16),
            vmem((PLANES, ROWS, NODES), bf16),
            vmem((PLANES, ROWS, NODES), bf16),
            vmem((PLANES, 3, NODES, NODES), bf16),
            vmem((PLANES, WIDTH, NODES), bf16),
            vmem((3, TRI // GRAM_PARTS, 2 * NODES), bf16),
            vmem((GRAM_ROWS, WIDTH)),
            vmem((GRAM_ROWS, WIDTH)),
            pltpu.SemaphoreType.DMA((2 * CHUNKS,)),
            pltpu.SemaphoreType.DMA((1,)),
            pltpu.SemaphoreType.DMA((2 * SWEEPS,)),
            pltpu.SemaphoreType.DMA((2 * SWEEPS,)),
            pltpu.SemaphoreType.DMA((SWEEPS * CHUNKS,)),
            pltpu.SemaphoreType.DMA((SWEEPS * CHUNKS,)),
            pltpu.SemaphoreType.DMA((4 * CHUNKS,)),
            pltpu.SemaphoreType.DMA((4 * CHUNKS,)),
            pltpu.SemaphoreType.DMA((GRAM_PARTS,)),
            pltpu.SemaphoreType.DMA((GRAM_PARTS,)),
            pltpu.SemaphoreType.DMA,
            pltpu.SemaphoreType.DMA,
            pltpu.SemaphoreType.DMA((PLANES,)),
        ],
        compiler_params=pltpu.CompilerParams(
            collective_id=0, has_side_effects=True, vmem_limit_bytes=57 * 1024 * 1024
        ),
        name="setup",
    )(
        tests.reshape(PLANES, 4 * ROWS, 64),
        block_inverse.reshape(PLANES * 36, 64),
        face_weight.reshape(PLANES * 24, 64),
        mixing.transpose(1, 2, 0),
        far_tiles.reshape(PLANES, 3, NODES, NODES),
        far_column.transpose(2, 1, 0),
        labels,
        owner_map.reshape(1, owner_map.shape[0]),
    )

    basis, prolong = pl.pallas_call(
        widen_kernel,
        out_shape=(
            jax.ShapeDtypeStruct((1, slots_total, K * K), jnp.float32),
            jax.ShapeDtypeStruct((PLANES, 4 * ROWS, 64), jnp.float32),
        ),
        in_specs=[whole, any_spec],
        out_specs=(whole, any_spec),
        scratch_shapes=[
            vmem((PLANES, 4 * ROWS, 64)),
            pltpu.SemaphoreType.DMA((PASSES,)),
            pltpu.SemaphoreType.DMA((PASSES,)),
        ],
        compiler_params=pltpu.CompilerParams(vmem_limit_bytes=57 * 1024 * 1024),
        name="widen",
    )(received, projected)
    return prolong.reshape(tests.shape), basis


def solution(mesh):
    in_specs = (
        P("wide", None, None, "narrow", None),
        P("wide", None, None, "narrow", None),
        P("wide", None, "narrow", None),
        P(),
        P("wide", "narrow", None, None, None),
        P("wide", "narrow", None),
        P("wide", "narrow", None),
        P(("wide", "narrow")),
    )
    out_specs = (P("wide", None, None, "narrow", None), P(("wide", "narrow"), None, None))
    body = functools.partial(shards, mesh.shape["wide"], mesh.shape["narrow"])
    return jax.shard_map(body, mesh=mesh, in_specs=in_specs, out_specs=out_specs, check_vma=False)
```

```python
import functools

import jax
import jax.numpy as jnp
from jax import lax
from jax.experimental import pallas as pl
from jax.experimental.pallas import tpu as pltpu
from jax.sharding import PartitionSpec as P

MESH = pl.DeviceIdType.MESH
SWEEPS = 3
SLOT = 2
K = 32
ROWS = 3 * K
PLANES = 16
NODES = 256
WIDTH = 128
RIDGE = 0.001

BLOCKS = [(k, b) for k in range(K) for b in range(k // 8, K // 8)]
TRI = 8 * len(BLOCKS)
STARTS = {}
for place, (block_k, block_b) in enumerate(BLOCKS):
    STARTS.setdefault(block_k, 8 * place)
GRAM_ROWS = TRI + 16
CHUNKS = 8
PART = PLANES // CHUNKS
GRAM_PARTS = 1
SIDES = 4
EARLY = 4
LAG = 8
PASSES = 4


def split3(x):
    hi = x.astype(jnp.bfloat16)
    rest = x - hi.astype(jnp.float32)
    mid = rest.astype(jnp.bfloat16)
    low = (rest - mid.astype(jnp.float32)).astype(jnp.bfloat16)
    return hi, mid, low


def join_rows(rows):
    return jnp.concatenate(rows, axis=1)


def setup_kernel(
    n_wide, n_narrow,
    tests_hbm, bi_ref, fw_ref, mix_ref, tiles_hbm, col_ref, label_ref, owner_ref,
    out_hbm, received_ref,
    comb_ref, lower, inv, inverse_ref, packed_ref, landing, look, spare,
    raw, x0, x1, x2, coef, xsend, xrecv, ysend, yrecv, ydup, from_left, planes, from_right, tiles, members, outer, acc, gram_in,
    tests_sems, tiles_sem, xsend_sems, xrecv_sems, ysend_sems, yrecv_sems, psend_sems, precv_sems, gsend_sems,
    grecv_sems, send_sem, recv_sem, out_sems,
):
    w = lax.axis_index("wide")
    n = lax.axis_index("narrow")
    right = lax.rem(w + 1, n_wide)
    left = lax.rem(w + n_wide - 1, n_wide)
    other = 1 - n
    fields = [x0, x1, x2]

    def plane_at(i):
        half = i // 2
        return jnp.where(lax.rem(i, 2) == 0, PLANES // 2 - 1 - half, PLANES // 2 + half)

    tests_copies = []
    for q in range(CHUNKS):
        for j, start in enumerate((PLANES // 2 - 1 - q, PLANES // 2 + q)):
            span = pl.ds(start, 1)
            copy = pltpu.make_async_copy(tests_hbm.at[span], raw.at[span], tests_sems.at[2 * q + j])
            copy.start()
            tests_copies.append(copy)
    tiles_copy = pltpu.make_async_copy(tiles_hbm, tiles, tiles_sem.at[0])
    tiles_copy.start()

    barrier = pltpu.get_barrier_semaphore()
    count = n_wide * n_narrow
    me = w * n_narrow + n

    def peer(i):
        index = lax.rem(me + i, count)
        return index, (index // n_narrow, lax.rem(index, n_narrow))

    def greet(i, carry):
        pl.semaphore_signal(barrier, inc=1, device_id=peer(i)[1], device_id_type=MESH)
        return carry

    lax.fori_loop(1, count, greet, 0)

    lane = lax.broadcasted_iota(jnp.int32, (K + 16, WIDTH), 1)
    low_half = lane < 64
    low8 = low_half[0:8]
    is_low = n == 0

    def pack_row(first, second):
        chosen = jnp.where(is_low, second, first)
        turned = pltpu.roll(chosen, 64, 1)
        a = jnp.where(is_low, turned, chosen)[0:48]
        b = jnp.where(is_low, chosen, turned)[48:96]
        return jnp.where(low_half, a, b).astype(jnp.bfloat16)

    def y_copy(s, q):
        span = pl.ds(q * PART, PART)
        return pltpu.make_async_remote_copy(
            src_ref=ysend.at[s, span], dst_ref=yrecv.at[s, span], send_sem=ysend_sems.at[s * CHUNKS + q],
            recv_sem=yrecv_sems.at[s * CHUNKS + q], device_id=(w, other), device_id_type=MESH,
        )

    def x_copies(s):
        up = pltpu.make_async_remote_copy(
            src_ref=xsend.at[s, 0], dst_ref=xrecv.at[s, 0], send_sem=xsend_sems.at[2 * s],
            recv_sem=xrecv_sems.at[2 * s], device_id=(right, n), device_id_type=MESH,
        )
        down = pltpu.make_async_remote_copy(
            src_ref=xsend.at[s, 1], dst_ref=xrecv.at[s, 1], send_sem=xsend_sems.at[2 * s + 1],
            recv_sem=xrecv_sems.at[2 * s + 1], device_id=(left, n), device_id_type=MESH,
        )
        return up, down

    has_right = w < n_wide - 1
    has_left = w > 0

    def start_x(s):
        up, down = x_copies(s)
        xsend[s, 0] = fields[s][PLANES].astype(jnp.bfloat16)
        xsend[s, 1] = fields[s][1].astype(jnp.bfloat16)
        pl.when(has_right)(up.start)
        pl.when(has_left)(down.start)

    def wait_x(s):
        up, down = x_copies(s)
        pl.when(has_right)(up.wait_send)
        pl.when(has_left)(up.wait_recv)
        pl.when(has_left)(down.wait_send)
        pl.when(has_right)(down.wait_recv)

        def widen_left():
            fields[s][0] = xrecv[s, 0].astype(jnp.float32)

        def widen_right():
            fields[s][PLANES + 1] = xrecv[s, 1].astype(jnp.float32)

        pl.when(has_left)(widen_left)
        pl.when(has_right)(widen_right)

    @pl.when(jnp.logical_not(has_left))
    def clear_left():
        for field in fields:
            field[0] = jnp.zeros((ROWS, NODES), jnp.float32)

    @pl.when(jnp.logical_not(has_right))
    def clear_right():
        for field in fields:
            field[PLANES + 1] = jnp.zeros((ROWS, NODES), jnp.float32)

    def unpack_tests(i, carry):
        p = plane_at(i)
        for c in range(3):
            for kb in range(K // 8):
                pieces = [raw[p, pl.ds(96 * kb + 4 * c + y, 8, stride=12), :] for y in range(4)]
                x0[p + 1, pl.ds(c * K + 8 * kb, 8), :] = join_rows(pieces)
        ysend[0, i] = pack_row(x0[p + 1, :, 0:128], x0[p + 1, :, 128:256])
        return carry

    for q in range(CHUNKS):
        tests_copies[2 * q].wait()
        tests_copies[2 * q + 1].wait()
        lax.fori_loop(q * PART, (q + 1) * PART, unpack_tests, 0)

    lane_wide = lax.broadcasted_iota(jnp.int32, (8, NODES), 1)
    z_place = lax.rem(lane_wide, 64)

    def make_coef(p, carry):
        def wide_row(ref, first):
            row = join_rows([ref[pl.ds(first + y, 1), :] for y in range(4)])
            return jnp.broadcast_to(row, (8, NODES))

        inv_rows = [wide_row(bi_ref, 36 * p + 4 * i) for i in range(9)]
        edges = [
            jnp.logical_and(p == PLANES - 1, w == n_wide - 1),
            jnp.logical_and(p == 0, w == 0),
            jnp.logical_and(lane_wide >= 192, n == 1),
            jnp.logical_and(lane_wide < 64, n == 0),
            z_place == 63,
            z_place == 0,
        ]
        for d in range(6):
            weight = jnp.where(edges[d], 0.0, 0.5 * wide_row(fw_ref, 24 * p + 4 * d))
            for a in range(3):
                for b in range(3):
                    total = inv_rows[3 * a] * mix_ref[0, b, d]
                    total += inv_rows[3 * a + 1] * mix_ref[1, b, d]
                    total += inv_rows[3 * a + 2] * mix_ref[2, b, d]
                    coef[p, 9 * d + 3 * a + b] = total * weight
        label = join_rows([label_ref[pl.ds(4 * p + y, 1), :] for y in range(4)])
        groups = lax.broadcasted_iota(jnp.int32, (WIDTH, NODES), 0)
        members[p] = jnp.where(groups == label, 1.0, 0.0).astype(jnp.bfloat16)
        return carry

    lax.fori_loop(0, EARLY, make_coef, 0)
    pl.semaphore_wait(barrier, count - 1)
    for q in range(CHUNKS):
        y_copy(0, q).start()
    start_x(0)
    lax.fori_loop(EARLY, PLANES, make_coef, 0)

    def sweep_plane(s, i):
        p = plane_at(i)
        src = fields[s]
        packed = yrecv[s, i].astype(jnp.float32)
        turned = pltpu.roll(packed, 64, 1)
        ydup[0:48] = jnp.where(low_half, packed, turned)
        ydup[48:96] = jnp.where(low_half, turned, packed)
        for kb in range(K // 8):
            near = []
            own = []
            for c in range(3):
                rows = pl.ds(c * K + kb * 8, 8)
                mid = src[p + 1, rows, :]
                own.append(mid)
                c0, c1 = mid[:, 0:128], mid[:, 128:256]
                r0, r1 = pltpu.roll(c0, 64, 1), pltpu.roll(c1, 64, 1)
                dup = ydup[rows]
                between = jnp.where(low8, r0, r1)
                y_up = jnp.concatenate([between, jnp.where(low8, r1, dup)], axis=1)
                y_down = jnp.concatenate([jnp.where(low8, dup, r0), between], axis=1)
                z_up = jnp.concatenate([pltpu.roll(c0, 127, 1), pltpu.roll(c1, 127, 1)], axis=1)
                z_down = jnp.concatenate([pltpu.roll(c0, 1, 1), pltpu.roll(c1, 1, 1)], axis=1)
                near.append([src[p + 2, rows, :], src[p, rows, :], y_up, y_down, z_up, z_down])
            for a in range(3):
                total = 0.5 * own[a]
                for d in range(6):
                    for b in range(3):
                        total += coef[p, 9 * d + 3 * a + b] * near[b][d]
                rows = pl.ds(a * K + kb * 8, 8)
                if s + 1 < SWEEPS:
                    fields[s + 1][p + 1, rows, :] = total
                else:
                    comb_ref[p, rows, :] = total
        if s + 1 < SWEEPS:
            ysend[s + 1, i] = pack_row(fields[s + 1][p + 1, :, 0:128], fields[s + 1][p + 1, :, 128:256])
        else:
            planes[p] = comb_ref[p].astype(jnp.bfloat16)

    def plane_copies(q):
        copies = []
        for j, start in enumerate((PLANES // 2 - 1 - q, PLANES // 2 + q)):
            span = pl.ds(start, 1)
            for side, (target, landing) in enumerate(((right, from_left), (left, from_right))):
                at = 4 * q + 2 * j + side
                copies.append(
                    pltpu.make_async_remote_copy(
                        src_ref=planes.at[span], dst_ref=landing.at[span], send_sem=psend_sems.at[at],
                        recv_sem=precv_sems.at[at], device_id=(target, n), device_id_type=MESH,
                    )
                )
        return copies

    def do_chunk(s, q):
        y_copy(s, q).wait()
        pl.when(q == CHUNKS - 1)(lambda: wait_x(s))

        def one_plane(j, inner):
            sweep_plane(s, q * PART + j)
            return inner

        lax.fori_loop(0, PART, one_plane, 0)
        if s + 1 < SWEEPS:
            y_copy(s + 1, q).start()
            pl.when(q == CHUNKS - 1)(lambda: start_x(s + 1))
        else:
            for copy in plane_copies(q):
                copy.start()

    def wave_step(t, carry):
        for s in range(SWEEPS):
            q = t - LAG * s
            pl.when(jnp.logical_and(q >= 0, q < CHUNKS))(functools.partial(do_chunk, s, q))
        return carry

    lax.fori_loop(0, CHUNKS + LAG * (SWEEPS - 1), wave_step, 0)

    tiles_copy.wait()
    sources = [from_left, planes, from_right]

    def far_product(r, slot):
        return jnp.dot(
            sources[slot][col_ref[slot, 0, r]], tiles[r, slot], preferred_element_type=jnp.float32
        )

    def near_far(r, carry):
        comb_ref[r] = comb_ref[r] + far_product(r, 1)
        return carry

    lax.fori_loop(0, PLANES, near_far, 0)

    acc[...] = jnp.zeros_like(acc)
    for q in range(CHUNKS):
        for copy in plane_copies(q):
            copy.wait()

    def side_far(r, carry):
        comb_ref[r] = comb_ref[r] + (far_product(r, 0) + far_product(r, 2))
        return carry

    lax.fori_loop(0, PLANES, side_far, 0)

    pairs = len(BLOCKS) // 2 // GRAM_PARTS
    rows_part = 16 * pairs

    def gram_copy(t):
        height = rows_part if t + 1 < GRAM_PARTS else GRAM_ROWS - rows_part * t
        span = pl.ds(rows_part * t, height)
        return pltpu.make_async_remote_copy(
            src_ref=acc.at[span], dst_ref=gram_in.at[span], send_sem=gsend_sems.at[t], recv_sem=grecv_sems.at[t],
            device_id=(w, other), device_id_type=MESH,
        )

    def contract(values, member):
        return lax.dot_general(values, member, (((1,), (1,)), ((), ())), preferred_element_type=jnp.float32)

    for t in range(GRAM_PARTS):

        def gram_planes(h, carry, t=t):
            for side in range(SIDES):
                r = SIDES * h + side
                lanes = pl.ds(side * NODES, NODES)
                for pair in range(pairs):
                    parts = []
                    for k, b in BLOCKS[2 * (pairs * t + pair) : 2 * (pairs * t + pair) + 2]:
                        value = None
                        for c in range(3):
                            term = comb_ref[r, c * K + k : c * K + k + 1, :] * comb_ref[r, pl.ds(c * K + 8 * b, 8), :]
                            value = term if value is None else value + term
                        parts.append(value)
                    for piece, values in enumerate(split3(jnp.concatenate(parts, axis=0))):
                        outer[piece, pl.ds(16 * pair, 16), lanes] = values
            total = None
            for side in range(SIDES):
                member = members[SIDES * h + side]
                lanes = pl.ds(side * NODES, NODES)
                for piece in range(3):
                    term = contract(outer[piece, :, lanes], member)
                    total = term if total is None else total + term
            acc[pl.ds(rows_part * t, rows_part), :] += total
            if t + 1 == GRAM_PARTS:
                ones = jnp.ones((16, NODES), jnp.bfloat16)
                for side in range(SIDES):
                    acc[TRI:GRAM_ROWS] += contract(ones, members[SIDES * h + side])
            return carry

        lax.fori_loop(0, PLANES // SIDES, gram_planes, 0)
        gram_copy(t).start()

    for t in range(GRAM_PARTS):
        gram_copy(t).wait()

    def gram_rows(first, height):
        span = pl.ds(first, height)
        return acc[span, :] + gram_in[span, :]

    factorize(gram_rows, owner_ref, packed_ref, inverse_ref, lower, inv)

    own_span = pl.ds(SLOT * me, SLOT)
    pltpu.make_async_copy(packed_ref.at[own_span], landing.at[own_span], recv_sem).start()
    pltpu.make_async_copy(packed_ref.at[own_span], spare, send_sem).start()

    def send(i, carry):
        index, device = peer(i)
        pltpu.make_async_remote_copy(
            src_ref=packed_ref.at[pl.ds(SLOT * index, SLOT)], dst_ref=landing.at[own_span], send_sem=send_sem,
            recv_sem=recv_sem, device_id=device, device_id_type=MESH,
        ).start()
        return carry

    lax.fori_loop(1, count, send, 0)

    def project_plane(r, carry):
        member = members[r]
        look[...] = jnp.dot(
            inverse_ref[...], jnp.concatenate([member, member, member], axis=0), preferred_element_type=jnp.float32
        )
        for b in range(K // 8):
            totals = [None] * 3
            for l in range(8 * (b + 1)):
                weight = look[pl.ds(STARTS[l] + 8 * (b - l // 8), 8), :]
                for c in range(3):
                    term = weight * comb_ref[r, c * K + l : c * K + l + 1, :]
                    totals[c] = term if totals[c] is None else totals[c] + term
            for c in range(3):
                for y in range(4):
                    raw[r, pl.ds(96 * b + 4 * c + y, 8, stride=12), :] = totals[c][:, 64 * y : 64 * (y + 1)]
        return carry

    def out_copy(r):
        return pltpu.make_async_copy(raw.at[r], out_hbm.at[r], out_sems.at[r])

    def project_out(r, carry):
        project_plane(r, carry)
        out_copy(r).start()
        return carry

    def wait_out(r, carry):
        out_copy(r).wait()
        return carry

    lax.fori_loop(0, PLANES, project_out, 0)
    everything = pltpu.make_async_remote_copy(
        src_ref=packed_ref, dst_ref=landing, send_sem=send_sem, recv_sem=recv_sem, device_id=peer(1)[1],
        device_id_type=MESH,
    )
    everything.wait_send()
    everything.wait_recv()
    received_ref[...] = landing[...]
    lax.fori_loop(0, PLANES, wait_out, 0)


def slot_table(owner_ref, slots_total):
    count = owner_ref.shape[1]
    owners = owner_ref[...].astype(jnp.float32)
    across = jnp.broadcast_to(owners, (count, count))
    row = lax.broadcasted_iota(jnp.int32, (count, count), 0)
    column = lax.broadcasted_iota(jnp.int32, (count, count), 1)
    down = jnp.sum(jnp.where(row == column, across, 0.0), axis=1, keepdims=True)
    earlier = jnp.where(jnp.logical_and(down == across, row < column), 1.0, 0.0)
    target = owners * SLOT + jnp.sum(earlier, axis=0, keepdims=True)
    none = jnp.full_like(target, -1.0)
    is_low = lax.axis_index("narrow") == 0
    lanes = join_rows([jnp.where(is_low, target, none), jnp.where(is_low, none, target)])
    slots = lax.broadcasted_iota(jnp.int32, (slots_total, WIDTH), 0).astype(jnp.float32)
    return jnp.where(slots == lanes, 1.0, 0.0).astype(jnp.bfloat16)


def factorize(gram_rows, owner_ref, packed_ref, inverse_ref, lower, inv):
    scale = 1.0 / (3.0 * gram_rows(TRI, 1))
    row = lax.broadcasted_iota(jnp.int32, (K, WIDTH), 0)
    columns = []
    for k in range(K):
        first = 8 * (k // 8)
        height = K - first
        column = gram_rows(STARTS[k], height) * scale
        columns.append(column + jnp.where(row[first:] == k, RIDGE, 0.0))
    reciprocals = []
    for k in range(K):
        first = 8 * (k // 8)
        at = k - first
        pivot = jnp.sqrt(columns[k][at : at + 1])
        reciprocal = 1.0 / pivot
        reciprocals.append(reciprocal)
        column = jnp.where(row[first:] >= k, columns[k] * reciprocal, 0.0)
        columns[k] = column
        for m in range(k + 1, K):
            begin = 8 * (m // 8)
            columns[m] = columns[m] - column[m - first : m - first + 1] * column[begin - first :]
        lower[pl.ds(STARTS[k], K - first), :] = column
    for l in range(K):
        first = 8 * (l // 8)
        solved = jnp.where(row[first:] == l, 1.0, 0.0)
        for m in range(l, K):
            base = 8 * (m // 8)
            value = solved[m - first : m - first + 1] * reciprocals[m]
            here = solved[base - first :]
            here = jnp.where(row[base:] == m, value, jnp.where(row[base:] > m, here - columns[m] * value, here))
            solved = here if base == first else jnp.concatenate([solved[: base - first], here], axis=0)
        inv[pl.ds(STARTS[l], K - first), :] = solved
    for i, piece in enumerate(split3(inv[...])):
        inverse_ref[:, i * WIDTH : (i + 1) * WIDTH] = piece
    table = slot_table(owner_ref, packed_ref.shape[0])
    total = None
    for piece in split3(lower[...]):
        term = lax.dot_general(table, piece, (((1,), (1,)), ((), ())), preferred_element_type=jnp.float32)
        total = term if total is None else total + term
    packed_ref[...] = total


def widen_kernel(
    received_hbm, prolong_in, basis_hbm, prolong_out, received, basis, passing, received_sem, in_sems, out_sems,
    basis_sems,
):
    received_copy = pltpu.make_async_copy(received_hbm, received, received_sem.at[0])
    received_copy.start()
    part = PLANES // PASSES
    inward, outward, basis_copies = [], [], []
    for i in range(PASSES):
        span = pl.ds(part * i, part)
        inward.append(pltpu.make_async_copy(prolong_in.at[span], passing.at[span], in_sems.at[i]))
        outward.append(pltpu.make_async_copy(passing.at[span], prolong_out.at[span], out_sems.at[i]))
    for copy in inward:
        copy.start()
    blocks = K * K // WIDTH
    places = {}
    for m in range(2, blocks):
        group = m // 2
        width = K - 8 * group
        start = STARTS[8 * group]
        first = STARTS[4 * m] // WIDTH * WIDTH
        last = -(-(STARTS[4 * m] + 4 * width) // WIDTH) * WIDTH
        source = lax.broadcasted_iota(jnp.int32, (last - first, WIDTH), 0) + first
        column = lax.broadcasted_iota(jnp.int32, (last - first, WIDTH), 1) + WIDTH * m
        k, l = column // K, lax.rem(column, K)
        wanted = start + (k - 8 * group) * width + l - 8 * group
        places[m] = (
            first,
            last,
            jnp.where(jnp.logical_and(source == wanted, l >= 8 * group), 1.0, 0.0).astype(jnp.bfloat16),
        )
    received_copy.wait()
    for m in range(blocks):
        lanes = pl.ds(WIDTH * m, WIDTH)
        if m < 2:
            basis[:, lanes] = received[:, lanes]
        else:
            first, last, place = places[m]
            total = None
            for piece in split3(received[:, first:last]):
                term = jnp.dot(piece, place, preferred_element_type=jnp.float32)
                total = term if total is None else total + term
            basis[:, lanes] = total
        copy = pltpu.make_async_copy(basis.at[:, lanes], basis_hbm.at[0, :, lanes], basis_sems.at[m])
        copy.start()
        basis_copies.append(copy)
        if m < PASSES:
            inward[m].wait()
            outward[m].start()
    for copy in outward + basis_copies:
        copy.wait()


def vmem(shape, dtype=jnp.float32):
    return pltpu.VMEM(shape, dtype)


def shards(n_wide, n_narrow, tests, block_inverse, face_weight, mixing, far_tiles, far_column, aggregate, owner_map):
    bf16 = jnp.bfloat16
    whole = pl.BlockSpec(memory_space=pltpu.VMEM)
    any_spec = pl.BlockSpec(memory_space=pl.ANY)
    hbm = pl.BlockSpec(memory_space=pltpu.HBM)
    smem = pl.BlockSpec(memory_space=pltpu.SMEM)
    labels = aggregate.reshape(PLANES * 4, 64)

    slots_total = n_wide * n_narrow * SLOT
    projected, received = pl.pallas_call(
        functools.partial(setup_kernel, n_wide, n_narrow),
        out_shape=(
            jax.ShapeDtypeStruct((PLANES, 4 * ROWS, 64), jnp.float32),
            jax.ShapeDtypeStruct((slots_total, TRI), jnp.float32),
        ),
        in_specs=[hbm, whole, whole, smem, hbm, smem, whole, whole],
        out_specs=(any_spec, whole),
        scratch_shapes=[
            vmem((PLANES, ROWS, NODES)),
            vmem((TRI, WIDTH)),
            vmem((TRI, WIDTH)),
            vmem((TRI, 3 * WIDTH), bf16),
            vmem((slots_total, TRI)),
            vmem((slots_total, TRI)),
            vmem((TRI, NODES)),
            vmem((SLOT, TRI)),
            vmem((PLANES, 4 * ROWS, 64)),
            vmem((PLANES + 2, ROWS, NODES)),
            vmem((PLANES + 2, ROWS, NODES)),
            vmem((PLANES + 2, ROWS, NODES)),
            vmem((PLANES, 54, 8, NODES)),
            vmem((SWEEPS, 2, ROWS, NODES), bf16),
            vmem((SWEEPS, 2, ROWS, NODES), bf16),
            vmem((SWEEPS, PLANES, 48, WIDTH), bf16),
            vmem((SWEEPS, PLANES, 48, WIDTH), bf16),
            vmem((ROWS, WIDTH)),
            vmem((PLANES, ROWS, NODES), bf16),
            vmem((PLANES, ROWS, NODES), bf16),
            vmem((PLANES, ROWS, NODES), bf16),
            vmem((PLANES, 3, NODES, NODES), bf16),
            vmem((PLANES, WIDTH, NODES), bf16),
            vmem((3, TRI // GRAM_PARTS, SIDES * NODES), bf16),
            vmem((GRAM_ROWS, WIDTH)),
            vmem((GRAM_ROWS, WIDTH)),
            pltpu.SemaphoreType.DMA((2 * CHUNKS,)),
            pltpu.SemaphoreType.DMA((1,)),
            pltpu.SemaphoreType.DMA((2 * SWEEPS,)),
            pltpu.SemaphoreType.DMA((2 * SWEEPS,)),
            pltpu.SemaphoreType.DMA((SWEEPS * CHUNKS,)),
            pltpu.SemaphoreType.DMA((SWEEPS * CHUNKS,)),
            pltpu.SemaphoreType.DMA((4 * CHUNKS,)),
            pltpu.SemaphoreType.DMA((4 * CHUNKS,)),
            pltpu.SemaphoreType.DMA((GRAM_PARTS,)),
            pltpu.SemaphoreType.DMA((GRAM_PARTS,)),
            pltpu.SemaphoreType.DMA,
            pltpu.SemaphoreType.DMA,
            pltpu.SemaphoreType.DMA((PLANES,)),
        ],
        compiler_params=pltpu.CompilerParams(
            collective_id=0, has_side_effects=True, vmem_limit_bytes=57 * 1024 * 1024
        ),
        name="setup",
    )(
        tests.reshape(PLANES, 4 * ROWS, 64),
        block_inverse.reshape(PLANES * 36, 64),
        face_weight.reshape(PLANES * 24, 64),
        mixing.transpose(1, 2, 0),
        far_tiles.reshape(PLANES, 3, NODES, NODES),
        far_column.transpose(2, 1, 0),
        labels,
        owner_map.reshape(1, owner_map.shape[0]),
    )

    basis, prolong = pl.pallas_call(
        widen_kernel,
        out_shape=(
            jax.ShapeDtypeStruct((1, slots_total, K * K), jnp.float32),
            jax.ShapeDtypeStruct((PLANES, 4 * ROWS, 64), jnp.float32),
        ),
        in_specs=[any_spec, any_spec],
        out_specs=(any_spec, any_spec),
        scratch_shapes=[
            vmem((slots_total, TRI)),
            vmem((slots_total, K * K)),
            vmem((PLANES, 4 * ROWS, 64)),
            pltpu.SemaphoreType.DMA((1,)),
            pltpu.SemaphoreType.DMA((PASSES,)),
            pltpu.SemaphoreType.DMA((PASSES,)),
            pltpu.SemaphoreType.DMA((K * K // WIDTH,)),
        ],
        compiler_params=pltpu.CompilerParams(vmem_limit_bytes=57 * 1024 * 1024),
        name="widen",
    )(received, projected)
    return prolong.reshape(tests.shape), basis


def solution(mesh):
    in_specs = (
        P("wide", None, None, "narrow", None),
        P("wide", None, None, "narrow", None),
        P("wide", None, "narrow", None),
        P(),
        P("wide", "narrow", None, None, None),
        P("wide", "narrow", None),
        P("wide", "narrow", None),
        P(("wide", "narrow")),
    )
    out_specs = (P("wide", None, None, "narrow", None), P(("wide", "narrow"), None, None))
    body = functools.partial(shards, mesh.shape["wide"], mesh.shape["narrow"])
    return jax.shard_map(body, mesh=mesh, in_specs=in_specs, out_specs=out_specs, check_vma=False)
```

```python
import functools

import jax
import jax.numpy as jnp
from jax import lax
from jax.experimental import pallas as pl
from jax.experimental.pallas import tpu as pltpu
from jax.sharding import PartitionSpec as P

MESH = pl.DeviceIdType.MESH
SWEEPS = 3
SLOT = 2
K = 32
ROWS = 3 * K
PLANES = 16
NODES = 256
WIDTH = 128
RIDGE = 0.001

BLOCKS = [(k, b) for k in range(K) for b in range(k // 8, K // 8)]
TRI = 8 * len(BLOCKS)
STARTS = {}
for place, (block_k, block_b) in enumerate(BLOCKS):
    STARTS.setdefault(block_k, 8 * place)
GRAM_ROWS = TRI + 16
CHUNKS = 8
PART = PLANES // CHUNKS
GRAM_PARTS = 1
SIDES = 4
EARLY = 4
LAG = 8
PASSES = 4


def split3(x):
    hi = x.astype(jnp.bfloat16)
    rest = x - hi.astype(jnp.float32)
    mid = rest.astype(jnp.bfloat16)
    low = (rest - mid.astype(jnp.float32)).astype(jnp.bfloat16)
    return hi, mid, low


def join_rows(rows):
    return jnp.concatenate(rows, axis=1)


def setup_kernel(
    n_wide, n_narrow,
    tests_hbm, bi_ref, fw_ref, mix_ref, tiles_hbm, col_ref, label_ref, owner_ref,
    out_hbm, received_ref,
    comb_ref, lower, inv, inverse_ref, packed_ref, landing, look, spare,
    raw, x0, x1, x2, coef, xsend, xrecv, ysend, yrecv, ydup, from_left, planes, from_right, tiles, members, outer, acc, gram_in,
    tests_sems, tiles_sem, xsend_sems, xrecv_sems, ysend_sems, yrecv_sems, psend_sems, precv_sems, gsend_sems,
    grecv_sems, send_sem, recv_sem, out_sems,
):
    w = lax.axis_index("wide")
    n = lax.axis_index("narrow")
    right = lax.rem(w + 1, n_wide)
    left = lax.rem(w + n_wide - 1, n_wide)
    other = 1 - n
    fields = [x0, x1, x2]

    def plane_at(i):
        half = i // 2
        return jnp.where(lax.rem(i, 2) == 0, PLANES // 2 - 1 - half, PLANES // 2 + half)

    tests_copies = []
    for q in range(CHUNKS):
        for j, start in enumerate((PLANES // 2 - 1 - q, PLANES // 2 + q)):
            span = pl.ds(start, 1)
            copy = pltpu.make_async_copy(tests_hbm.at[span], raw.at[span], tests_sems.at[2 * q + j])
            copy.start()
            tests_copies.append(copy)
    tiles_copy = pltpu.make_async_copy(tiles_hbm, tiles, tiles_sem.at[0])
    tiles_copy.start()

    barrier = pltpu.get_barrier_semaphore()
    count = n_wide * n_narrow
    me = w * n_narrow + n

    def peer(i):
        index = lax.rem(me + i, count)
        return index, (index // n_narrow, lax.rem(index, n_narrow))

    def greet(i, carry):
        pl.semaphore_signal(barrier, inc=1, device_id=peer(i)[1], device_id_type=MESH)
        return carry

    lax.fori_loop(1, count, greet, 0)

    lane = lax.broadcasted_iota(jnp.int32, (K + 16, WIDTH), 1)
    low_half = lane < 64
    low8 = low_half[0:8]
    is_low = n == 0

    def pack_row(first, second):
        chosen = jnp.where(is_low, second, first)
        turned = pltpu.roll(chosen, 64, 1)
        a = jnp.where(is_low, turned, chosen)[0:48]
        b = jnp.where(is_low, chosen, turned)[48:96]
        return jnp.where(low_half, a, b).astype(jnp.bfloat16)

    def y_copy(s, q):
        span = pl.ds(q * PART, PART)
        return pltpu.make_async_remote_copy(
            src_ref=ysend.at[s, span], dst_ref=yrecv.at[s, span], send_sem=ysend_sems.at[s * CHUNKS + q],
            recv_sem=yrecv_sems.at[s * CHUNKS + q], device_id=(w, other), device_id_type=MESH,
        )

    def x_copies(s):
        up = pltpu.make_async_remote_copy(
            src_ref=xsend.at[s, 0], dst_ref=xrecv.at[s, 0], send_sem=xsend_sems.at[2 * s],
            recv_sem=xrecv_sems.at[2 * s], device_id=(right, n), device_id_type=MESH,
        )
        down = pltpu.make_async_remote_copy(
            src_ref=xsend.at[s, 1], dst_ref=xrecv.at[s, 1], send_sem=xsend_sems.at[2 * s + 1],
            recv_sem=xrecv_sems.at[2 * s + 1], device_id=(left, n), device_id_type=MESH,
        )
        return up, down

    has_right = w < n_wide - 1
    has_left = w > 0

    def start_x(s):
        up, down = x_copies(s)
        xsend[s, 0] = fields[s][PLANES].astype(jnp.bfloat16)
        xsend[s, 1] = fields[s][1].astype(jnp.bfloat16)
        pl.when(has_right)(up.start)
        pl.when(has_left)(down.start)

    def wait_x(s):
        up, down = x_copies(s)
        pl.when(has_right)(up.wait_send)
        pl.when(has_left)(up.wait_recv)
        pl.when(has_left)(down.wait_send)
        pl.when(has_right)(down.wait_recv)

        def widen_left():
            fields[s][0] = xrecv[s, 0].astype(jnp.float32)

        def widen_right():
            fields[s][PLANES + 1] = xrecv[s, 1].astype(jnp.float32)

        pl.when(has_left)(widen_left)
        pl.when(has_right)(widen_right)

    @pl.when(jnp.logical_not(has_left))
    def clear_left():
        for field in fields:
            field[0] = jnp.zeros((ROWS, NODES), jnp.float32)

    @pl.when(jnp.logical_not(has_right))
    def clear_right():
        for field in fields:
            field[PLANES + 1] = jnp.zeros((ROWS, NODES), jnp.float32)

    def unpack_tests(i, carry):
        p = plane_at(i)
        for c in range(3):
            for kb in range(K // 8):
                pieces = [raw[p, pl.ds(96 * kb + 4 * c + y, 8, stride=12), :] for y in range(4)]
                x0[p + 1, pl.ds(c * K + 8 * kb, 8), :] = join_rows(pieces)
        ysend[0, i] = pack_row(x0[p + 1, :, 0:128], x0[p + 1, :, 128:256])
        return carry

    for q in range(CHUNKS):
        tests_copies[2 * q].wait()
        tests_copies[2 * q + 1].wait()
        lax.fori_loop(q * PART, (q + 1) * PART, unpack_tests, 0)

    lane_wide = lax.broadcasted_iota(jnp.int32, (8, NODES), 1)
    z_place = lax.rem(lane_wide, 64)

    def make_coef(p, carry):
        def wide_row(ref, first):
            row = join_rows([ref[pl.ds(first + y, 1), :] for y in range(4)])
            return jnp.broadcast_to(row, (8, NODES))

        inv_rows = [wide_row(bi_ref, 36 * p + 4 * i) for i in range(9)]
        edges = [
            jnp.logical_and(p == PLANES - 1, w == n_wide - 1),
            jnp.logical_and(p == 0, w == 0),
            jnp.logical_and(lane_wide >= 192, n == 1),
            jnp.logical_and(lane_wide < 64, n == 0),
            z_place == 63,
            z_place == 0,
        ]
        for d in range(6):
            weight = jnp.where(edges[d], 0.0, 0.5 * wide_row(fw_ref, 24 * p + 4 * d))
            for a in range(3):
                for b in range(3):
                    total = inv_rows[3 * a] * mix_ref[0, b, d]
                    total += inv_rows[3 * a + 1] * mix_ref[1, b, d]
                    total += inv_rows[3 * a + 2] * mix_ref[2, b, d]
                    coef[p, 9 * d + 3 * a + b] = total * weight
        label = join_rows([label_ref[pl.ds(4 * p + y, 1), :] for y in range(4)])
        groups = lax.broadcasted_iota(jnp.int32, (WIDTH, NODES), 0)
        members[p] = jnp.where(groups == label, 1.0, 0.0).astype(jnp.bfloat16)
        return carry

    lax.fori_loop(0, EARLY, make_coef, 0)
    pl.semaphore_wait(barrier, count - 1)
    for q in range(CHUNKS):
        y_copy(0, q).start()
    start_x(0)
    lax.fori_loop(EARLY, PLANES, make_coef, 0)

    def sweep_plane(s, i):
        p = plane_at(i)
        src = fields[s]
        packed = yrecv[s, i].astype(jnp.float32)
        turned = pltpu.roll(packed, 64, 1)
        ydup[0:48] = jnp.where(low_half, packed, turned)
        ydup[48:96] = jnp.where(low_half, turned, packed)
        for kb in range(K // 8):
            near = []
            own = []
            for c in range(3):
                rows = pl.ds(c * K + kb * 8, 8)
                mid = src[p + 1, rows, :]
                own.append(mid)
                c0, c1 = mid[:, 0:128], mid[:, 128:256]
                r0, r1 = pltpu.roll(c0, 64, 1), pltpu.roll(c1, 64, 1)
                dup = ydup[rows]
                between = jnp.where(low8, r0, r1)
                y_up = jnp.concatenate([between, jnp.where(low8, r1, dup)], axis=1)
                y_down = jnp.concatenate([jnp.where(low8, dup, r0), between], axis=1)
                z_up = jnp.concatenate([pltpu.roll(c0, 127, 1), pltpu.roll(c1, 127, 1)], axis=1)
                z_down = jnp.concatenate([pltpu.roll(c0, 1, 1), pltpu.roll(c1, 1, 1)], axis=1)
                near.append([src[p + 2, rows, :], src[p, rows, :], y_up, y_down, z_up, z_down])
            for a in range(3):
                total = 0.5 * own[a]
                for d in range(6):
                    for b in range(3):
                        total += coef[p, 9 * d + 3 * a + b] * near[b][d]
                rows = pl.ds(a * K + kb * 8, 8)
                if s + 1 < SWEEPS:
                    fields[s + 1][p + 1, rows, :] = total
                else:
                    comb_ref[p, rows, :] = total
        if s + 1 < SWEEPS:
            ysend[s + 1, i] = pack_row(fields[s + 1][p + 1, :, 0:128], fields[s + 1][p + 1, :, 128:256])
        else:
            planes[p] = comb_ref[p].astype(jnp.bfloat16)

    def plane_copies(q):
        copies = []
        for j, start in enumerate((PLANES // 2 - 1 - q, PLANES // 2 + q)):
            span = pl.ds(start, 1)
            for side, (target, landing) in enumerate(((right, from_left), (left, from_right))):
                at = 4 * q + 2 * j + side
                copies.append(
                    pltpu.make_async_remote_copy(
                        src_ref=planes.at[span], dst_ref=landing.at[span], send_sem=psend_sems.at[at],
                        recv_sem=precv_sems.at[at], device_id=(target, n), device_id_type=MESH,
                    )
                )
        return copies

    def do_chunk(s, q):
        y_copy(s, q).wait()
        pl.when(q == CHUNKS - 1)(lambda: wait_x(s))

        def one_plane(j, inner):
            sweep_plane(s, q * PART + j)
            return inner

        lax.fori_loop(0, PART, one_plane, 0)
        if s + 1 < SWEEPS:
            y_copy(s + 1, q).start()
            pl.when(q == CHUNKS - 1)(lambda: start_x(s + 1))
        else:
            for copy in plane_copies(q):
                copy.start()

    def wave_step(t, carry):
        for s in range(SWEEPS):
            q = t - LAG * s
            pl.when(jnp.logical_and(q >= 0, q < CHUNKS))(functools.partial(do_chunk, s, q))
        return carry

    lax.fori_loop(0, CHUNKS + LAG * (SWEEPS - 1), wave_step, 0)

    tiles_copy.wait()
    sources = [from_left, planes, from_right]

    def far_product(r, slot):
        return jnp.dot(
            sources[slot][col_ref[slot, 0, r]], tiles[r, slot], preferred_element_type=jnp.float32
        )

    def near_far(h, carry):
        products = [far_product(SIDES * h + side, 1) for side in range(SIDES)]
        for side in range(SIDES):
            comb_ref[SIDES * h + side] = comb_ref[SIDES * h + side] + products[side]
        return carry

    lax.fori_loop(0, PLANES // SIDES, near_far, 0)

    acc[...] = jnp.zeros_like(acc)
    for q in range(CHUNKS):
        for copy in plane_copies(q):
            copy.wait()

    def side_far(h, carry):
        products = [far_product(SIDES * h + side, 0) + far_product(SIDES * h + side, 2) for side in range(SIDES)]
        for side in range(SIDES):
            comb_ref[SIDES * h + side] = comb_ref[SIDES * h + side] + products[side]
        return carry

    lax.fori_loop(0, PLANES // SIDES, side_far, 0)

    pairs = len(BLOCKS) // 2 // GRAM_PARTS
    rows_part = 16 * pairs

    def gram_copy(t):
        height = rows_part if t + 1 < GRAM_PARTS else GRAM_ROWS - rows_part * t
        span = pl.ds(rows_part * t, height)
        return pltpu.make_async_remote_copy(
            src_ref=acc.at[span], dst_ref=gram_in.at[span], send_sem=gsend_sems.at[t], recv_sem=grecv_sems.at[t],
            device_id=(w, other), device_id_type=MESH,
        )

    def contract(values, member):
        return lax.dot_general(values, member, (((1,), (1,)), ((), ())), preferred_element_type=jnp.float32)

    for t in range(GRAM_PARTS):

        def gram_planes(h, carry, t=t):
            for side in range(SIDES):
                r = SIDES * h + side
                lanes = pl.ds(side * NODES, NODES)
                for pair in range(pairs):
                    parts = []
                    for k, b in BLOCKS[2 * (pairs * t + pair) : 2 * (pairs * t + pair) + 2]:
                        value = None
                        for c in range(3):
                            term = comb_ref[r, c * K + k : c * K + k + 1, :] * comb_ref[r, pl.ds(c * K + 8 * b, 8), :]
                            value = term if value is None else value + term
                        parts.append(value)
                    for piece, values in enumerate(split3(jnp.concatenate(parts, axis=0))):
                        outer[piece, pl.ds(16 * pair, 16), lanes] = values
            total = None
            for side in range(SIDES):
                member = members[SIDES * h + side]
                lanes = pl.ds(side * NODES, NODES)
                for piece in range(3):
                    term = contract(outer[piece, :, lanes], member)
                    total = term if total is None else total + term
            acc[pl.ds(rows_part * t, rows_part), :] += total
            if t + 1 == GRAM_PARTS:
                ones = jnp.ones((16, NODES), jnp.bfloat16)
                for side in range(SIDES):
                    acc[TRI:GRAM_ROWS] += contract(ones, members[SIDES * h + side])
            return carry

        lax.fori_loop(0, PLANES // SIDES, gram_planes, 0)
        gram_copy(t).start()

    for t in range(GRAM_PARTS):
        gram_copy(t).wait()

    def gram_rows(first, height):
        span = pl.ds(first, height)
        return acc[span, :] + gram_in[span, :]

    factorize(gram_rows, owner_ref, packed_ref, inverse_ref, lower, inv)

    own_span = pl.ds(SLOT * me, SLOT)
    pltpu.make_async_copy(packed_ref.at[own_span], landing.at[own_span], recv_sem).start()
    pltpu.make_async_copy(packed_ref.at[own_span], spare, send_sem).start()

    def send(i, carry):
        index, device = peer(i)
        pltpu.make_async_remote_copy(
            src_ref=packed_ref.at[pl.ds(SLOT * index, SLOT)], dst_ref=landing.at[own_span], send_sem=send_sem,
            recv_sem=recv_sem, device_id=device, device_id_type=MESH,
        ).start()
        return carry

    lax.fori_loop(1, count, send, 0)

    def project_plane(r, carry):
        member = members[r]
        look[...] = jnp.dot(
            inverse_ref[...], jnp.concatenate([member, member, member], axis=0), preferred_element_type=jnp.float32
        )
        for b in range(K // 8):
            totals = [None] * 3
            for l in range(8 * (b + 1)):
                weight = look[pl.ds(STARTS[l] + 8 * (b - l // 8), 8), :]
                for c in range(3):
                    term = weight * comb_ref[r, c * K + l : c * K + l + 1, :]
                    totals[c] = term if totals[c] is None else totals[c] + term
            for c in range(3):
                for y in range(4):
                    raw[r, pl.ds(96 * b + 4 * c + y, 8, stride=12), :] = totals[c][:, 64 * y : 64 * (y + 1)]
        return carry

    def out_copy(r):
        return pltpu.make_async_copy(raw.at[r], out_hbm.at[r], out_sems.at[r])

    def project_out(r, carry):
        project_plane(r, carry)
        out_copy(r).start()
        return carry

    def wait_out(r, carry):
        out_copy(r).wait()
        return carry

    lax.fori_loop(0, PLANES, project_out, 0)
    everything = pltpu.make_async_remote_copy(
        src_ref=packed_ref, dst_ref=landing, send_sem=send_sem, recv_sem=recv_sem, device_id=peer(1)[1],
        device_id_type=MESH,
    )
    everything.wait_send()
    everything.wait_recv()
    received_ref[...] = landing[...]
    lax.fori_loop(0, PLANES, wait_out, 0)


def slot_table(owner_ref, slots_total):
    count = owner_ref.shape[1]
    owners = owner_ref[...].astype(jnp.float32)
    across = jnp.broadcast_to(owners, (count, count))
    row = lax.broadcasted_iota(jnp.int32, (count, count), 0)
    column = lax.broadcasted_iota(jnp.int32, (count, count), 1)
    down = jnp.sum(jnp.where(row == column, across, 0.0), axis=1, keepdims=True)
    earlier = jnp.where(jnp.logical_and(down == across, row < column), 1.0, 0.0)
    target = owners * SLOT + jnp.sum(earlier, axis=0, keepdims=True)
    none = jnp.full_like(target, -1.0)
    is_low = lax.axis_index("narrow") == 0
    lanes = join_rows([jnp.where(is_low, target, none), jnp.where(is_low, none, target)])
    slots = lax.broadcasted_iota(jnp.int32, (slots_total, WIDTH), 0).astype(jnp.float32)
    return jnp.where(slots == lanes, 1.0, 0.0).astype(jnp.bfloat16)


def factorize(gram_rows, owner_ref, packed_ref, inverse_ref, lower, inv):
    scale = 1.0 / (3.0 * gram_rows(TRI, 1))
    row = lax.broadcasted_iota(jnp.int32, (K, WIDTH), 0)
    columns = []
    for k in range(K):
        first = 8 * (k // 8)
        height = K - first
        column = gram_rows(STARTS[k], height) * scale
        columns.append(column + jnp.where(row[first:] == k, RIDGE, 0.0))
    reciprocals = []
    for k in range(K):
        first = 8 * (k // 8)
        at = k - first
        pivot = jnp.sqrt(columns[k][at : at + 1])
        reciprocal = 1.0 / pivot
        reciprocals.append(reciprocal)
        column = jnp.where(row[first:] >= k, columns[k] * reciprocal, 0.0)
        columns[k] = column
        for m in range(k + 1, K):
            begin = 8 * (m // 8)
            columns[m] = columns[m] - column[m - first : m - first + 1] * column[begin - first :]
        lower[pl.ds(STARTS[k], K - first), :] = column
    for l in range(K):
        first = 8 * (l // 8)
        solved = jnp.where(row[first:] == l, 1.0, 0.0)
        for m in range(l, K):
            base = 8 * (m // 8)
            value = solved[m - first : m - first + 1] * reciprocals[m]
            here = solved[base - first :]
            here = jnp.where(row[base:] == m, value, jnp.where(row[base:] > m, here - columns[m] * value, here))
            solved = here if base == first else jnp.concatenate([solved[: base - first], here], axis=0)
        inv[pl.ds(STARTS[l], K - first), :] = solved
    for i, piece in enumerate(split3(inv[...])):
        inverse_ref[:, i * WIDTH : (i + 1) * WIDTH] = piece
    table = slot_table(owner_ref, packed_ref.shape[0])
    total = None
    for piece in split3(lower[...]):
        term = lax.dot_general(table, piece, (((1,), (1,)), ((), ())), preferred_element_type=jnp.float32)
        total = term if total is None else total + term
    packed_ref[...] = total


def widen_kernel(
    received_hbm, prolong_in, basis_hbm, prolong_out, received, basis, passing, received_sem, in_sems, out_sems,
    basis_sems,
):
    received_copy = pltpu.make_async_copy(received_hbm, received, received_sem.at[0])
    received_copy.start()
    part = PLANES // PASSES
    inward, outward, basis_copies = [], [], []
    for i in range(PASSES):
        span = pl.ds(part * i, part)
        inward.append(pltpu.make_async_copy(prolong_in.at[span], passing.at[span], in_sems.at[i]))
        outward.append(pltpu.make_async_copy(passing.at[span], prolong_out.at[span], out_sems.at[i]))
    for copy in inward:
        copy.start()
    blocks = K * K // WIDTH
    places = {}
    for m in range(2, blocks):
        group = m // 2
        width = K - 8 * group
        start = STARTS[8 * group]
        first = STARTS[4 * m] // WIDTH * WIDTH
        last = -(-(STARTS[4 * m] + 4 * width) // WIDTH) * WIDTH
        source = lax.broadcasted_iota(jnp.int32, (last - first, WIDTH), 0) + first
        column = lax.broadcasted_iota(jnp.int32, (last - first, WIDTH), 1) + WIDTH * m
        k, l = column // K, lax.rem(column, K)
        wanted = start + (k - 8 * group) * width + l - 8 * group
        places[m] = (
            first,
            last,
            jnp.where(jnp.logical_and(source == wanted, l >= 8 * group), 1.0, 0.0).astype(jnp.bfloat16),
        )
    received_copy.wait()
    for m in range(blocks):
        lanes = pl.ds(WIDTH * m, WIDTH)
        if m < 2:
            basis[:, lanes] = received[:, lanes]
        else:
            first, last, place = places[m]
            total = None
            for piece in split3(received[:, first:last]):
                term = jnp.dot(piece, place, preferred_element_type=jnp.float32)
                total = term if total is None else total + term
            basis[:, lanes] = total
        copy = pltpu.make_async_copy(basis.at[:, lanes], basis_hbm.at[0, :, lanes], basis_sems.at[m])
        copy.start()
        basis_copies.append(copy)
        if m < PASSES:
            inward[m].wait()
            outward[m].start()
    for copy in outward + basis_copies:
        copy.wait()


def vmem(shape, dtype=jnp.float32):
    return pltpu.VMEM(shape, dtype)


def shards(n_wide, n_narrow, tests, block_inverse, face_weight, mixing, far_tiles, far_column, aggregate, owner_map):
    bf16 = jnp.bfloat16
    whole = pl.BlockSpec(memory_space=pltpu.VMEM)
    any_spec = pl.BlockSpec(memory_space=pl.ANY)
    hbm = pl.BlockSpec(memory_space=pltpu.HBM)
    smem = pl.BlockSpec(memory_space=pltpu.SMEM)
    labels = aggregate.reshape(PLANES * 4, 64)

    slots_total = n_wide * n_narrow * SLOT
    projected, received = pl.pallas_call(
        functools.partial(setup_kernel, n_wide, n_narrow),
        out_shape=(
            jax.ShapeDtypeStruct((PLANES, 4 * ROWS, 64), jnp.float32),
            jax.ShapeDtypeStruct((slots_total, TRI), jnp.float32),
        ),
        in_specs=[hbm, whole, whole, smem, hbm, smem, whole, whole],
        out_specs=(any_spec, whole),
        scratch_shapes=[
            vmem((PLANES, ROWS, NODES)),
            vmem((TRI, WIDTH)),
            vmem((TRI, WIDTH)),
            vmem((TRI, 3 * WIDTH), bf16),
            vmem((slots_total, TRI)),
            vmem((slots_total, TRI)),
            vmem((TRI, NODES)),
            vmem((SLOT, TRI)),
            vmem((PLANES, 4 * ROWS, 64)),
            vmem((PLANES + 2, ROWS, NODES)),
            vmem((PLANES + 2, ROWS, NODES)),
            vmem((PLANES + 2, ROWS, NODES)),
            vmem((PLANES, 54, 8, NODES)),
            vmem((SWEEPS, 2, ROWS, NODES), bf16),
            vmem((SWEEPS, 2, ROWS, NODES), bf16),
            vmem((SWEEPS, PLANES, 48, WIDTH), bf16),
            vmem((SWEEPS, PLANES, 48, WIDTH), bf16),
            vmem((ROWS, WIDTH)),
            vmem((PLANES, ROWS, NODES), bf16),
            vmem((PLANES, ROWS, NODES), bf16),
            vmem((PLANES, ROWS, NODES), bf16),
            vmem((PLANES, 3, NODES, NODES), bf16),
            vmem((PLANES, WIDTH, NODES), bf16),
            vmem((3, TRI // GRAM_PARTS, SIDES * NODES), bf16),
            vmem((GRAM_ROWS, WIDTH)),
            vmem((GRAM_ROWS, WIDTH)),
            pltpu.SemaphoreType.DMA((2 * CHUNKS,)),
            pltpu.SemaphoreType.DMA((1,)),
            pltpu.SemaphoreType.DMA((2 * SWEEPS,)),
            pltpu.SemaphoreType.DMA((2 * SWEEPS,)),
            pltpu.SemaphoreType.DMA((SWEEPS * CHUNKS,)),
            pltpu.SemaphoreType.DMA((SWEEPS * CHUNKS,)),
            pltpu.SemaphoreType.DMA((4 * CHUNKS,)),
            pltpu.SemaphoreType.DMA((4 * CHUNKS,)),
            pltpu.SemaphoreType.DMA((GRAM_PARTS,)),
            pltpu.SemaphoreType.DMA((GRAM_PARTS,)),
            pltpu.SemaphoreType.DMA,
            pltpu.SemaphoreType.DMA,
            pltpu.SemaphoreType.DMA((PLANES,)),
        ],
        compiler_params=pltpu.CompilerParams(
            collective_id=0, has_side_effects=True, vmem_limit_bytes=57 * 1024 * 1024
        ),
        name="setup",
    )(
        tests.reshape(PLANES, 4 * ROWS, 64),
        block_inverse.reshape(PLANES * 36, 64),
        face_weight.reshape(PLANES * 24, 64),
        mixing.transpose(1, 2, 0),
        far_tiles.reshape(PLANES, 3, NODES, NODES),
        far_column.transpose(2, 1, 0),
        labels,
        owner_map.reshape(1, owner_map.shape[0]),
    )

    basis, prolong = pl.pallas_call(
        widen_kernel,
        out_shape=(
            jax.ShapeDtypeStruct((1, slots_total, K * K), jnp.float32),
            jax.ShapeDtypeStruct((PLANES, 4 * ROWS, 64), jnp.float32),
        ),
        in_specs=[any_spec, any_spec],
        out_specs=(any_spec, any_spec),
        scratch_shapes=[
            vmem((slots_total, TRI)),
            vmem((slots_total, K * K)),
            vmem((PLANES, 4 * ROWS, 64)),
            pltpu.SemaphoreType.DMA((1,)),
            pltpu.SemaphoreType.DMA((PASSES,)),
            pltpu.SemaphoreType.DMA((PASSES,)),
            pltpu.SemaphoreType.DMA((K * K // WIDTH,)),
        ],
        compiler_params=pltpu.CompilerParams(vmem_limit_bytes=57 * 1024 * 1024),
        name="widen",
    )(received, projected)
    return prolong.reshape(tests.shape), basis


def solution(mesh):
    in_specs = (
        P("wide", None, None, "narrow", None),
        P("wide", None, None, "narrow", None),
        P("wide", None, "narrow", None),
        P(),
        P("wide", "narrow", None, None, None),
        P("wide", "narrow", None),
        P("wide", "narrow", None),
        P(("wide", "narrow")),
    )
    out_specs = (P("wide", None, None, "narrow", None), P(("wide", "narrow"), None, None))
    body = functools.partial(shards, mesh.shape["wide"], mesh.shape["narrow"])
    return jax.shard_map(body, mesh=mesh, in_specs=in_specs, out_specs=out_specs, check_vma=False)
```
